128 devices in a mesh: grp: 4 (over x), leaf: 32 (over z, y, core).
Axes of the slice: x: 4, y: 4, z: 4, core: 2. Of those that a mesh axis runs over, the one named last changes fastest.
Arguments:
- potentials: float32 [131072, 256], P(('grp', 'leaf')), may hold values from -16 to 16, as said below
- leaf_panels: int32 [128, 1024], P(('grp', 'leaf')), may hold values from 0 to 1023, each once within a row
- near_blocks: bfloat16 [49152, 128, 128], P(('grp', 'leaf')), may hold values from -0.125 to 0.125
- near_target: int32 [128, 384], P(('grp', 'leaf')), may hold values from 0 to 7
- near_source: int32 [128, 384], P(('grp', 'leaf')), may hold values from 0 to 23, as said below
- near_count: int32 [128], P(('grp', 'leaf')), may hold values from 48 to 384, as said below
- leaf_basis: bfloat16 [1024, 64, 128], P(('grp', 'leaf')), may hold values from -0.5 to 0.5
- far_leaf: bfloat16 [24576, 64, 64], P(('grp', 'leaf')), may hold values from -0.15625 to 0.15625
- far_leaf_target: int32 [128, 192], P(('grp', 'leaf')), may hold values from 0 to 7
- far_leaf_source: int32 [128, 192], P(('grp', 'leaf')), may hold values from 0 to 23, as said below
- leaf_transfer: bfloat16 [1024, 64, 64], P(('grp', 'leaf')), may hold values from -0.375 to 0.375
- leaf_parent: int32 [1024], P(('grp', 'leaf')), may hold values from 0 to 31
- far_two: bfloat16 [2048, 64, 64], P(('grp', 'leaf')), may hold values from -0.125 to 0.125
- far_two_target: int32 [128, 16], P(('grp', 'leaf')), may hold values from 0 to 31
- far_two_source: int32 [128, 16], P(('grp', 'leaf')), may hold values from 0 to 127
- two_transfer: bfloat16 [128, 64, 64], replicated, may hold values from -0.375 to 0.375
- two_parent: int32 [128], replicated, may hold values from 0 to 15
- far_one: bfloat16 [32, 64, 64], replicated, may hold values from -0.5 to 0.5
- far_one_target: int32 [32], replicated, may hold values from 0 to 15
- far_one_source: int32 [32], replicated, may hold values from 0 to 15
Outputs:
- solution: float32 [131072, 256], P(('grp', 'leaf'))
- residual_estimate: float32 [256], replicated
The draws below stay inside these ranges and needn't reach their ends.
Inputs may be any that keep to these rules, and one draw needn't show every extreme that they name: `potentials`: entries of order one, larger towards later panels. `near_source`: window index: values below 8 name the previous device's leaves, from 16 the next device's; the first device names none before it, the last none after it. `far_leaf_source`: window index as for near_source, with the same rule at the two end devices. Slots of a device from near_count on hold no block; some device is full.
All inputs are finite; a program needn't handle non-finite values.
Results may differ from the reference program's by a relative error of at most 0.009.
Values may be sent and summed in bfloat16 or wider, within the bound.
A program may use at most 192 MiB of HBM per device.

```python
import jax
import jax.numpy as jnp
from jax import lax

P_SIZE = 128
K = 64
FL_LEAF = 24
R = 256
LEAF_DEV = 8
NB_DEV = 384
FL_DEV = 192
F2_DEV = 16
SHARDS = 128
LEAVES = 1024
PANELS = 131072
C2 = 32
CLUSTERS2 = 128
C1 = 16
F1 = 32
N_LEAF = 32


def window_sources(key, count):
    raw = jax.random.randint(key, (SHARDS, count), 0, 6 * LEAF_DEV)
    position = jnp.arange(SHARDS, dtype=jnp.int32)[:, None]
    lowest = jnp.where(position == 0, LEAF_DEV, 0)
    highest = jnp.where(position == SHARDS - 1, 2 * LEAF_DEV, 3 * LEAF_DEV)
    return (lowest + raw % (highest - lowest)).astype(jnp.int32)


def draw_near_source(key, part):
    key = jax.random.fold_in(key, 11)
    return window_sources(key, NB_DEV)


def draw_far_leaf_source(key, part):
    key = jax.random.fold_in(key, 12)
    return window_sources(key, FL_DEV)


def draw_near_count(key, part):
    key = jax.random.fold_in(key, 13)
    key_levels, key_busy = jax.random.split(key)
    levels = jax.random.randint(key_levels, (SHARDS,), 0, 8)
    counts = NB_DEV // 8 * (1 + levels * levels // 7)
    busiest = jax.random.randint(key_busy, (), 0, SHARDS)
    return counts.at[busiest].set(NB_DEV).astype(jnp.int32)


def draw_potentials(key, part):
    key = jax.random.fold_in(key, 14)
    position = jnp.arange(PANELS, dtype=jnp.float32)[:, None] / max(PANELS - 1, 1)
    growth = 3.0 ** position
    values_drawn = jax.random.truncated_normal(key, -4.0, 4.0, (PANELS, R), jnp.float32) * growth
    return values_drawn.astype(jnp.float32)


def plant(array, stream_key, least, largest):
    dims = array.shape
    place = [jax.random.randint(jax.random.fold_in(stream_key, axis), (), 0, dims[axis]) for axis in range(len(dims))]
    array = array.at[tuple(place)].set(least)
    longest = dims.index(max(dims))
    place[longest] = (place[longest] + 1) % dims[longest]
    return array.at[tuple(place)].set(largest)


def level_of(key, dims, cuts, smallest, high):
    level, own = 1.0, jax.random.fold_in(key, 6)
    for dim, blocks in cuts:
        heights = jnp.exp(jax.random.uniform(jax.random.fold_in(own, dim), (blocks,), jnp.float32, smallest / len(cuts), high / len(cuts)))
        level = level * jnp.repeat(heights, dims[dim] // blocks).reshape([-1 if axis == dim else 1 for axis in range(len(dims))])
    return level


def bell_draw(own_key, shape, deviation, limit, cuts=(), held_as=jnp.bfloat16):
    gain = level_of(own_key, shape, cuts, -0.22, 0.18) if cuts else 1.0
    values = jax.random.normal(own_key, shape, jnp.float32) * deviation * gain
    return jnp.minimum(jnp.maximum(values, -limit), limit).astype(held_as)


def setup_inputs(seed: int = 0) -> dict:
    streams_of = jax.random.split(jax.random.key(seed), 21)
    potentials = draw_potentials(jax.random.fold_in(streams_of[20], 71), 0)
    leaf_panels = jax.vmap(lambda own: jax.random.permutation(own, LEAF_DEV * P_SIZE))(jax.random.split(streams_of[1], SHARDS)).reshape((SHARDS, LEAF_DEV * P_SIZE)).astype(jnp.int32)
    near_blocks = bell_draw(streams_of[2], (SHARDS * NB_DEV, P_SIZE, P_SIZE), (P_SIZE * 16) ** -0.5, 0.125, ((0, 128),))
    near_target = plant(jax.random.randint(streams_of[3], (SHARDS, NB_DEV), 0, LEAF_DEV), jax.random.fold_in(streams_of[3], 1), 0, LEAF_DEV - 1).astype(jnp.int32)
    near_source = draw_near_source(jax.random.fold_in(streams_of[20], 71), 0)
    near_count = draw_near_count(jax.random.fold_in(streams_of[20], 71), 0)
    leaf_basis = bell_draw(streams_of[6], (LEAVES, K, P_SIZE), P_SIZE ** -0.5, 0.5, ((0, 128),))
    far_leaf = bell_draw(streams_of[7], (SHARDS * FL_DEV, K, K), (K * FL_LEAF) ** -0.5, 0.15625, ((0, 128),))
    far_leaf_target = plant(jax.random.randint(streams_of[8], (SHARDS, FL_DEV), 0, LEAF_DEV), jax.random.fold_in(streams_of[8], 1), 0, LEAF_DEV - 1).astype(jnp.int32)
    far_leaf_source = draw_far_leaf_source(jax.random.fold_in(streams_of[20], 71), 0)
    leaf_transfer = bell_draw(streams_of[10], (LEAVES, K, K), (K * 4) ** -0.5, 0.375, ((0, 128),))
    leaf_parent = plant(jax.random.randint(streams_of[11], (LEAVES,), 0, C2), jax.random.fold_in(streams_of[11], 1), 0, C2 - 1).astype(jnp.int32)
    far_two = bell_draw(streams_of[12], (SHARDS * F2_DEV, K, K), (K * 32) ** -0.5, 0.125, ((0, 128),))
    far_two_target = plant(jax.random.randint(streams_of[13], (SHARDS, F2_DEV), 0, C2), jax.random.fold_in(streams_of[13], 1), 0, C2 - 1).astype(jnp.int32)
    far_two_source = plant(jax.random.randint(streams_of[14], (SHARDS, F2_DEV), 0, CLUSTERS2), jax.random.fold_in(streams_of[14], 1), 0, CLUSTERS2 - 1).astype(jnp.int32)
    two_transfer = bell_draw(streams_of[15], (CLUSTERS2, K, K), (K * 4) ** -0.5, 0.375)
    two_parent = plant(jax.random.randint(streams_of[16], (CLUSTERS2,), 0, C1), jax.random.fold_in(streams_of[16], 1), 0, C1 - 1).astype(jnp.int32)
    far_one = bell_draw(streams_of[17], (F1, K, K), (K * 2) ** -0.5, 0.5)
    far_one_target = plant(jax.random.randint(streams_of[18], (F1,), 0, C1), jax.random.fold_in(streams_of[18], 1), 0, C1 - 1).astype(jnp.int32)
    far_one_source = plant(jax.random.randint(streams_of[19], (F1,), 0, C1), jax.random.fold_in(streams_of[19], 1), 0, C1 - 1).astype(jnp.int32)
    return dict(potentials=potentials, leaf_panels=leaf_panels, near_blocks=near_blocks, near_target=near_target, near_source=near_source, near_count=near_count, leaf_basis=leaf_basis, far_leaf=far_leaf, far_leaf_target=far_leaf_target, far_leaf_source=far_leaf_source, leaf_transfer=leaf_transfer, leaf_parent=leaf_parent, far_two=far_two, far_two_target=far_two_target, far_two_source=far_two_source, two_transfer=two_transfer, two_parent=two_parent, far_one=far_one, far_one_target=far_one_target, far_one_source=far_one_source)


EPS = 1e-06
HIGH = lax.Precision.HIGHEST

def least_squares(beta_norm, first_diag, first_below, second_top, second_diag, second_below):
    first_radius = jnp.sqrt(first_diag * first_diag + first_below * first_below)
    first_cos = first_diag / first_radius
    first_sin = first_below / first_radius
    upper_term = first_cos * second_top + first_sin * second_diag
    lower_term = first_cos * second_diag - first_sin * second_top
    second_radius = jnp.sqrt(lower_term * lower_term + second_below * second_below)
    second_cos = lower_term / second_radius
    second_sin = second_below / second_radius
    weight_two = -first_sin * beta_norm * second_cos / second_radius
    weight_one = (first_cos * beta_norm - upper_term * weight_two) / first_radius
    return (weight_one, weight_two, first_sin * second_sin * beta_norm)

def reference(potentials, leaf_panels, near_blocks, near_target, near_source, near_count, leaf_basis, far_leaf, far_leaf_target, far_leaf_source, leaf_transfer, leaf_parent, far_two, far_two_target, far_two_source, two_transfer, two_parent, far_one, far_one_target, far_one_source):
    device_ids = jnp.arange(SHARDS, dtype=jnp.int32)
    panel_rows = (device_ids[:, None] * (LEAF_DEV * P_SIZE) + leaf_panels).reshape(-1).astype(jnp.int32)
    group_of = jnp.arange(LEAVES, dtype=jnp.int32) // (LEAF_DEV * N_LEAF)
    cluster_of = (group_of * C2 + leaf_parent).astype(jnp.int32)
    slot_group = jnp.arange(SHARDS * F2_DEV, dtype=jnp.int32) // (F2_DEV * N_LEAF)
    two_target = (slot_group * C2 + far_two_target.reshape(-1)).astype(jnp.int32)
    two_source = far_two_source.reshape(-1)
    window_len = 3 * LEAF_DEV
    basis = leaf_basis.astype(jnp.float32)
    transfer = leaf_transfer.astype(jnp.float32)
    upper_transfer = two_transfer.astype(jnp.float32)

    def apply(vector_in):
        lined = vector_in.astype(jnp.bfloat16)[panel_rows].reshape(LEAVES, P_SIZE, R)
        coeffs = jnp.einsum('lkp,lpr->lkr', basis, lined.astype(jnp.float32), precision=HIGH).astype(jnp.bfloat16)
        joined = jnp.concatenate([lined, coeffs], axis=1)
        padded = jnp.pad(joined, ((LEAF_DEV, LEAF_DEV), (0, 0), (0, 0)))

        def device_terms(device):
            window = lax.dynamic_slice_in_dim(padded, (device * LEAF_DEV).astype(jnp.int32), window_len, 0).astype(jnp.float32)
            blocks = lax.dynamic_slice_in_dim(near_blocks, (device * NB_DEV).astype(jnp.int32), NB_DEV, 0).astype(jnp.float32)
            alive_mask = (jnp.arange(NB_DEV, dtype=jnp.int32) < near_count[device]).astype(jnp.float32)
            keys = (near_target[device] * window_len + near_source[device]).astype(jnp.int32)
            combined = jax.ops.segment_sum(blocks * alive_mask[:, None, None], keys, num_segments=LEAF_DEV * window_len)
            combined = combined.reshape(LEAF_DEV, window_len, P_SIZE, P_SIZE)
            near_part = jnp.einsum('tspq,sqr->tpr', combined, window[:, :P_SIZE], precision=HIGH)
            slab = lax.dynamic_slice_in_dim(far_leaf, (device * FL_DEV).astype(jnp.int32), FL_DEV, 0).astype(jnp.float32)
            pieces = jnp.einsum('jab,jbr->jar', slab, window[:, P_SIZE:][far_leaf_source[device]], precision=HIGH)
            leaf_local = jax.ops.segment_sum(pieces, far_leaf_target[device], num_segments=LEAF_DEV)
            return (near_part, leaf_local)
        near_part, leaf_local = lax.map(device_terms, device_ids)
        near_part = near_part.reshape(LEAVES, P_SIZE, R)
        leaf_local = leaf_local.reshape(LEAVES, K, R)
        rising = jnp.einsum('lab,lar->lbr', transfer, coeffs.astype(jnp.float32), precision=HIGH)
        q_two = jax.ops.segment_sum(rising, cluster_of, num_segments=CLUSTERS2).astype(jnp.bfloat16)
        q_wide = q_two.astype(jnp.float32)
        pieces_two = jnp.einsum('jab,jbr->jar', far_two.astype(jnp.float32), q_wide[two_source], precision=HIGH)
        far_two_sum = jax.ops.segment_sum(pieces_two, two_target, num_segments=CLUSTERS2)
        rising_two = jnp.einsum('cab,car->cbr', upper_transfer, q_wide, precision=HIGH)
        q_one = jax.ops.segment_sum(rising_two, two_parent, num_segments=C1).astype(jnp.bfloat16)
        pieces_one = jnp.einsum('jab,jbr->jar', far_one.astype(jnp.float32), q_one.astype(jnp.float32)[far_one_source], precision=HIGH)
        l_one = jax.ops.segment_sum(pieces_one, far_one_target, num_segments=C1).astype(jnp.bfloat16)
        l_two = far_two_sum + jnp.einsum('cab,cbr->car', upper_transfer, l_one.astype(jnp.float32)[two_parent], precision=HIGH)
        l_two = l_two.astype(jnp.bfloat16)
        l_leaf = leaf_local + jnp.einsum('lab,lbr->lar', transfer, l_two.astype(jnp.float32)[cluster_of], precision=HIGH)
        l_leaf = l_leaf.astype(jnp.bfloat16)
        result = near_part + jnp.einsum('lkp,lkr->lpr', basis, l_leaf.astype(jnp.float32), precision=HIGH)
        return jnp.zeros((PANELS, R), jnp.float32).at[panel_rows].set(result.reshape(PANELS, R))
    beta_norm = jnp.sqrt(lax.optimization_barrier(jnp.sum(potentials * potentials, axis=0)) + EPS)
    first = potentials / beta_norm
    image = apply(first)
    first_diag = lax.optimization_barrier(jnp.sum(first * image, axis=0))
    rest = image - first_diag * first
    first_below = jnp.sqrt(lax.optimization_barrier(jnp.sum(rest * rest, axis=0)) + EPS)
    second = rest / first_below
    image_two = apply(second)
    second_top = lax.optimization_barrier(jnp.sum(first * image_two, axis=0))
    second_diag = lax.optimization_barrier(jnp.sum(second * image_two, axis=0))
    rest_two = image_two - second_top * first - second_diag * second
    second_below = jnp.sqrt(lax.optimization_barrier(jnp.sum(rest_two * rest_two, axis=0)) + EPS)
    weight_one, weight_two, estimate = least_squares(beta_norm, first_diag, first_below, second_top, second_diag, second_below)
    return (weight_one * first + weight_two * second, estimate)
```

```python
import jax
import jax.numpy as jnp
from jax import lax
from jax.experimental import pallas as pl
from jax.experimental.pallas import tpu as pltpu
from jax.sharding import PartitionSpec as P

P_SIZE = 128
K = 64
HALF = 128
EPS = 1e-06
BF = jnp.bfloat16
F32 = jnp.float32
MESH = pl.DeviceIdType.MESH
VMEM = pltpu.VMEM
DMA = pltpu.SemaphoreType.DMA
NEAR_STEPS = 8


def dot(a, b):
    return jnp.dot(a, b, preferred_element_type=F32)


def combine_kernel(
    near_target, near_source, near_count, far_target, far_source, near_ref, far_ref, c_ref, fl_ref, acc, facc
):
    step = pl.program_id(0)
    per_step = near_ref.shape[0]
    window = 24

    @pl.when(step == 0)
    def _():
        def zero(i, carry):
            acc[i] = jnp.zeros((P_SIZE, P_SIZE), F32)
            facc[i] = jnp.zeros((K, K), F32)
            return carry

        lax.fori_loop(0, acc.shape[0], zero, 0)

    live = jnp.clip(near_count[0] - step * per_step, 0, per_step)

    def add(j, carry):
        slot = step * per_step + j
        key = near_target[0, slot] * window + near_source[0, slot]
        acc[key] = acc[key] + near_ref[j].astype(F32)
        return carry

    lax.fori_loop(0, live, add, 0)

    @pl.when(step == pl.num_programs(0) - 1)
    def _():
        def add_far(j, carry):
            key = far_target[0, j] * window + far_source[0, j]
            facc[key] = facc[key] + far_ref[j].astype(F32)
            return carry

        lax.fori_loop(0, far_ref.shape[0], add_far, 0)

        def write(i, carry):
            t, s = i // window, i % window
            rows = pl.ds(pl.multiple_of(t * P_SIZE, P_SIZE), P_SIZE)
            lanes = pl.ds(pl.multiple_of(s * P_SIZE, P_SIZE), P_SIZE)
            c_ref[rows, lanes] = acc[i].astype(BF)
            return carry

        lax.fori_loop(0, acc.shape[0], write, 0)

        def write_far(i, carry):
            t, s = i // (window // 2), i % (window // 2)
            rows = pl.ds(pl.multiple_of(t * K, K), K)
            lanes = pl.ds(pl.multiple_of(s * 2 * K, 2 * K), 2 * K)
            both = jnp.concatenate([facc[2 * i], facc[2 * i + 1]], axis=1)
            fl_ref[rows, lanes] = both.astype(BF)
            return carry

        lax.fori_loop(0, facc.shape[0] // 2, write_far, 0)


def combine(near_target, near_source, near_count, far_target, far_source, near_blocks, far_leaf):
    smem = pl.BlockSpec(memory_space=pltpu.SMEM)
    slots = near_blocks.shape[0]
    per_step = slots // NEAR_STEPS
    return pl.pallas_call(
        combine_kernel,
        grid=(NEAR_STEPS,),
        out_shape=(
            jax.ShapeDtypeStruct((1024, 3072), BF),
            jax.ShapeDtypeStruct((512, 1536), BF),
        ),
        in_specs=[smem] * 5
        + [
            pl.BlockSpec((per_step, P_SIZE, P_SIZE), lambda i: (i, 0, 0)),
            pl.BlockSpec(far_leaf.shape, lambda i: (0, 0, 0)),
        ],
        out_specs=(
            pl.BlockSpec((1024, 3072), lambda i: (0, 0)),
            pl.BlockSpec((512, 1536), lambda i: (0, 0)),
        ),
        scratch_shapes=[VMEM((192, P_SIZE, P_SIZE), F32), VMEM((192, K, K), F32)],
        compiler_params=pltpu.CompilerParams(
            vmem_limit_bytes=56 * 1024 * 1024, dimension_semantics=("arbitrary",)
        ),
        cost_estimate=pl.CostEstimate(flops=10**7, bytes_accessed=20 * 10**6, transcendentals=0),
        name="combine",
    )(near_target, near_source, near_count, far_target, far_source, near_blocks, far_leaf)


def remote(src, dst, send, recv, device):
    return pltpu.make_async_remote_copy(
        src_ref=src, dst_ref=dst, send_sem=send, recv_sem=recv, device_id=device, device_id_type=MESH
    )


def place():
    x = lax.axis_index("grp")
    leaf = lax.axis_index("leaf")
    core = lax.rem(leaf, 2)
    chip = lax.div(leaf, 2)
    return x, lax.div(chip, 4), lax.rem(chip, 4), core


def leaf_of(z, y, core):
    return (z * 4 + y) * 2 + core


def apply_kernel(
    idx_s,
    v_ref,
    basis,
    falling_ref,
    c_hbm,
    fl_hbm,
    tv_hbm,
    s_hbm,
    down_hbm,
    w_ref,
    wb_ref,
    c_mat,
    fl_mat,
    tv_mat,
    s_mat,
    down_mat,
    win,
    cw,
    chalf,
    c2,
    local_half,
    rs_out,
    rs_in,
    q1x,
    q1,
    ag,
    gathered,
    far_out,
    far_in,
    l2,
    sib_out,
    sib_in,
    merged,
    load_sem,
    win_send,
    win_recv,
    sib_send,
    sib_recv,
    rs_send,
    rs_recv,
    q1x_send,
    q1x_recv,
    q1_send,
    q1_recv,
    ag_send,
    ag_recv,
    far_send,
    far_recv,
    l2_send,
    l2_recv,
):
    x, z, y, core = place()
    chip = z * 4 + y
    me = x * 32 + chip * 2 + core

    loads = [
        pltpu.make_async_copy(src, dst, load_sem.at[i])
        for i, (src, dst) in enumerate(
            ((tv_hbm, tv_mat), (c_hbm, c_mat), (fl_hbm, fl_mat), (s_hbm, s_mat), (down_hbm, down_mat))
        )
    ]
    for load in loads:
        load.start()

    sibling = (x, chip * 2 + 1 - core)
    before = (lax.div(me + 127, 32) % 4, lax.rem(me + 31, 32))
    after = (lax.div(me + 1, 32) % 4, lax.rem(me + 1, 32))
    has_before = me > 0
    has_after = me < 127

    def plane(k):
        tz = lax.rem(z + lax.div(k, 4), 4)
        ty = lax.rem(y + lax.rem(k, 4), 4)
        return tz * 4 + ty, (x, leaf_of(tz, ty, core))

    def along(axis, k):
        if axis == "x":
            return (lax.rem(x + k, 4), leaf_of(z, y, core))
        if axis == "y":
            return (x, leaf_of(z, lax.rem(y + k, 4), core))
        return (x, leaf_of(lax.rem(z + k, 4), y, core))

    barrier = pltpu.get_barrier_semaphore()

    def greet(k, carry):
        pl.semaphore_signal(barrier, inc=1, device_id=plane(k)[1], device_id_type=MESH)
        return carry

    lax.fori_loop(1, 16, greet, 0)
    for k in range(1, 4):
        pl.semaphore_signal(barrier, inc=1, device_id=along("x", k), device_id_type=MESH)
    pl.semaphore_signal(barrier, inc=1, device_id=sibling, device_id_type=MESH)

    @pl.when(has_before)
    def _():
        pl.semaphore_signal(barrier, inc=1, device_id=before, device_id_type=MESH)

    @pl.when(has_after)
    def _():
        pl.semaphore_signal(barrier, inc=1, device_id=after, device_id_type=MESH)

    win[pl.ds(1024, 1024), :] = v_ref[...]

    @pl.when(jnp.logical_not(has_before))
    def _():
        win[pl.ds(0, 1024), :] = jnp.zeros((1024, 256), BF)

    @pl.when(jnp.logical_not(has_after))
    def _():
        win[pl.ds(2048, 1024), :] = jnp.zeros((1024, 256), BF)

    def own_coeffs(i, carry):
        rows = pl.ds(pl.multiple_of(i * P_SIZE, P_SIZE), P_SIZE)
        part = dot(basis[8 + i], v_ref[rows, :]).astype(BF)
        into = pl.ds(pl.multiple_of(i * K, K), K)
        chalf[0, into, :] = part[:, :HALF]
        chalf[1, into, :] = part[:, HALF:]
        return carry

    lax.fori_loop(0, 8, own_coeffs, 0)
    c2[pl.ds(0, 512), :] = chalf[core]

    pl.semaphore_wait(barrier, 19 + has_before.astype(jnp.int32) + has_after.astype(jnp.int32))

    coeff_swap = remote(
        chalf.at[1 - core], c2.at[pl.ds(512, 512)], sib_send.at[0], sib_recv.at[0], sibling
    )
    coeff_swap.start()
    mine = win.at[pl.ds(1024, 1024)]
    to_after = remote(mine, win.at[pl.ds(0, 1024)], win_send.at[0], win_recv.at[0], after)
    to_before = remote(mine, win.at[pl.ds(2048, 1024)], win_send.at[1], win_recv.at[1], before)

    loads[0].wait()
    coeff_swap.wait_recv()

    def rs_copy(k):
        there, device = plane(k)
        return remote(rs_out.at[there], rs_in.at[k], rs_send.at[k], rs_recv.at[k], device)

    def rs_step(k, carry):
        there, _ = plane(k)
        rs_out[there] = dot(tv_mat[there], c2[...]).astype(BF)
        rs_copy(k).start()
        return carry

    lax.fori_loop(1, 16, rs_step, 0)
    rs_in[0] = dot(tv_mat[chip], c2[...]).astype(BF)

    @pl.when(has_after)
    def _():
        to_after.start()

    @pl.when(has_before)
    def _():
        to_before.start()

    def rs_sum(k, total):
        rs_copy(k).wait_recv()
        return total + rs_in[k].astype(F32)

    total = lax.fori_loop(1, 16, rs_sum, rs_in[0].astype(F32)).astype(BF)

    even = (z * 4 + y) * 4 + x
    odd = 64 + (y * 4 + x) * 4 + z
    ag[even] = total[0:K]
    ag[odd] = total[K : 2 * K]
    q1x[x] = total[2 * K : 3 * K]

    stages = (
        (0, 0, "x", even, 1),
        (1, 0, "z", odd, 1),
        (0, 1, "y", (z * 4 + y) * 4, 4),
        (1, 1, "x", 64 + (y * 4 + x) * 4, 4),
        (0, 2, "z", z * 16, 16),
        (1, 2, "y", 64 + y * 16, 16),
    )

    def ag_copy(number, k):
        _, _, axis, first, count = stages[number]
        part = ag.at[pl.ds(first, count)]
        i = number * 3 + k - 1
        return remote(part, part, ag_send.at[i], ag_recv.at[i], along(axis, k))

    def ag_start(number):
        for k in range(1, 4):
            ag_copy(number, k).start()

    def ag_land(number):
        for k in range(1, 4):
            ag_copy(number, k).wait_recv()

    def q1x_copy(k):
        return remote(q1x.at[x], q1x.at[x], q1x_send.at[k], q1x_recv.at[k], along("x", k))

    def q1_copy(k):
        part = q1.at[pl.ds(pl.multiple_of(chip * K, K), K)]
        return remote(part, part, q1_send.at[k], q1_recv.at[k], plane(k)[1])

    ag_start(0)
    ag_start(1)
    for k in range(1, 4):
        q1x_copy(k).start()
    ag_land(0)
    ag_start(2)
    ag_land(1)
    ag_start(3)
    for k in range(1, 4):
        q1x_copy(k).wait_recv()
    level_one = q1x[0].astype(F32) + q1x[1].astype(F32) + q1x[2].astype(F32) + q1x[3].astype(F32)
    q1[pl.ds(pl.multiple_of(chip * K, K), K), :] = level_one.astype(BF)

    def q1_start(k, carry):
        q1_copy(k).start()
        return carry

    lax.fori_loop(1, 16, q1_start, 0)
    ag_land(2)
    ag_start(4)
    ag_land(3)
    ag_start(5)

    @pl.when(has_before)
    def _():
        to_after_wait = remote(mine, win.at[pl.ds(0, 1024)], win_send.at[0], win_recv.at[0], after)
        to_after_wait.wait_recv()

    @pl.when(has_after)
    def _():
        to_before_wait = remote(mine, win.at[pl.ds(2048, 1024)], win_send.at[1], win_recv.at[1], before)
        to_before_wait.wait_recv()

    def window_coeffs(i, carry):
        rows = pl.ds(pl.multiple_of(i * P_SIZE, P_SIZE), P_SIZE)
        into = pl.ds(pl.multiple_of(i * K, K), K)
        cw[into, :] = dot(basis[i], win[rows, :]).astype(BF)
        return carry

    lax.fori_loop(0, 24, window_coeffs, 0)
    loads[1].wait()
    loads[2].wait()

    def leaf_far(i, carry):
        rows = pl.ds(pl.multiple_of(i * 128, 128), 128)
        part = dot(fl_mat[rows, :], cw[...])
        local_half[0, rows, :] = part[:, :HALF]
        local_half[1, rows, :] = part[:, HALF:]
        return carry

    lax.fori_loop(0, 4, leaf_far, 0)

    def near(i, carry):
        rows = pl.ds(pl.multiple_of(i * 128, 128), 128)
        w_ref[rows, :] = dot(c_mat[rows, :], win[...])
        return carry

    lax.fori_loop(0, 8, near, 0)

    loads[3].wait()
    loads[4].wait()
    ag_land(4)
    ag_land(5)

    def pick(j, carry):
        gathered[pl.ds(pl.multiple_of(j * K, K), K), :] = ag[idx_s[j]]
        return carry

    lax.fori_loop(0, 32, pick, 0)

    def far_copy(k):
        there, device = plane(k)
        return remote(far_out.at[there], far_in.at[k], far_send.at[k], far_recv.at[k], device)

    def far_step(k, carry):
        there, _ = plane(k)
        far_out[there] = dot(s_mat[there], gathered[...]).astype(BF)
        far_copy(k).start()
        return carry

    lax.fori_loop(1, 16, far_step, 0)

    def q1_land(k, carry):
        q1_copy(k).wait_recv()
        return carry

    lax.fori_loop(1, 16, q1_land, 0)
    own = dot(s_mat[chip], gathered[...]) + dot(falling_ref[...], q1[...])

    def far_sum(k, total):
        far_copy(k).wait_recv()
        return total + far_in[k].astype(F32)

    own = lax.fori_loop(1, 16, far_sum, own)
    l2[pl.ds(pl.multiple_of(chip * 128, 128), 128), :] = own.astype(BF)

    def l2_copy(k):
        part = l2.at[pl.ds(pl.multiple_of(chip * 128, 128), 128)]
        return remote(part, part, l2_send.at[k], l2_recv.at[k], plane(k)[1])

    def l2_start(k, carry):
        l2_copy(k).start()
        return carry

    lax.fori_loop(1, 16, l2_start, 0)

    def l2_land(k, carry):
        l2_copy(k).wait_recv()
        return carry

    lax.fori_loop(1, 16, l2_land, 0)

    def down_sibling(i, carry):
        rows = pl.ds(pl.multiple_of(512 + i * 128, 128), 128)
        into = pl.ds(pl.multiple_of(i * 128, 128), 128)
        sib_out[into, :] = dot(down_mat[rows, :], l2[...]).astype(BF)
        return carry

    lax.fori_loop(0, 4, down_sibling, 0)
    leaf_swap = remote(sib_out, sib_in, sib_send.at[1], sib_recv.at[1], sibling)
    leaf_swap.start()

    def down_own(i, carry):
        rows = pl.ds(pl.multiple_of(i * 128, 128), 128)
        merged[core, rows, :] = (local_half[core, rows, :] + dot(down_mat[rows, :], l2[...])).astype(BF)
        return carry

    lax.fori_loop(0, 4, down_own, 0)
    leaf_swap.wait_recv()
    merged[1 - core] = (local_half[1 - core] + sib_in[...].astype(F32)).astype(BF)

    def finish(i, carry):
        rows = pl.ds(pl.multiple_of(i * P_SIZE, P_SIZE), P_SIZE)
        part = pl.ds(pl.multiple_of(i * K, K), K)
        for h in range(2):
            lanes = pl.ds(h * HALF, HALF)
            value = w_ref[rows, lanes] + lax.dot_general(
                basis[8 + i], merged[h, part, :], (((0,), (0,)), ((), ())), preferred_element_type=F32
            )
            w_ref[rows, lanes] = value
            wb_ref[rows, lanes] = value.astype(BF)
        return carry

    lax.fori_loop(0, 8, finish, 0)

    coeff_swap.wait_send()
    leaf_swap.wait_send()

    @pl.when(has_after)
    def _():
        to_after.wait_send()

    @pl.when(has_before)
    def _():
        to_before.wait_send()

    for number in range(6):
        for k in range(1, 4):
            ag_copy(number, k).wait_send()
    for k in range(1, 4):
        q1x_copy(k).wait_send()

    def drain(k, carry):
        rs_copy(k).wait_send()
        q1_copy(k).wait_send()
        far_copy(k).wait_send()
        l2_copy(k).wait_send()
        return carry

    lax.fori_loop(1, 16, drain, 0)


def apply_operator(idx, v, basis, falling, c_mat, fl_mat, tv, s_mat, down):
    smem = pl.BlockSpec(memory_space=pltpu.SMEM)
    vmem = pl.BlockSpec(memory_space=pltpu.VMEM)
    anywhere = pl.BlockSpec(memory_space=pl.ANY)
    return pl.pallas_call(
        apply_kernel,
        out_shape=(
            jax.ShapeDtypeStruct((1024, 256), F32),
            jax.ShapeDtypeStruct((1024, 256), BF),
        ),
        in_specs=[smem, vmem, vmem, vmem] + [anywhere] * 5,
        out_specs=(vmem, vmem),
        scratch_shapes=[
            VMEM(c_mat.shape, BF),
            VMEM(fl_mat.shape, BF),
            VMEM(tv.shape, BF),
            VMEM(s_mat.shape, BF),
            VMEM(down.shape, BF),
            VMEM((3072, 256), BF),
            VMEM((1536, 256), BF),
            VMEM((2, 512, HALF), BF),
            VMEM((1024, HALF), BF),
            VMEM((2, 512, HALF), F32),
            VMEM((16, 192, HALF), BF),
            VMEM((16, 192, HALF), BF),
            VMEM((4, K, HALF), BF),
            VMEM((1024, HALF), BF),
            VMEM((128, K, HALF), BF),
            VMEM((2048, HALF), BF),
            VMEM((16, 128, HALF), BF),
            VMEM((16, 128, HALF), BF),
            VMEM((2048, HALF), BF),
            VMEM((512, HALF), BF),
            VMEM((512, HALF), BF),
            VMEM((2, 512, HALF), BF),
            DMA((5,)),
            DMA((2,)),
            DMA((2,)),
            DMA((2,)),
            DMA((2,)),
            DMA((16,)),
            DMA((16,)),
            DMA((4,)),
            DMA((4,)),
            DMA((16,)),
            DMA((16,)),
            DMA((18,)),
            DMA((18,)),
            DMA((16,)),
            DMA((16,)),
            DMA((16,)),
            DMA((16,)),
        ],
        compiler_params=pltpu.CompilerParams(
            collective_id=1, has_side_effects=True, vmem_limit_bytes=56 * 1024 * 1024
        ),
        name="apply_operator",
    )(idx, v, basis, falling, c_mat, fl_mat, tv, s_mat, down)


def least_squares(beta_norm, first_diag, first_below, second_top, second_diag, second_below):
    first_radius = jnp.sqrt(first_diag * first_diag + first_below * first_below)
    first_cos = first_diag / first_radius
    first_sin = first_below / first_radius
    upper_term = first_cos * second_top + first_sin * second_diag
    lower_term = first_cos * second_diag - first_sin * second_top
    second_radius = jnp.sqrt(lower_term * lower_term + second_below * second_below)
    second_cos = lower_term / second_radius
    second_sin = second_below / second_radius
    weight_two = -first_sin * beta_norm * second_cos / second_radius
    weight_one = (first_cos * beta_norm - upper_term * weight_two) / first_radius
    return (weight_one, weight_two, first_sin * second_sin * beta_norm)


def project(sums, sizes):
    pp, pa, aa, pb, ab, bb = sums
    size_p, size_a, size_b = sizes
    beta = jnp.sqrt(size_p * size_p * pp + EPS)
    scale_p, scale_a, scale_b = size_p / beta, size_a / beta, size_b / beta
    first_first = scale_p * scale_p * pp
    first_image = scale_p * scale_a * pa
    first_diag = first_image
    image_image = scale_a * scale_a * aa
    rest = image_image - first_diag * first_diag * (2.0 - first_first)
    first_below = jnp.sqrt(jnp.maximum(rest, 0.0) + EPS)
    inverse = 1.0 / first_below
    first_second = (first_image - first_diag * first_first) * inverse
    second_second = jnp.maximum(rest, 0.0) * inverse * inverse
    scale_two = scale_b * inverse
    diag_two = first_diag * inverse
    first_b = scale_p * scale_two * pb
    a_b = scale_a * scale_two * ab
    b_b = scale_two * scale_two * bb
    second_top = first_b - diag_two * first_image
    image_image_two = a_b - diag_two * image_image
    second_diag = (image_image_two - first_diag * second_top) * inverse
    square = b_b - 2.0 * diag_two * a_b + diag_two * diag_two * image_image
    rest_two = (
        square
        - second_top * second_top * (2.0 - first_first)
        - second_diag * second_diag * (2.0 - second_second)
        + 2.0 * second_top * second_diag * first_second
    )
    second_below = jnp.sqrt(jnp.maximum(rest_two, 0.0) + EPS)
    weight_one, weight_two, estimate = least_squares(
        beta, first_diag, first_below, second_top, second_diag, second_below
    )
    along_a = weight_two * inverse / beta
    along_p = weight_one / beta - along_a * first_diag
    return along_p, along_a, estimate


def finish_kernel(
    p_ref, w1_ref, w2_ref, panels_ref, pot_ref, out_ref, est_ref, high, low, w1_panel, part, box, send_sem, recv_sem
):
    x, z, y, core = place()

    def along(stage, k):
        if stage == 0:
            return (x, leaf_of(z, y, 1 - core))
        if stage == 1:
            return (lax.rem(x + k, 4), leaf_of(z, y, core))
        if stage == 2:
            return (x, leaf_of(z, lax.rem(y + k, 4), core))
        return (x, leaf_of(lax.rem(z + k, 4), y, core))

    peers = [(stage, k) for stage in range(4) for k in range(1, 2 if stage == 0 else 4)]
    coords = (core, x, y, z)

    barrier = pltpu.get_barrier_semaphore()
    for stage, k in peers:
        pl.semaphore_signal(barrier, inc=1, device_id=along(stage, k), device_id_type=MESH)

    def col_max(ref):
        return jnp.maximum(jnp.max(jnp.abs(ref[...]), axis=0, keepdims=True), 1e-30)

    size_p, size_a, size_b = col_max(p_ref), col_max(w1_ref), col_max(w2_ref)
    inv_p, inv_a, inv_b = 1.0 / size_p, 1.0 / size_a, 1.0 / size_b

    def add(i, carry):
        rows = pl.ds(pl.multiple_of(i * 32, 32), 32)
        p, a, b = p_ref[rows, :] * inv_p, w1_ref[rows, :] * inv_a, w2_ref[rows, :] * inv_b
        terms = (p * p, p * a, a * a, p * b, a * b, b * b)
        return tuple(c + jnp.sum(t.reshape(4, 8, 256), axis=0) for c, t in zip(carry, terms))

    sums = lax.fori_loop(0, 32, add, tuple(jnp.zeros((8, 256), F32) for _ in range(6)))
    sums = [jnp.sum(s, axis=0, keepdims=True) for s in sums]
    sizes = [size_p, size_a, size_b]

    pl.semaphore_wait(barrier, len(peers))

    pairs = ((0, 0), (0, 1), (1, 1), (0, 2), (1, 2), (2, 2))

    def copy(stage, k):
        i = stage * 4 + k
        return remote(
            box.at[stage, coords[stage]], box.at[stage, coords[stage]], send_sem.at[i], recv_sem.at[i], along(stage, k)
        )

    for stage in range(4):
        count = 2 if stage == 0 else 4
        for i in range(6):
            part[i : i + 1, :] = sums[i]
        for i in range(3):
            part[8 + i : 9 + i, :] = sizes[i]
        box[stage, coords[stage]] = part[...]
        for k in range(1, count):
            copy(stage, k).start()
        if stage == 0:
            value = w1_ref[...]
            top = value.astype(BF)
            high[...] = top
            low[...] = (value - top.astype(F32)).astype(BF)
        if stage in (1, 2):
            def unorder(i, carry):
                rows = pl.ds(pl.multiple_of(i * 128, 128), 128)
                wanted = lax.broadcasted_iota(jnp.int32, (128, 1024), 0) + i * 128
                hot = jnp.where(panels_ref[...] == wanted, 1.0, 0.0).astype(BF)
                w1_panel[rows, :] = dot(hot, high[...]) + dot(hot, low[...])
                return carry

            lax.fori_loop(4 * (stage - 1), 4 * stage, unorder, 0)
        for k in range(1, count):
            copy(stage, k).wait_recv()
        got = [box[stage, i] for i in range(count)]
        new_sizes = []
        for i in range(3):
            top_size = got[0][8 + i : 9 + i]
            for g in got[1:]:
                top_size = jnp.maximum(top_size, g[8 + i : 9 + i])
            new_sizes.append(top_size)
        factors = [[g[8 + i : 9 + i] / new_sizes[i] for i in range(3)] for g in got]
        sums = []
        for i, (a, b) in enumerate(pairs):
            value = got[0][i : i + 1] * (factors[0][a] * factors[0][b])
            for g, f in zip(got[1:], factors[1:]):
                value = value + g[i : i + 1] * (f[a] * f[b])
            sums.append(value)
        sizes = new_sizes

    along_p, along_a, estimate = project(sums, sizes)
    est_ref[...] = estimate

    def write(i, carry):
        rows = pl.ds(pl.multiple_of(i * 32, 32), 32)
        out_ref[rows, :] = along_p * pot_ref[rows, :] + along_a * w1_panel[rows, :]
        return carry

    lax.fori_loop(0, 32, write, 0)
    for stage, k in peers:
        copy(stage, k).wait_send()


def finish(p_slot, w1, w2, panels, potentials):
    vmem = pl.BlockSpec(memory_space=pltpu.VMEM)
    return pl.pallas_call(
        finish_kernel,
        out_shape=(jax.ShapeDtypeStruct((1024, 256), F32), jax.ShapeDtypeStruct((1, 256), F32)),
        in_specs=[vmem] * 5,
        out_specs=(vmem, vmem),
        scratch_shapes=[
            VMEM((1024, 256), BF),
            VMEM((1024, 256), BF),
            VMEM((1024, 256), F32),
            VMEM((16, 256), F32),
            VMEM((4, 4, 16, 256), F32),
            DMA((16,)),
            DMA((16,)),
        ],
        compiler_params=pltpu.CompilerParams(
            collective_id=2, has_side_effects=True, vmem_limit_bytes=40 * 1024 * 1024
        ),
        name="finish",
    )(p_slot, w1, w2, panels, potentials)


def on_device(
    potentials,
    leaf_panels,
    near_blocks,
    near_target,
    near_source,
    near_count,
    leaf_basis,
    far_leaf,
    far_leaf_target,
    far_leaf_source,
    leaf_transfer,
    leaf_parent,
    far_two,
    far_two_target,
    far_two_source,
    two_transfer,
    two_parent,
    far_one,
    far_one_target,
    far_one_source,
):
    group = lax.axis_index("grp")
    chip = lax.axis_index("leaf") // 2
    axes = ("grp", "leaf")

    swap = [(i, i ^ 1) for i in range(32)]
    numbers = jnp.concatenate([far_two_target[0], far_two_source[0], leaf_parent])
    matrices = jnp.concatenate([far_two, leaf_transfer], axis=0)
    other_numbers = lax.ppermute(numbers, "leaf", swap)
    other_matrices = lax.ppermute(matrices, "leaf", swap)
    basis_before = lax.ppermute(leaf_basis, axes, [(i, i + 1) for i in range(127)])
    basis_after = lax.ppermute(leaf_basis, axes, [(i + 1, i) for i in range(127)])

    c_mat, fl_mat = combine(
        near_target, near_source, near_count, far_leaf_target, far_leaf_source, near_blocks, far_leaf
    )

    high = potentials.astype(BF)
    low = (potentials - lax.reduce_precision(potentials, 8, 7)).astype(BF)
    slots = (leaf_panels[0][:, None] == jnp.arange(1024, dtype=jnp.int32)[None, :]).astype(BF)
    ordered = dot(slots, jnp.concatenate([high, low], axis=1))
    v0 = ordered[:, :256].astype(BF)
    p_slot = ordered[:, :256] + ordered[:, 256:]

    basis = jnp.concatenate([basis_before, leaf_basis, basis_after], axis=0)
    targets = jnp.concatenate([far_two_target[0], other_numbers[:16]])
    sources = jnp.concatenate([far_two_source[0], other_numbers[16:32]])
    parents = jnp.concatenate([leaf_parent, other_numbers[32:]])
    far_all = jnp.concatenate([far_two, other_matrices[:16]], axis=0)
    transfer = jnp.concatenate([leaf_transfer, other_matrices[16:]], axis=0)

    zero = jnp.zeros((), BF)
    clusters = jnp.arange(32, dtype=jnp.int32)
    parent_rows = jnp.repeat(parents, K)
    up = jnp.transpose(transfer, (2, 0, 1)).reshape(K, 1024)
    t2 = jnp.where(parent_rows[None, None, :] == clusters[:, None, None], up[None], zero)
    own_two = jnp.take(two_transfer, group * 32 + parents, axis=0)
    top_of = jnp.take(two_parent, group * 32 + parents)
    composite = jnp.einsum("lxb,lax->bla", own_two, transfer, preferred_element_type=F32)
    composite = composite.astype(BF).reshape(K, 1024)
    tops = jnp.arange(16, dtype=jnp.int32)
    v_up = jnp.where(jnp.repeat(top_of, K)[None, None, :] == tops[:, None, None], composite[None], zero)
    tv = jnp.concatenate([t2.reshape(16, 128, 1024), v_up], axis=1)

    down = jnp.where(
        parent_rows[:, None] == (jnp.arange(2048, dtype=jnp.int32) // K)[None, :],
        jnp.tile(transfer.reshape(1024, K), (1, 32)),
        zero,
    )

    far_flat = jnp.transpose(far_all, (1, 0, 2)).reshape(K, 2048)
    s_mat = jnp.where(
        jnp.repeat(targets, K)[None, None, :] == clusters[:, None, None], far_flat[None], zero
    ).reshape(16, 128, 2048)

    source_group, source_cluster = sources // 32, sources % 32
    source_chip, parity = source_cluster // 2, source_cluster % 2
    idx = jnp.where(
        parity == 0,
        source_chip * 4 + source_group,
        64 + ((source_chip % 4) * 4 + source_group) * 4 + source_chip // 4,
    )

    mine = group * 32 + chip * 2
    own_pair = lax.dynamic_slice_in_dim(two_transfer, mine, 2, 0)
    pair_top = lax.dynamic_slice_in_dim(two_parent, mine, 2, 0)
    pick = (far_one_target[None, None, :] == pair_top[:, None, None]) & (
        far_one_source[None, None, :] == tops[None, :, None]
    )
    rows_one = dot(pick.reshape(32, 32).astype(BF), far_one.reshape(32, K * K)).astype(BF)
    falling = jnp.einsum(
        "pax,pvxb->pavb", own_pair, rows_one.reshape(2, 16, K, K), preferred_element_type=F32
    )
    falling = falling.astype(BF).reshape(128, 1024)

    def operator(v):
        return apply_operator(idx, v, basis, falling, c_mat, fl_mat, tv, s_mat, down)

    w1, w1_short = operator(v0)
    w2, _ = operator(w1_short)
    solution_part, estimate = finish(p_slot, w1, w2, leaf_panels, potentials)
    return solution_part, estimate[0]


def solution(mesh):
    both = P(("grp", "leaf"))
    in_specs = (both,) * 15 + (P(),) * 5
    return jax.shard_map(
        on_device, mesh=mesh, in_specs=in_specs, out_specs=(both, P()), check_vma=False
    )
```

```python
import jax
import jax.numpy as jnp
from jax import lax
from jax.experimental import pallas as pl
from jax.experimental.pallas import tpu as pltpu
from jax.sharding import PartitionSpec as P

P_SIZE = 128
K = 64
HALF = 128
EPS = 1e-06
BF = jnp.bfloat16
F32 = jnp.float32
MESH = pl.DeviceIdType.MESH
VMEM = pltpu.VMEM
DMA = pltpu.SemaphoreType.DMA
NEAR_STEPS = 8


def dot(a, b):
    return jnp.dot(a, b, preferred_element_type=F32)


def combine_kernel(
    near_target, near_source, near_count, far_target, far_source, near_ref, far_ref, c_ref, fl_ref, acc, facc
):
    step = pl.program_id(0)
    per_step = near_ref.shape[0]
    window = 24

    @pl.when(step == 0)
    def _():
        def zero(i, carry):
            acc[i] = jnp.zeros((P_SIZE, P_SIZE), F32)
            facc[i] = jnp.zeros((K, K), F32)
            return carry

        lax.fori_loop(0, acc.shape[0], zero, 0, unroll=8)

    live = jnp.clip(near_count[0] - step * per_step, 0, per_step)

    def add(j, carry):
        slot = step * per_step + j
        key = near_target[0, slot] * window + near_source[0, slot]
        acc[key] = acc[key] + near_ref[j].astype(F32)
        return carry

    lax.fori_loop(0, live, add, 0)

    @pl.when(step == pl.num_programs(0) - 1)
    def _():
        def add_far(j, carry):
            key = far_target[0, j] * window + far_source[0, j]
            facc[key] = facc[key] + far_ref[j].astype(F32)
            return carry

        lax.fori_loop(0, far_ref.shape[0], add_far, 0, unroll=4)

        def write(i, carry):
            t, s = i // window, i % window
            rows = pl.ds(pl.multiple_of(t * P_SIZE, P_SIZE), P_SIZE)
            lanes = pl.ds(pl.multiple_of(s * P_SIZE, P_SIZE), P_SIZE)
            c_ref[rows, lanes] = acc[i].astype(BF)
            return carry

        lax.fori_loop(0, acc.shape[0], write, 0, unroll=8)

        def write_far(i, carry):
            t, s = i // (window // 2), i % (window // 2)
            rows = pl.ds(pl.multiple_of(t * K, K), K)
            lanes = pl.ds(pl.multiple_of(s * 2 * K, 2 * K), 2 * K)
            both = jnp.concatenate([facc[2 * i], facc[2 * i + 1]], axis=1)
            fl_ref[rows, lanes] = both.astype(BF)
            return carry

        lax.fori_loop(0, facc.shape[0] // 2, write_far, 0, unroll=8)


def combine(near_target, near_source, near_count, far_target, far_source, near_blocks, far_leaf):
    smem = pl.BlockSpec(memory_space=pltpu.SMEM)
    slots = near_blocks.shape[0]
    per_step = slots // NEAR_STEPS
    return pl.pallas_call(
        combine_kernel,
        grid=(NEAR_STEPS,),
        out_shape=(
            jax.ShapeDtypeStruct((1024, 3072), BF),
            jax.ShapeDtypeStruct((512, 1536), BF),
        ),
        in_specs=[smem] * 5
        + [
            pl.BlockSpec((per_step, P_SIZE, P_SIZE), lambda i: (i, 0, 0)),
            pl.BlockSpec(far_leaf.shape, lambda i: (0, 0, 0)),
        ],
        out_specs=(
            pl.BlockSpec((1024, 3072), lambda i: (0, 0)),
            pl.BlockSpec((512, 1536), lambda i: (0, 0)),
        ),
        scratch_shapes=[VMEM((192, P_SIZE, P_SIZE), F32), VMEM((192, K, K), F32)],
        compiler_params=pltpu.CompilerParams(
            vmem_limit_bytes=56 * 1024 * 1024, dimension_semantics=("arbitrary",)
        ),
        cost_estimate=pl.CostEstimate(flops=10**7, bytes_accessed=20 * 10**6, transcendentals=0),
        name="combine",
    )(near_target, near_source, near_count, far_target, far_source, near_blocks, far_leaf)


def remote(src, dst, send, recv, device):
    return pltpu.make_async_remote_copy(
        src_ref=src, dst_ref=dst, send_sem=send, recv_sem=recv, device_id=device, device_id_type=MESH
    )


def place():
    x = lax.axis_index("grp")
    leaf = lax.axis_index("leaf")
    core = lax.rem(leaf, 2)
    chip = lax.div(leaf, 2)
    return x, lax.div(chip, 4), lax.rem(chip, 4), core


def leaf_of(z, y, core):
    return (z * 4 + y) * 2 + core


def loop(start, stop, body, unroll=1):
    def step(i, carry):
        body(i)
        return carry

    lax.fori_loop(start, stop, step, 0, unroll=unroll)


def rows_at(i, size):
    return pl.ds(pl.multiple_of(i * size, size), size)


BUFFERS = dict(
    c_mat=VMEM((1024, 3072), BF),
    fl_mat=VMEM((512, 1536), BF),
    tv_mat=VMEM((16, 192, 1024), BF),
    s_mat=VMEM((16, 128, 2048), BF),
    down_mat=VMEM((1024, 2048), BF),
    top_mat=VMEM((128, 2048), BF),
    up=VMEM((K, 1024), BF),
    composite=VMEM((K, 1024), BF),
    far_flat=VMEM((K, 2048), BF),
    transfer=VMEM((16, K, K), BF),
    far_all=VMEM((32, K, K), BF),
    basis=VMEM((24, K, P_SIZE), BF),
    other_numbers=VMEM((8, 128), jnp.int32),
    other_s=pltpu.SMEM((8, 128), jnp.int32),
    v0=VMEM((1024, 256), BF),
    p_slot=VMEM((1024, 256), F32),
    w1=VMEM((1024, 256), F32),
    w2=VMEM((1024, 256), F32),
    high=VMEM((1024, 512), BF),
    w1_panel=VMEM((1024, 256), F32),
    part=VMEM((16, 256), F32),
    box=VMEM((4, 4, 16, 256), F32),
    win=VMEM((2, 3072, 256), BF),
    cw=VMEM((1536, 256), BF),
    chalf=VMEM((2, 512, HALF), BF),
    c2=VMEM((2, 1024, HALF), BF),
    local_half=VMEM((2, 512, HALF), F32),
    rs_out=VMEM((16, 192, HALF), BF),
    rs_in=VMEM((2, 16, 192, HALF), BF),
    q1x=VMEM((2, 4, K, HALF), BF),
    q1=VMEM((2, 16, K, HALF), BF),
    ag0=VMEM((2, 64, 48, HALF), BF),
    ag1=VMEM((2, 64, 48, HALF), BF),
    ag2=VMEM((2, 64, 32, HALF), BF),
    q_two=VMEM((128, K, HALF), BF),
    gathered=VMEM((2048, HALF), BF),
    far_out=VMEM((16, 128, HALF), BF),
    far_in=VMEM((2, 16, 128, HALF), BF),
    l2=VMEM((2, 2048, HALF), BF),
    sib_out=VMEM((512, HALF), BF),
    sib_in=VMEM((2, 512, HALF), BF),
    merged=VMEM((2, 512, HALF), BF),
    load_sem=DMA((3,)),
    ex_send=DMA((5,)),
    ex_recv=DMA((5,)),
    win_send=DMA((2, 2)),
    win_recv=DMA((2, 2)),
    sib_send=DMA((2, 2)),
    sib_recv=DMA((2, 2)),
    rs_send=DMA((2, 16)),
    rs_recv=DMA((2, 16)),
    q1x_send=DMA((2, 4)),
    q1x_recv=DMA((2, 4)),
    q1_send=DMA((2, 16)),
    q1_recv=DMA((2, 16)),
    ag_send=DMA((2, 27)),
    ag_recv=DMA((2, 27)),
    far_send=DMA((2, 16)),
    far_recv=DMA((2, 16)),
    l2_send=DMA((2, 16)),
    l2_recv=DMA((2, 16)),
    sum_send=DMA((16,)),
    sum_recv=DMA((16,)),
)
NAMES = tuple(BUFFERS)


def steps_kernel(
    numbers_s,
    one_target_s,
    one_source_s,
    numbers_ref,
    panels_row,
    panels_col,
    pot_ref,
    basis_ref,
    transfer_ref,
    far_ref,
    two_ref,
    one_ref,
    c_hbm,
    fl_hbm,
    out_ref,
    est_ref,
    *scratch,
):
    b = dict(zip(NAMES, scratch))
    basis, transfer, far_all, other_s = b["basis"], b["transfer"], b["far_all"], b["other_s"]
    up, composite, far_flat = b["up"], b["composite"], b["far_flat"]
    tv_mat, s_mat, down_mat, top_mat = b["tv_mat"], b["s_mat"], b["down_mat"], b["top_mat"]
    x, z, y, core = place()
    chip = z * 4 + y
    me = x * 32 + chip * 2 + core

    loads = [
        pltpu.make_async_copy(c_hbm, b["c_mat"], b["load_sem"].at[0]),
        pltpu.make_async_copy(fl_hbm, b["fl_mat"], b["load_sem"].at[1]),
    ]
    for load in loads:
        load.start()

    sibling = (x, chip * 2 + 1 - core)
    before = (lax.rem(lax.div(me + 127, 32), 4), lax.rem(me + 31, 32))
    after = (lax.rem(lax.div(me + 1, 32), 4), lax.rem(me + 1, 32))
    has_before = me > 0
    has_after = me < 127

    def plane(k):
        tz = lax.rem(z + lax.div(k, 4), 4)
        ty = lax.rem(y + lax.rem(k, 4), 4)
        return tz * 4 + ty, (x, leaf_of(tz, ty, core))

    def along(axis, k):
        if axis == "x":
            return (lax.rem(x + k, 4), leaf_of(z, y, core))
        if axis == "y":
            return (x, leaf_of(z, lax.rem(y + k, 4), core))
        if axis == "z":
            return (x, leaf_of(lax.rem(z + k, 4), y, core))
        return sibling

    barrier = pltpu.get_barrier_semaphore()

    def greet(k):
        pl.semaphore_signal(barrier, inc=1, device_id=plane(k)[1], device_id_type=MESH)

    loop(1, 16, greet)
    for k in range(1, 4):
        pl.semaphore_signal(barrier, inc=1, device_id=along("x", k), device_id_type=MESH)
    pl.semaphore_signal(barrier, inc=1, device_id=sibling, device_id_type=MESH)

    @pl.when(has_before)
    def _():
        pl.semaphore_signal(barrier, inc=1, device_id=before, device_id_type=MESH)

    @pl.when(has_after)
    def _():
        pl.semaphore_signal(barrier, inc=1, device_id=after, device_id_type=MESH)

    high = b["high"]

    def split(i):
        rows = rows_at(i, 128)
        value = pot_ref[rows, :]
        top = value.astype(BF)
        high[rows, pl.ds(0, 256)] = top
        high[rows, pl.ds(256, 256)] = (value - top.astype(F32)).astype(BF)

    loop(0, 8, split)

    def order(i):
        rows = rows_at(i, 128)
        wanted = lax.broadcasted_iota(jnp.int32, (128, 1024), 1)
        hot = jnp.where(panels_col[rows, :] == wanted, 1.0, 0.0).astype(BF)
        value = dot(hot, high[...])
        b["v0"][rows, :] = value[:, :256].astype(BF)
        b["p_slot"][rows, :] = value[:, :256] + value[:, 256:]

    loop(0, 8, order)
    basis[pl.ds(8, 8)] = basis_ref[...]
    transfer[pl.ds(0, 8)] = transfer_ref[...]
    far_all[pl.ds(0, 16)] = far_ref[...]

    for it in range(2):

        @pl.when(jnp.logical_not(has_before))
        def _():
            b["win"][it, pl.ds(0, 1024), :] = jnp.zeros((1024, 256), BF)

        @pl.when(jnp.logical_not(has_after))
        def _():
            b["win"][it, pl.ds(2048, 1024), :] = jnp.zeros((1024, 256), BF)

    @pl.when(jnp.logical_not(has_before))
    def _():
        basis[pl.ds(0, 8)] = jnp.zeros((8, K, P_SIZE), BF)

    @pl.when(jnp.logical_not(has_after))
    def _():
        basis[pl.ds(16, 8)] = jnp.zeros((8, K, P_SIZE), BF)

    pl.semaphore_wait(barrier, 19 + has_before.astype(jnp.int32) + has_after.astype(jnp.int32))

    ex_send, ex_recv = b["ex_send"], b["ex_recv"]
    swaps = [
        remote(numbers_ref, b["other_numbers"], ex_send.at[0], ex_recv.at[0], sibling),
        remote(transfer_ref, transfer.at[pl.ds(8, 8)], ex_send.at[1], ex_recv.at[1], sibling),
        remote(far_ref, far_all.at[pl.ds(16, 16)], ex_send.at[2], ex_recv.at[2], sibling),
    ]
    for swap in swaps:
        swap.start()
    basis_after = remote(basis_ref, basis.at[pl.ds(0, 8)], ex_send.at[3], ex_recv.at[3], after)
    basis_before = remote(basis_ref, basis.at[pl.ds(16, 8)], ex_send.at[4], ex_recv.at[4], before)

    @pl.when(has_after)
    def _():
        basis_after.start()

    @pl.when(has_before)
    def _():
        basis_before.start()

    def number(row, i, count):
        return numbers_s[row, i] if i < count else other_s[row, i - count]

    def spread(values, lanes):
        index = lax.broadcasted_iota(jnp.int32, (1, lanes), 1) // K
        found = jnp.zeros((1, lanes), jnp.int32)
        for i, value in enumerate(values):
            found = jnp.where(index == i, value, found)
        return found

    def chosen(found, value):
        return jnp.where(found == value, 1.0, 0.0).astype(BF)

    def build_up():
        for swap in swaps[:2]:
            swap.wait_recv()
        fetch = pltpu.make_async_copy(b["other_numbers"], other_s, b["load_sem"].at[2])
        fetch.start()
        fetch.wait()
        parents = [number(2, l, 8) for l in range(16)]
        for i in range(8):
            lanes = pl.ds(i * 128, 128)
            pair = transfer[pl.ds(2 * i, 2)].reshape(128, K)
            up[:, lanes] = pair.astype(F32).T.astype(BF)
            both = [dot(transfer[2 * i + h], two_ref[parents[2 * i + h]]) for h in range(2)]
            composite[:, lanes] = jnp.concatenate(both, axis=0).T.astype(BF)
        parent_lanes = spread(parents, 1024)
        top_lanes = spread([numbers_s[3, parent] for parent in parents], 1024)

        def build(c):
            tv_mat[c // 2, rows_at(c % 2, K), :] = up[...] * chosen(parent_lanes, c)

        loop(0, 32, build)

        def build_top(u):
            tv_mat[u, pl.ds(128, K), :] = composite[...] * chosen(top_lanes, u)

        loop(0, 16, build_top)

    def build_rest():
        swaps[2].wait_recv()
        targets = [number(0, j, 16) for j in range(32)]
        for i in range(16):
            far_flat[:, pl.ds(i * 128, 128)] = jnp.concatenate([far_all[2 * i], far_all[2 * i + 1]], axis=1)
        target_lanes = spread(targets, 2048)

        def build_far(c):
            s_mat[c // 2, rows_at(c % 2, K), :] = far_flat[...] * chosen(target_lanes, c)

        loop(0, 32, build_far)

        for l in range(16):
            pair = jnp.concatenate([transfer[l], transfer[l]], axis=1)
            half = lax.broadcasted_iota(jnp.int32, (1, 128), 1) // K
            parent = number(2, l, 8)

            def build_down(i, l=l, pair=pair, half=half, parent=parent):
                down_mat[pl.ds(l * K, K), rows_at(i, 128)] = pair * chosen(half + 2 * i, parent)

            loop(0, 16, build_down, 4)

        one_lanes = spread([one_target_s[j] for j in range(32)], 2048)
        for i in range(16):
            far_flat[:, pl.ds(i * 128, 128)] = jnp.concatenate([one_ref[2 * i], one_ref[2 * i + 1]], axis=1)
        for h in range(2):
            wanted = numbers_s[3, chip * 2 + h]
            top_mat[pl.ds(h * K, K), :] = far_flat[...] * chosen(one_lanes, wanted)

    def apply(it, v, w, wb, beside_rs, beside_far):
        win, chalf, c2 = b["win"].at[it], b["chalf"], b["c2"].at[it]
        local_half, cw = b["local_half"], b["cw"]
        rs_out, rs_in, q1x, q1 = b["rs_out"], b["rs_in"].at[it], b["q1x"].at[it], b["q1"].at[it]
        ag = [b["ag0"].at[it], b["ag1"].at[it], b["ag2"].at[it]]
        q_two, gathered = b["q_two"], b["gathered"]
        far_out, far_in, l2 = b["far_out"], b["far_in"].at[it], b["l2"].at[it]
        sib_out, sib_in, merged = b["sib_out"], b["sib_in"].at[it], b["merged"]

        to_after = remote(v, win.at[pl.ds(0, 1024)], b["win_send"].at[it, 0], b["win_recv"].at[it, 0], after)
        to_before = remote(v, win.at[pl.ds(2048, 1024)], b["win_send"].at[it, 1], b["win_recv"].at[it, 1], before)

        def own_coeffs(i):
            part = dot(basis[8 + i], v[rows_at(i, P_SIZE), :]).astype(BF)
            chalf[0, rows_at(i, K), :] = part[:, :HALF]
            chalf[1, rows_at(i, K), :] = part[:, HALF:]

        loop(0, 8, own_coeffs, 8)
        coeff_swap = remote(
            chalf.at[1 - core], c2.at[pl.ds(512, 512)], b["sib_send"].at[it, 0], b["sib_recv"].at[it, 0], sibling
        )
        coeff_swap.start()

        @pl.when(has_after)
        def _():
            to_after.start()

        @pl.when(has_before)
        def _():
            to_before.start()

        c2[pl.ds(0, 512), :] = chalf[core]
        win[pl.ds(1024, 1024), :] = v[...]
        if it == 0:
            build_up()
        coeff_swap.wait_recv()

        def rs_copy(k):
            there, device = plane(k)
            return remote(rs_out.at[there], rs_in.at[k], b["rs_send"].at[it, k], b["rs_recv"].at[it, k], device)

        def rs_step(k):
            there, _ = plane(k)
            rs_out[there] = dot(tv_mat[there], c2[...]).astype(BF)
            rs_copy(k).start()

        loop(1, 16, rs_step)
        rs_in[0] = dot(tv_mat[chip], c2[...]).astype(BF)
        beside_rs()

        def rs_sum(k, total):
            rs_copy(k).wait_recv()
            return total + rs_in[k].astype(F32)

        total = lax.fori_loop(1, 16, rs_sum, rs_in[0].astype(F32)).astype(BF)

        homes = ((z * 4 + y) * 4 + x, (x * 4 + z) * 4 + y, (y * 4 + x) * 4 + z)
        orders = (("x", "y", "z"), ("y", "z", "x"), ("z", "x", "y"))
        lasts = (z, x, y)
        ag[0][homes[0]] = total[0:48]
        ag[1][homes[1]] = total[48:96]
        ag[2][homes[2]] = total[96:128]
        q1x[x] = total[128:192]

        def ag_copy(stream, stage, k):
            if stage == 0:
                first, count = homes[stream], 1
            elif stage == 1:
                first, count = lax.div(homes[stream], 4) * 4, 4
            else:
                first, count = lasts[stream] * 16, 16
            part = ag[stream].at[pl.ds(first, count)]
            i = (stream * 3 + stage) * 3 + k - 1
            return remote(
                part, part, b["ag_send"].at[it, i], b["ag_recv"].at[it, i], along(orders[stream][stage], k)
            )

        def ag_start(stream, stage):
            for k in range(1, 4):
                ag_copy(stream, stage, k).start()

        def ag_land(stream, stage):
            for k in range(1, 4):
                ag_copy(stream, stage, k).wait_recv()

        def q1x_copy(k):
            return remote(q1x.at[x], q1x.at[x], b["q1x_send"].at[it, k], b["q1x_recv"].at[it, k], along("x", k))

        def q1_copy(k):
            part = q1.at[chip]
            return remote(part, part, b["q1_send"].at[it, k], b["q1_recv"].at[it, k], plane(k)[1])

        for stream in range(3):
            ag_start(stream, 0)
        for k in range(1, 4):
            q1x_copy(k).start()
        for stream in range(3):
            ag_land(stream, 0)
            ag_start(stream, 1)
        for k in range(1, 4):
            q1x_copy(k).wait_recv()
        level_one = q1x[0].astype(F32) + q1x[1].astype(F32) + q1x[2].astype(F32) + q1x[3].astype(F32)
        q1[chip] = level_one.astype(BF)

        def q1_start(k):
            q1_copy(k).start()

        for stream in range(3):
            ag_land(stream, 1)
            ag_start(stream, 2)
        loop(1, 16, q1_start)

        @pl.when(has_before)
        def _():
            to_after.wait_recv()
            if it == 0:
                basis_after.wait_recv()

        @pl.when(has_after)
        def _():
            to_before.wait_recv()
            if it == 0:
                basis_before.wait_recv()

        def window_coeffs(i):
            cw[rows_at(i, K), :] = dot(basis[i], win[rows_at(i, P_SIZE), :]).astype(BF)

        loop(0, 24, window_coeffs, 4)
        if it == 0:
            for load in loads:
                load.wait()

        def leaf_far(i):
            part = dot(b["fl_mat"][rows_at(i, 128), :], cw[...])
            local_half[0, rows_at(i, 128), :] = part[:, :HALF]
            local_half[1, rows_at(i, 128), :] = part[:, HALF:]

        loop(0, 4, leaf_far)

        def near(i):
            w[rows_at(i, 128), :] = dot(b["c_mat"][rows_at(i, 128), :], win[...])

        loop(0, 8, near)

        for stream in range(3):
            ag_land(stream, 2)

        def join(i):
            ip, g = i // 4, i % 4
            iz, iy = ip // 4, ip % 4
            first, second, third = ag[0][i], ag[1][(g * 4 + iz) * 4 + iy], ag[2][(iy * 4 + g) * 4 + iz]
            q_two[g * 32 + 2 * ip] = jnp.concatenate([first, second[0:16]], axis=0)
            q_two[g * 32 + 2 * ip + 1] = jnp.concatenate([second[16:48], third], axis=0)

        loop(0, 64, join, 4)

        for j in range(32):
            gathered[pl.ds(j * K, K), :] = q_two[number(1, j, 16)]

        def far_copy(k):
            there, device = plane(k)
            return remote(far_out.at[there], far_in.at[k], b["far_send"].at[it, k], b["far_recv"].at[it, k], device)

        def far_step(k):
            there, _ = plane(k)
            far_out[there] = dot(s_mat[there], gathered[...]).astype(BF)
            far_copy(k).start()

        loop(1, 16, far_step)
        own = dot(s_mat[chip], gathered[...])

        def q1_land(k):
            q1_copy(k).wait_recv()

        loop(1, 16, q1_land)
        for j in range(32):
            gathered[pl.ds(j * K, K), :] = q1[one_source_s[j]]
        l_one = dot(top_mat[...], gathered[...]).astype(BF)
        falling = [dot(two_ref[chip * 2 + h], l_one[h * K : (h + 1) * K]) for h in range(2)]
        own = own + jnp.concatenate(falling, axis=0)
        beside_far()

        def far_sum(k, total):
            far_copy(k).wait_recv()
            return total + far_in[k].astype(F32)

        own = lax.fori_loop(1, 16, far_sum, own)
        l2[rows_at(chip, 128), :] = own.astype(BF)

        def l2_copy(k):
            part = l2.at[rows_at(chip, 128)]
            return remote(part, part, b["l2_send"].at[it, k], b["l2_recv"].at[it, k], plane(k)[1])

        def l2_start(k):
            l2_copy(k).start()

        loop(1, 16, l2_start)

        def drain(k):
            rs_copy(k).wait_send()
            q1_copy(k).wait_send()
            far_copy(k).wait_send()

        loop(1, 16, drain)
        coeff_swap.wait_send()
        for stream in range(3):
            for stage in range(3):
                for k in range(1, 4):
                    ag_copy(stream, stage, k).wait_send()
        for k in range(1, 4):
            q1x_copy(k).wait_send()

        @pl.when(has_after)
        def _():
            to_after.wait_send()

        @pl.when(has_before)
        def _():
            to_before.wait_send()

        def l2_land(k):
            l2_copy(k).wait_recv()

        loop(1, 16, l2_land)

        def down_sibling(i):
            sib_out[rows_at(i, 128), :] = dot(down_mat[rows_at(i + 4, 128), :], l2[...]).astype(BF)

        loop(0, 4, down_sibling)
        leaf_swap = remote(sib_out, sib_in, b["sib_send"].at[it, 1], b["sib_recv"].at[it, 1], sibling)
        leaf_swap.start()

        def down_own(i):
            rows = rows_at(i, 128)
            merged[core, rows, :] = (local_half[core, rows, :] + dot(down_mat[rows, :], l2[...])).astype(BF)

        loop(0, 4, down_own)
        leaf_swap.wait_recv()
        merged[1 - core] = (local_half[1 - core] + sib_in[...].astype(F32)).astype(BF)

        def finish(i):
            rows = rows_at(i, P_SIZE)
            for h in range(2):
                lanes = pl.ds(h * HALF, HALF)
                value = w[rows, lanes] + lax.dot_general(
                    basis[8 + i],
                    merged[h, rows_at(i, K), :],
                    (((0,), (0,)), ((), ())),
                    preferred_element_type=F32,
                )
                w[rows, lanes] = value
                if wb is not None:
                    wb[rows, lanes] = value.astype(BF)

        loop(0, 8, finish, 2)
        leaf_swap.wait_send()

        def l2_sent(k):
            l2_copy(k).wait_send()

        loop(1, 16, l2_sent)

    p_slot, w1, w2, w1_panel = b["p_slot"], b["w1"], b["w2"], b["w1_panel"]

    def unorder():
        def split_image(i):
            rows = rows_at(i, 128)
            value = w1[rows, :]
            top = value.astype(BF)
            high[rows, pl.ds(0, 256)] = top
            high[rows, pl.ds(256, 256)] = (value - top.astype(F32)).astype(BF)

        loop(0, 8, split_image)

        def reorder(i):
            wanted = lax.broadcasted_iota(jnp.int32, (128, 1024), 0) + i * 128
            hot = jnp.where(panels_row[...] == wanted, 1.0, 0.0).astype(BF)
            value = dot(hot, high[...])
            w1_panel[rows_at(i, 128), :] = value[:, :256] + value[:, 256:]

        loop(0, 8, reorder)

    def col_max(ref):
        return jnp.maximum(jnp.max(jnp.abs(ref[...]), axis=0, keepdims=True), 1e-30)

    def col_sums(terms):
        def add(i, carry):
            return tuple(
                c + jnp.sum(t.reshape(4, 8, 256), axis=0) for c, t in zip(carry, terms(rows_at(i, 32)))
            )

        sums = lax.fori_loop(0, 32, add, tuple(jnp.zeros((8, 256), F32) for _ in range(3)), unroll=2)
        return [jnp.sum(s, axis=0, keepdims=True) for s in sums]

    early = []

    def early_sums():
        size_p, size_a = col_max(p_slot), col_max(w1)
        inv_p, inv_a = 1.0 / size_p, 1.0 / size_a

        def terms(rows):
            p, a = p_slot[rows, :] * inv_p, w1[rows, :] * inv_a
            return p * p, p * a, a * a

        early.extend((size_p, size_a, col_sums(terms)))

    v1 = b["v0"]
    apply(0, b["v0"], w1, v1, build_rest, lambda: None)
    for swap in swaps:
        swap.wait_send()

    @pl.when(has_after)
    def _():
        basis_after.wait_send()

    @pl.when(has_before)
    def _():
        basis_before.wait_send()

    apply(1, v1, w2, None, unorder, early_sums)

    size_p, size_a, sums = early
    size_b = col_max(w2)
    inv_p, inv_a, inv_b = 1.0 / size_p, 1.0 / size_a, 1.0 / size_b

    def late_terms(rows):
        value = w2[rows, :] * inv_b
        return p_slot[rows, :] * inv_p * value, w1[rows, :] * inv_a * value, value * value

    sums = sums + col_sums(late_terms)
    sizes = [size_p, size_a, size_b]
    part, box = b["part"], b["box"]
    pairs = ((0, 0), (0, 1), (1, 1), (0, 2), (1, 2), (2, 2))
    coords = (core, x, y, z)
    axes = ("core", "x", "y", "z")

    def sum_copy(stage, k):
        i = stage * 4 + k
        here = box.at[stage, coords[stage]]
        return remote(here, here, b["sum_send"].at[i], b["sum_recv"].at[i], along(axes[stage], k))

    for stage in range(4):
        count = 2 if stage == 0 else 4
        for i in range(6):
            part[i : i + 1, :] = sums[i]
        for i in range(3):
            part[8 + i : 9 + i, :] = sizes[i]
        box[stage, coords[stage]] = part[...]
        for k in range(1, count):
            sum_copy(stage, k).start()
        for k in range(1, count):
            sum_copy(stage, k).wait_recv()
        got = [box[stage, i] for i in range(count)]
        new_sizes = []
        for i in range(3):
            top_size = got[0][8 + i : 9 + i]
            for g in got[1:]:
                top_size = jnp.maximum(top_size, g[8 + i : 9 + i])
            new_sizes.append(top_size)
        factors = [[g[8 + i : 9 + i] / new_sizes[i] for i in range(3)] for g in got]
        sums = []
        for i, (first, second) in enumerate(pairs):
            value = got[0][i : i + 1] * (factors[0][first] * factors[0][second])
            for g, f in zip(got[1:], factors[1:]):
                value = value + g[i : i + 1] * (f[first] * f[second])
            sums.append(value)
        sizes = new_sizes

    along_p, along_a, estimate = project(sums, sizes)
    est_ref[...] = estimate

    def write(i):
        rows = rows_at(i, 32)
        out_ref[rows, :] = along_p * pot_ref[rows, :] + along_a * w1_panel[rows, :]

    loop(0, 32, write, 4)
    for stage in range(4):
        for k in range(1, 2 if stage == 0 else 4):
            sum_copy(stage, k).wait_send()


def both_steps(smem_args, vmem_args, hbm_args):
    smem = pl.BlockSpec(memory_space=pltpu.SMEM)
    vmem = pl.BlockSpec(memory_space=pltpu.VMEM)
    anywhere = pl.BlockSpec(memory_space=pl.ANY)
    return pl.pallas_call(
        steps_kernel,
        out_shape=(jax.ShapeDtypeStruct((1024, 256), F32), jax.ShapeDtypeStruct((1, 256), F32)),
        in_specs=[smem] * len(smem_args) + [vmem] * len(vmem_args) + [anywhere] * len(hbm_args),
        out_specs=(vmem, vmem),
        scratch_shapes=list(BUFFERS.values()),
        compiler_params=pltpu.CompilerParams(
            collective_id=1, has_side_effects=True, vmem_limit_bytes=60 * 1024 * 1024
        ),
        name="both_steps",
    )(*smem_args, *vmem_args, *hbm_args)


def least_squares(beta_norm, first_diag, first_below, second_top, second_diag, second_below):
    first_radius = jnp.sqrt(first_diag * first_diag + first_below * first_below)
    first_cos = first_diag / first_radius
    first_sin = first_below / first_radius
    upper_term = first_cos * second_top + first_sin * second_diag
    lower_term = first_cos * second_diag - first_sin * second_top
    second_radius = jnp.sqrt(lower_term * lower_term + second_below * second_below)
    second_cos = lower_term / second_radius
    second_sin = second_below / second_radius
    weight_two = -first_sin * beta_norm * second_cos / second_radius
    weight_one = (first_cos * beta_norm - upper_term * weight_two) / first_radius
    return (weight_one, weight_two, first_sin * second_sin * beta_norm)


def project(sums, sizes):
    pp, pa, aa, pb, ab, bb = sums
    size_p, size_a, size_b = sizes
    beta = jnp.sqrt(size_p * size_p * pp + EPS)
    scale_p, scale_a, scale_b = size_p / beta, size_a / beta, size_b / beta
    first_first = scale_p * scale_p * pp
    first_image = scale_p * scale_a * pa
    first_diag = first_image
    image_image = scale_a * scale_a * aa
    rest = image_image - first_diag * first_diag * (2.0 - first_first)
    first_below = jnp.sqrt(jnp.maximum(rest, 0.0) + EPS)
    inverse = 1.0 / first_below
    first_second = (first_image - first_diag * first_first) * inverse
    second_second = jnp.maximum(rest, 0.0) * inverse * inverse
    scale_two = scale_b * inverse
    diag_two = first_diag * inverse
    first_b = scale_p * scale_two * pb
    a_b = scale_a * scale_two * ab
    b_b = scale_two * scale_two * bb
    second_top = first_b - diag_two * first_image
    image_image_two = a_b - diag_two * image_image
    second_diag = (image_image_two - first_diag * second_top) * inverse
    square = b_b - 2.0 * diag_two * a_b + diag_two * diag_two * image_image
    rest_two = (
        square
        - second_top * second_top * (2.0 - first_first)
        - second_diag * second_diag * (2.0 - second_second)
        + 2.0 * second_top * second_diag * first_second
    )
    second_below = jnp.sqrt(jnp.maximum(rest_two, 0.0) + EPS)
    weight_one, weight_two, estimate = least_squares(
        beta, first_diag, first_below, second_top, second_diag, second_below
    )
    along_a = weight_two * inverse / beta
    along_p = weight_one / beta - along_a * first_diag
    return along_p, along_a, estimate


def on_device(
    potentials,
    leaf_panels,
    near_blocks,
    near_target,
    near_source,
    near_count,
    leaf_basis,
    far_leaf,
    far_leaf_target,
    far_leaf_source,
    leaf_transfer,
    leaf_parent,
    far_two,
    far_two_target,
    far_two_source,
    two_transfer,
    two_parent,
    far_one,
    far_one_target,
    far_one_source,
):
    group = lax.axis_index("grp")
    c_mat, fl_mat = combine(
        near_target, near_source, near_count, far_leaf_target, far_leaf_source, near_blocks, far_leaf
    )
    numbers = jnp.zeros((8, 128), jnp.int32)
    numbers = numbers.at[0, :16].set(far_two_target[0]).at[1, :16].set(far_two_source[0])
    numbers = numbers.at[2, :8].set(leaf_parent)
    numbers = numbers.at[3, :32].set(lax.dynamic_slice_in_dim(two_parent, group * 32, 32, 0))
    own_two = lax.dynamic_slice_in_dim(two_transfer, group * 32, 32, 0)
    solution_part, estimate = both_steps(
        (numbers, far_one_target, far_one_source),
        (
            numbers,
            leaf_panels,
            leaf_panels.reshape(1024, 1),
            potentials,
            leaf_basis,
            leaf_transfer,
            far_two,
            own_two,
            far_one,
        ),
        (c_mat, fl_mat),
    )
    return solution_part, estimate[0]


def solution(mesh):
    both = P(("grp", "leaf"))
    in_specs = (both,) * 15 + (P(),) * 5
    return jax.shard_map(
        on_device, mesh=mesh, in_specs=in_specs, out_specs=(both, P()), check_vma=False
    )
```

```python
import jax
import jax.numpy as jnp
from jax import lax
from jax.experimental import pallas as pl
from jax.experimental.pallas import tpu as pltpu
from jax.sharding import PartitionSpec as P

P_SIZE = 128
K = 64
HALF = 128
EPS = 1e-06
BF = jnp.bfloat16
F32 = jnp.float32
MESH = pl.DeviceIdType.MESH
VMEM = pltpu.VMEM
DMA = pltpu.SemaphoreType.DMA
NEAR_STEPS = 8


def dot(a, b):
    return jnp.dot(a, b, preferred_element_type=F32)


def combine_kernel(
    near_target,
    near_source,
    near_count,
    far_target,
    far_source,
    near_ref,
    far_ref,
    c_hbm,
    fl_ref,
    acc,
    stage,
    far_sum,
    sems,
):
    step = pl.program_id(0)
    per_step = near_ref.shape[0]
    window = 24

    @pl.when(step == 0)
    def _():
        def zero(i, carry):
            acc[i] = jnp.zeros((P_SIZE, P_SIZE), F32)
            return carry

        lax.fori_loop(0, acc.shape[0], zero, 0, unroll=8)

    live = jnp.clip(near_count[0] - step * per_step, 0, per_step)

    def add(j, carry):
        slot = step * per_step + j
        key = near_target[0, slot] * window + near_source[0, slot]
        acc[key] = acc[key] + near_ref[j].astype(F32)
        return carry

    lax.fori_loop(0, live, add, 0)

    keys = far_target[...] * window + far_source[...]
    row = lax.broadcasted_iota(jnp.int32, (96, keys.shape[1]), 0)
    wanted = (row % 8) * window + 2 * (row // 8)
    even = jnp.where(keys == wanted, 1.0, 0.0).astype(BF)
    odd = jnp.where(keys == wanted + 1, 1.0, 0.0).astype(BF)
    per_far = K // NEAR_STEPS
    turned = (((1,), (1,)), ((), ()))
    for i in range(per_far):
        a = step * per_far + i
        block = far_ref[i]
        both = jnp.concatenate(
            [
                lax.dot_general(even, block, turned, preferred_element_type=F32),
                lax.dot_general(odd, block, turned, preferred_element_type=F32),
            ],
            axis=1,
        )
        for s in range(window // 2):
            far_sum[pl.ds(s * 512 + a, 8, stride=K), :] = both[8 * s : 8 * s + 8]

    @pl.when(step == pl.num_programs(0) - 1)
    def _():
        copies = []
        for t in range(8):
            rows = pl.ds(t * P_SIZE, P_SIZE)

            def write(s, carry, t=t, rows=rows):
                lanes = pl.ds(pl.multiple_of(s * P_SIZE, P_SIZE), P_SIZE)
                stage[rows, lanes] = acc[t * window + s].astype(BF)
                return carry

            lax.fori_loop(0, window, write, 0, unroll=8)
            copies.append(pltpu.make_async_copy(stage.at[rows], c_hbm.at[rows], sems.at[t]))
            copies[-1].start()

        def write_far(i, carry):
            rows = pl.ds(pl.multiple_of(i * 16, 16), 16)
            for s in range(window // 2):
                part = far_sum[pl.ds(pl.multiple_of(s * 512 + i * 16, 16), 16), :]
                fl_ref[rows, pl.ds(s * P_SIZE, P_SIZE)] = part.astype(BF)
            return carry

        lax.fori_loop(0, 32, write_far, 0, unroll=2)
        for copy in copies:
            copy.wait()


def combine(near_target, near_source, near_count, far_target, far_source, near_blocks, far_leaf):
    smem = pl.BlockSpec(memory_space=pltpu.SMEM)
    vmem = pl.BlockSpec(memory_space=pltpu.VMEM)
    slots = near_blocks.shape[0]
    per_step = slots // NEAR_STEPS
    far_turned = jnp.transpose(far_leaf, (1, 2, 0))
    return pl.pallas_call(
        combine_kernel,
        grid=(NEAR_STEPS,),
        out_shape=(
            jax.ShapeDtypeStruct((1024, 3072), BF),
            jax.ShapeDtypeStruct((512, 1536), BF),
        ),
        in_specs=[smem] * 3
        + [vmem] * 2
        + [
            pl.BlockSpec((per_step, P_SIZE, P_SIZE), lambda i: (i, 0, 0)),
            pl.BlockSpec((K // NEAR_STEPS,) + far_turned.shape[1:], lambda i: (i, 0, 0)),
        ],
        out_specs=(
            pl.BlockSpec(memory_space=pl.ANY),
            pl.BlockSpec((512, 1536), lambda i: (0, 0)),
        ),
        scratch_shapes=[
            VMEM((192, P_SIZE, P_SIZE), F32),
            VMEM((1024, 3072), BF),
            VMEM((6144, P_SIZE), F32),
            DMA((8,)),
        ],
        compiler_params=pltpu.CompilerParams(
            vmem_limit_bytes=56 * 1024 * 1024, dimension_semantics=("arbitrary",)
        ),
        cost_estimate=pl.CostEstimate(flops=10**7, bytes_accessed=20 * 10**6, transcendentals=0),
        name="combine",
    )(near_target, near_source, near_count, far_target, far_source, near_blocks, far_turned)


def remote(src, dst, send, recv, device):
    return pltpu.make_async_remote_copy(
        src_ref=src, dst_ref=dst, send_sem=send, recv_sem=recv, device_id=device, device_id_type=MESH
    )


def place():
    x = lax.axis_index("grp")
    leaf = lax.axis_index("leaf")
    core = lax.rem(leaf, 2)
    chip = lax.div(leaf, 2)
    return x, lax.div(chip, 4), lax.rem(chip, 4), core


def leaf_of(z, y, core):
    return (z * 4 + y) * 2 + core


def loop(start, stop, body, unroll=1):
    def step(i, carry):
        body(i)
        return carry

    lax.fori_loop(start, stop, step, 0, unroll=unroll)


def rows_at(i, size):
    return pl.ds(pl.multiple_of(i * size, size), size)


BUFFERS = dict(
    c_mat=VMEM((1024, 3072), BF),
    fl_mat=VMEM((512, 1536), BF),
    tv_mat=VMEM((16, 128, 1024), BF),
    s_mat=VMEM((16, 128, 2048), BF),
    down_mat=VMEM((1024, 2048), BF),
    top_mat=VMEM((128, 2048), BF),
    turned=VMEM((4096, 128), F32),
    two=VMEM((128, K, K), BF),
    top_sums=VMEM((16, 128, K), BF),
    top_all=VMEM((128, 8192), BF),
    up=VMEM((K, 1024), BF),
    far_flat=VMEM((K, 2048), BF),
    transfer=VMEM((16, K, K), BF),
    far_all=VMEM((32, K, K), BF),
    basis=VMEM((24, K, P_SIZE), BF),
    other_target=VMEM((1, 16), jnp.int32),
    other_source=VMEM((1, 16), jnp.int32),
    other_parent=VMEM((1, 8), jnp.int32),
    target_o=pltpu.SMEM((1, 16), jnp.int32),
    source_o=pltpu.SMEM((1, 16), jnp.int32),
    parent_o=pltpu.SMEM((1, 8), jnp.int32),
    v0=VMEM((1024, 256), BF),
    p_slot=VMEM((1024, 256), F32),
    w1=VMEM((1024, 256), F32),
    w2=VMEM((1024, 256), F32),
    high=VMEM((1024, 512), BF),
    part=VMEM((16, 256), F32),
    box=VMEM((4, 4, 16, 256), F32),
    win=VMEM((2, 3072, 256), BF),
    cw=VMEM((1536, 256), BF),
    chalf=VMEM((2, 512, HALF), BF),
    c2=VMEM((2, 1024, HALF), BF),
    local_half=VMEM((2, 512, HALF), F32),
    rs_out=VMEM((16, 128, HALF), BF),
    rs_in=VMEM((2, 16, 128, HALF), BF),
    ag0=VMEM((2, 64, 48, HALF), BF),
    ag1=VMEM((2, 64, 48, HALF), BF),
    ag2=VMEM((2, 64, 32, HALF), BF),
    q_two=VMEM((128, K, HALF), BF),
    gathered=VMEM((2048, HALF), BF),
    far_out=VMEM((16, 128, HALF), BF),
    far_in=VMEM((2, 16, 128, HALF), BF),
    l2=VMEM((2, 2048, HALF), BF),
    sib_out=VMEM((512, HALF), BF),
    sib_in=VMEM((2, 512, HALF), BF),
    merged=VMEM((2, 512, HALF), BF),
    load_sem=DMA((5,)),
    ex_send=DMA((7,)),
    ex_recv=DMA((7,)),
    win_send=DMA((2, 4)),
    win_recv=DMA((2, 4)),
    sib_send=DMA((2, 2)),
    sib_recv=DMA((2, 2)),
    rs_send=DMA((2, 32)),
    rs_recv=DMA((2, 32)),
    ag_send=DMA((2, 27)),
    ag_recv=DMA((2, 27)),
    far_send=DMA((2, 32)),
    far_recv=DMA((2, 32)),
    l2_send=DMA((2, 32)),
    l2_recv=DMA((2, 32)),
    sum_send=DMA((16,)),
    sum_recv=DMA((16,)),
)
NAMES = tuple(BUFFERS)


def steps_kernel(
    target_s,
    source_s,
    parent_s,
    two_parent_s,
    one_target_s,
    one_source_s,
    target_ref,
    source_ref,
    parent_ref,
    panels_row,
    pot_ref,
    basis_ref,
    transfer_ref,
    far_ref,
    two_ref,
    one_ref,
    c_hbm,
    fl_hbm,
    w1_panel,
    weights_ref,
    *scratch,
):
    b = dict(zip(NAMES, scratch))
    basis, transfer, far_all = b["basis"], b["transfer"], b["far_all"]
    up, far_flat = b["up"], b["far_flat"]
    tv_mat, s_mat, down_mat, top_mat = b["tv_mat"], b["s_mat"], b["down_mat"], b["top_mat"]
    x, z, y, core = place()
    chip = z * 4 + y
    me = x * 32 + chip * 2 + core

    loads = [
        pltpu.make_async_copy(c_hbm, b["c_mat"], b["load_sem"].at[0]),
        pltpu.make_async_copy(fl_hbm, b["fl_mat"], b["load_sem"].at[1]),
    ]
    for load in loads:
        load.start()

    sibling = (x, chip * 2 + 1 - core)
    before = (lax.rem(lax.div(me + 127, 32), 4), lax.rem(me + 31, 32))
    after = (lax.rem(lax.div(me + 1, 32), 4), lax.rem(me + 1, 32))
    has_before = me > 0
    has_after = me < 127

    def plane(k):
        k = lax.rem(5 * k, 16)
        tz = lax.rem(z + lax.div(k, 4), 4)
        ty = lax.rem(y + lax.rem(k, 4), 4)
        return tz * 4 + ty, (x, leaf_of(tz, ty, core))

    def along(axis, k):
        if axis == "x":
            return (lax.rem(x + k, 4), leaf_of(z, y, core))
        if axis == "y":
            return (x, leaf_of(z, lax.rem(y + k, 4), core))
        if axis == "z":
            return (x, leaf_of(lax.rem(z + k, 4), y, core))
        return sibling

    barrier = pltpu.get_barrier_semaphore()

    def greet(k):
        pl.semaphore_signal(barrier, inc=1, device_id=plane(k)[1], device_id_type=MESH)

    loop(1, 16, greet)
    for k in range(1, 4):
        pl.semaphore_signal(barrier, inc=1, device_id=along("x", k), device_id_type=MESH)
    pl.semaphore_signal(barrier, inc=1, device_id=sibling, device_id_type=MESH)

    @pl.when(has_before)
    def _():
        pl.semaphore_signal(barrier, inc=1, device_id=before, device_id_type=MESH)

    @pl.when(has_after)
    def _():
        pl.semaphore_signal(barrier, inc=1, device_id=after, device_id_type=MESH)

    high = b["high"]

    def split(i):
        rows = rows_at(i, 128)
        value = pot_ref[rows, :]
        top = value.astype(BF)
        high[rows, pl.ds(0, 256)] = top
        high[rows, pl.ds(256, 256)] = (value - top.astype(F32)).astype(BF)

    loop(0, 8, split)

    def order(i):
        rows = rows_at(i, 128)
        wanted = lax.broadcasted_iota(jnp.int32, (128, 128), 1).astype(F32)
        column = jnp.broadcast_to(panels_row[:, rows].astype(F32), (128, 128)).T
        hot = [jnp.where(column == wanted + 128.0 * q, 1.0, 0.0).astype(BF) for q in range(8)]
        hot = jnp.concatenate(hot, axis=1)
        value = dot(hot, high[...])
        b["v0"][rows, :] = value[:, :256].astype(BF)
        b["p_slot"][rows, :] = value[:, :256] + value[:, 256:]

    loop(0, 8, order)
    basis[pl.ds(8, 8)] = basis_ref[...]
    transfer[pl.ds(0, 8)] = transfer_ref[...]
    far_all[pl.ds(0, 16)] = far_ref[...]

    for it in range(2):

        @pl.when(jnp.logical_not(has_before))
        def _():
            b["win"][it, pl.ds(0, 1024), :] = jnp.zeros((1024, 256), BF)

        @pl.when(jnp.logical_not(has_after))
        def _():
            b["win"][it, pl.ds(2048, 1024), :] = jnp.zeros((1024, 256), BF)

    @pl.when(jnp.logical_not(has_before))
    def _():
        basis[pl.ds(0, 8)] = jnp.zeros((8, K, P_SIZE), BF)

    @pl.when(jnp.logical_not(has_after))
    def _():
        basis[pl.ds(16, 8)] = jnp.zeros((8, K, P_SIZE), BF)

    pl.semaphore_wait(barrier, 19 + has_before.astype(jnp.int32) + has_after.astype(jnp.int32))

    ex_send, ex_recv = b["ex_send"], b["ex_recv"]
    swaps = [
        remote(target_ref, b["other_target"], ex_send.at[0], ex_recv.at[0], sibling),
        remote(source_ref, b["other_source"], ex_send.at[5], ex_recv.at[5], sibling),
        remote(parent_ref, b["other_parent"], ex_send.at[6], ex_recv.at[6], sibling),
        remote(transfer_ref, transfer.at[pl.ds(8, 8)], ex_send.at[1], ex_recv.at[1], sibling),
        remote(far_ref, far_all.at[pl.ds(16, 16)], ex_send.at[2], ex_recv.at[2], sibling),
    ]
    for swap in swaps:
        swap.start()
    basis_after = remote(basis_ref, basis.at[pl.ds(0, 8)], ex_send.at[3], ex_recv.at[3], after)
    basis_before = remote(basis_ref, basis.at[pl.ds(16, 8)], ex_send.at[4], ex_recv.at[4], before)

    @pl.when(has_after)
    def _():
        basis_after.start()

    @pl.when(has_before)
    def _():
        basis_before.start()

    numbers = (
        (target_s, b["target_o"]),
        (source_s, b["source_o"]),
        (parent_s, b["parent_o"]),
    )

    def number(row, i, count):
        own, other = numbers[row]
        return own[0, i] if i < count else other[0, i - count]

    def spread(values, lanes):
        index = lax.broadcasted_iota(jnp.int32, (1, lanes), 1) // K
        found = jnp.zeros((1, lanes), jnp.int32)
        for i, value in enumerate(values):
            found = jnp.where(index == i, value, found)
        return found

    def chosen(found, value):
        return jnp.where(found == value, 1.0, 0.0).astype(BF)

    def build_up():
        for swap in swaps[:4]:
            swap.wait_recv()
        fetches = [
            pltpu.make_async_copy(b["other_" + name], b[name + "_o"], b["load_sem"].at[2 + i])
            for i, name in enumerate(("target", "source", "parent"))
        ]
        for fetch in fetches:
            fetch.start()
        for fetch in fetches:
            fetch.wait()
        parents = [number(2, l, 8) for l in range(16)]
        for i in range(8):
            lanes = pl.ds(i * 128, 128)
            pair = transfer[pl.ds(2 * i, 2)].reshape(128, K)
            up[:, lanes] = pair.astype(F32).T.astype(BF)
        parent_lanes = spread(parents, 1024)

        def build(c):
            tv_mat[c // 2, rows_at(c % 2, K), :] = up[...] * chosen(parent_lanes, c)

        loop(0, 32, build)

    def build_rest():
        swaps[4].wait_recv()
        targets = [number(0, j, 16) for j in range(32)]
        for i in range(16):
            far_flat[:, pl.ds(i * 128, 128)] = jnp.concatenate([far_all[2 * i], far_all[2 * i + 1]], axis=1)
        target_lanes = spread(targets, 2048)

        def build_far(c):
            s_mat[c // 2, rows_at(c % 2, K), :] = far_flat[...] * chosen(target_lanes, c)

        loop(0, 32, build_far)

        turned, two = b["turned"], b["two"]

        def turn(a):
            block = two_ref[a].astype(F32).T
            turned[pl.ds(a, K, stride=K), :] = jnp.concatenate([block[:K], block[K:]], axis=1)

        loop(0, K, turn, 4)

        def shorten(c):
            block = turned[rows_at(c, K), :].astype(BF)
            two[c] = block[:, :K]
            two[K + c] = block[:, K:]

        loop(0, K, shorten, 4)

    def build_top():
        one_lanes = spread([one_target_s[j] for j in range(32)], 2048)
        for i in range(16):
            far_flat[:, pl.ds(i * 128, 128)] = jnp.concatenate([one_ref[2 * i], one_ref[2 * i + 1]], axis=1)
        for h in range(2):
            wanted = two_parent_s[x * 32 + chip * 2 + h]
            top_mat[pl.ds(h * K, K), :] = far_flat[...] * chosen(one_lanes, wanted)

        turned, two, sums, top_all = (b[n] for n in ("turned", "two", "top_sums", "top_all"))

        for h in range(2):
            value = dot(two[x * 32 + chip * 2 + h], top_mat[pl.ds(h * K, K), :])
            for i in range(16):
                turned[pl.ds(i * 128 + h * K, K), :] = value[:, i * 128 : (i + 1) * 128]
        source_lanes = spread([one_source_s[j] for j in range(32)], 2048)

        def pick_sources(u):
            found = jnp.where(source_lanes == u, 1.0, 0.0)
            value = turned[pl.ds(0, 128), :] * found[:, 0:128]
            for i in range(1, 16):
                value = value + turned[pl.ds(i * 128, 128), :] * found[:, i * 128 : (i + 1) * 128]
            sums[u] = (value[:, :K] + value[:, K:]).astype(BF)

        loop(0, 16, pick_sources)

        def whole(i):
            pair = [
                lax.dot_general(
                    sums[two_parent_s[2 * i + h]], two[2 * i + h], (((1,), (1,)), ((), ())), preferred_element_type=F32
                )
                for h in range(2)
            ]
            top_all[:, rows_at(i, 128)] = jnp.concatenate(pair, axis=1).astype(BF)

        loop(0, 64, whole, 4)

    def build_last():
        for l in range(16):
            pair = jnp.concatenate([transfer[l], transfer[l]], axis=1)
            half = lax.broadcasted_iota(jnp.int32, (1, 128), 1) // K
            parent = number(2, l, 8)

            def build_down(i, l=l, pair=pair, half=half, parent=parent):
                down_mat[pl.ds(l * K, K), rows_at(i, 128)] = pair * chosen(half + 2 * i, parent)

            loop(0, 16, build_down, 4)

    def apply(it, v, w, wb, beside_rs, beside_ag, beside_l2):
        win, chalf, c2 = b["win"].at[it], b["chalf"], b["c2"].at[it]
        local_half, cw = b["local_half"], b["cw"]
        rs_out, rs_in = b["rs_out"], b["rs_in"].at[it]
        ag = [b["ag0"].at[it], b["ag1"].at[it], b["ag2"].at[it]]
        q_two, gathered = b["q_two"], b["gathered"]
        far_out, far_in, l2 = b["far_out"], b["far_in"].at[it], b["l2"].at[it]
        sib_out, sib_in, merged = b["sib_out"], b["sib_in"].at[it], b["merged"]

        def window_copy(side, half):
            first, device = (0, after) if side == 0 else (2048, before)
            i = side * 2 + half
            return remote(
                v.at[pl.ds(half * 512, 512)],
                win.at[pl.ds(first + half * 512, 512)],
                b["win_send"].at[it, i],
                b["win_recv"].at[it, i],
                device,
            )

        def window_start(half):
            @pl.when(has_after)
            def _():
                window_copy(0, half).start()

            @pl.when(has_before)
            def _():
                window_copy(1, half).start()

        def window_land(half):
            @pl.when(has_before)
            def _():
                window_copy(0, half).wait_recv()

            @pl.when(has_after)
            def _():
                window_copy(1, half).wait_recv()


        def own_coeffs(i):
            part = dot(basis[8 + i], v[rows_at(i, P_SIZE), :]).astype(BF)
            chalf[0, rows_at(i, K), :] = part[:, :HALF]
            chalf[1, rows_at(i, K), :] = part[:, HALF:]

        loop(0, 8, own_coeffs, 8)
        coeff_swap = remote(
            chalf.at[1 - core], c2.at[pl.ds(512, 512)], b["sib_send"].at[it, 0], b["sib_recv"].at[it, 0], sibling
        )
        coeff_swap.start()

        window_start(0)
        if it == 0:
            window_start(1)
        c2[pl.ds(0, 512), :] = chalf[core]
        win[pl.ds(1024, 1024), :] = v[...]
        if it == 0:
            build_up()
        coeff_swap.wait_recv()

        rs_rows = (pl.ds(0, 96), pl.ds(96, 32))

        def rs_copy(h, k):
            there, device = plane(k)
            rows, i = rs_rows[h], h * 16 + k
            return remote(
                rs_out.at[there, rows], rs_in.at[k, rows], b["rs_send"].at[it, i], b["rs_recv"].at[it, i], device
            )

        for h in range(2):

            def rs_step(k, h=h):
                there, _ = plane(k)
                rs_out[there, rs_rows[h]] = dot(tv_mat[there, rs_rows[h]], c2[...]).astype(BF)
                rs_copy(h, k).start()

            loop(1, 16, rs_step)
        rs_in[0] = dot(tv_mat[chip], c2[...]).astype(BF)
        beside_rs()

        def rs_total(h):
            def rs_sum(k, total):
                rs_copy(h, k).wait_recv()
                return total + rs_in[k, rs_rows[h]].astype(F32)

            return lax.fori_loop(1, 16, rs_sum, rs_in[0, rs_rows[h]].astype(F32)).astype(BF)

        homes = ((z * 4 + y) * 4 + x, (x * 4 + z) * 4 + y, (y * 4 + x) * 4 + z)
        orders = (("x", "y", "z"), ("y", "z", "x"), ("z", "x", "y"))
        lasts = (z, x, y)

        def ag_copy(stream, stage, k):
            if stage == 0:
                first, count = homes[stream], 1
            elif stage == 1:
                first, count = lax.div(homes[stream], 4) * 4, 4
            else:
                first, count = lasts[stream] * 16, 16
            part = ag[stream].at[pl.ds(first, count)]
            i = (stream * 3 + stage) * 3 + k - 1
            return remote(
                part, part, b["ag_send"].at[it, i], b["ag_recv"].at[it, i], along(orders[stream][stage], k)
            )

        def ag_start(stream, stage):
            for k in range(1, 4):
                ag_copy(stream, stage, k).start()

        def ag_land(stream, stage):
            for k in range(1, 4):
                ag_copy(stream, stage, k).wait_recv()

        total = rs_total(0)
        ag[0][homes[0]] = total[0:48]
        ag[1][homes[1]] = total[48:96]
        ag_start(0, 0)
        ag_start(1, 0)
        total = rs_total(1)
        ag[2][homes[2]] = total
        ag_start(2, 0)
        for stream in range(3):
            ag_land(stream, 0)
            ag_start(stream, 1)
        for stream in range(3):
            ag_land(stream, 1)
            ag_start(stream, 2)

        beside_ag()

        window_land(0)
        if it == 0:
            for load in loads:
                load.wait()

            @pl.when(has_before)
            def _():
                basis_after.wait_recv()

            @pl.when(has_after)
            def _():
                basis_before.wait_recv()

        def window_coeffs(i):
            cw[rows_at(i, K), :] = dot(basis[i], win[rows_at(i, P_SIZE), :]).astype(BF)

        loop(0, 4, window_coeffs, 4)
        loop(8, 20, window_coeffs, 4)

        def near_dot(i, first, size):
            return dot(b["c_mat"][rows_at(i, 128), pl.ds(first, size)], win[pl.ds(first, size), :])

        def near_most(i):
            w[rows_at(i, 128), :] = near_dot(i, 0, 512) + near_dot(i, 1024, 1536)

        loop(0, 8, near_most)
        for stream in range(3):
            ag_land(stream, 2)

        if it == 1:
            window_start(1)

        def join(i):
            ip, g = i // 4, i % 4
            iz, iy = ip // 4, ip % 4
            first, second, third = ag[0][i], ag[1][(g * 4 + iz) * 4 + iy], ag[2][(iy * 4 + g) * 4 + iz]
            q_two[g * 32 + 2 * ip] = jnp.concatenate([first, second[0:16]], axis=0)
            q_two[g * 32 + 2 * ip + 1] = jnp.concatenate([second[16:48], third], axis=0)

        loop(0, 64, join, 4)

        for j in range(32):
            gathered[pl.ds(j * K, K), :] = q_two[number(1, j, 16)]

        def far_copy(h, k):
            there, device = plane(k)
            rows, i = pl.ds(h * K, K), h * 16 + k
            return remote(
                far_out.at[there, rows],
                far_in.at[k, rows],
                b["far_send"].at[it, i],
                b["far_recv"].at[it, i],
                device,
            )

        for h in range(2):

            def far_step(k, h=h):
                there, _ = plane(k)
                far_out[there, pl.ds(h * K, K)] = dot(s_mat[there, pl.ds(h * K, K)], gathered[...]).astype(BF)
                far_copy(h, k).start()

            loop(1, 16, far_step)
        own = dot(s_mat[chip], gathered[...])

        def fall(i, total):
            part = q_two[pl.ds(i * 16, 16)].reshape(1024, HALF)
            return total + dot(b["top_all"][:, rows_at(i, 1024)], part)

        own = lax.fori_loop(0, 8, fall, own)

        def l2_copy(h, k):
            part = l2.at[rows_at(chip * 2 + h, K)]
            i = h * 16 + k
            return remote(part, part, b["l2_send"].at[it, i], b["l2_recv"].at[it, i], plane(k)[1])

        for h in range(2):

            def far_sum(k, total, h=h):
                far_copy(h, k).wait_recv()
                return total + far_in[k, pl.ds(h * K, K)].astype(F32)

            half_sum = lax.fori_loop(1, 16, far_sum, own[h * K : (h + 1) * K])
            l2[rows_at(chip * 2 + h, K), :] = half_sum.astype(BF)

            def l2_start(k, h=h):
                l2_copy(h, k).start()

            loop(1, 16, l2_start)

        def drain(k):
            for h in range(2):
                rs_copy(h, k).wait_send()
                far_copy(h, k).wait_send()

        loop(1, 16, drain)
        coeff_swap.wait_send()
        for stream in range(3):
            for stage in range(3):
                for k in range(1, 4):
                    ag_copy(stream, stage, k).wait_send()

        for half in range(2):

            @pl.when(has_after)
            def _(half=half):
                window_copy(0, half).wait_send()

            @pl.when(has_before)
            def _(half=half):
                window_copy(1, half).wait_send()

        beside_l2()

        window_land(1)
        loop(4, 8, window_coeffs, 4)
        loop(20, 24, window_coeffs, 4)

        def leaf_far(i):
            part = dot(b["fl_mat"][rows_at(i, 128), :], cw[...])
            local_half[0, rows_at(i, 128), :] = part[:, :HALF]
            local_half[1, rows_at(i, 128), :] = part[:, HALF:]

        loop(0, 4, leaf_far)

        def near_rest(i):
            w[rows_at(i, 128), :] = w[rows_at(i, 128), :] + near_dot(i, 512, 512) + near_dot(i, 2560, 512)

        loop(0, 8, near_rest)

        def l2_land(k):
            for h in range(2):
                l2_copy(h, k).wait_recv()

        loop(1, 16, l2_land)

        def down_sibling(i):
            sib_out[rows_at(i, 128), :] = dot(down_mat[rows_at(i + 4, 128), :], l2[...]).astype(BF)

        loop(0, 4, down_sibling)
        leaf_swap = remote(sib_out, sib_in, b["sib_send"].at[it, 1], b["sib_recv"].at[it, 1], sibling)
        leaf_swap.start()

        def down_own(i):
            rows = rows_at(i, 128)
            merged[core, rows, :] = (local_half[core, rows, :] + dot(down_mat[rows, :], l2[...])).astype(BF)

        loop(0, 4, down_own)
        leaf_swap.wait_recv()
        merged[1 - core] = (local_half[1 - core] + sib_in[...].astype(F32)).astype(BF)

        def finish(i):
            rows = rows_at(i, P_SIZE)
            for h in range(2):
                lanes = pl.ds(h * HALF, HALF)
                value = w[rows, lanes] + lax.dot_general(
                    basis[8 + i],
                    merged[h, rows_at(i, K), :],
                    (((0,), (0,)), ((), ())),
                    preferred_element_type=F32,
                )
                w[rows, lanes] = value
                if wb is not None:
                    wb[rows, lanes] = value.astype(BF)

        loop(0, 8, finish, 2)
        leaf_swap.wait_send()

        def l2_sent(k):
            for h in range(2):
                l2_copy(h, k).wait_send()

        loop(1, 16, l2_sent)

    p_slot, w1, w2 = b["p_slot"], b["w1"], b["w2"]

    def unorder():
        def split_image(i):
            rows = rows_at(i, 128)
            value = w1[rows, :]
            top = value.astype(BF)
            high[rows, pl.ds(0, 256)] = top
            high[rows, pl.ds(256, 256)] = (value - top.astype(F32)).astype(BF)

        loop(0, 8, split_image)

        def reorder(i):
            wanted = lax.broadcasted_iota(jnp.int32, (128, 1024), 0) + i * 128
            hot = jnp.where(panels_row[...] == wanted, 1.0, 0.0).astype(BF)
            value = dot(hot, high[...])
            w1_panel[rows_at(i, 128), :] = value[:, :256] + value[:, 256:]

        loop(0, 8, reorder)

    def col_max(ref):
        return jnp.maximum(jnp.max(jnp.abs(ref[...]), axis=0, keepdims=True), 1e-30)

    def col_sums(terms):
        def add(i, carry):
            return tuple(
                c + jnp.sum(t.reshape(4, 8, 256), axis=0) for c, t in zip(carry, terms(rows_at(i, 32)))
            )

        sums = lax.fori_loop(0, 32, add, tuple(jnp.zeros((8, 256), F32) for _ in range(3)), unroll=2)
        return [jnp.sum(s, axis=0, keepdims=True) for s in sums]

    early = []

    def early_sums():
        size_p, size_a = col_max(p_slot), col_max(w1)
        inv_p, inv_a = 1.0 / size_p, 1.0 / size_a

        def terms(rows):
            p, a = p_slot[rows, :] * inv_p, w1[rows, :] * inv_a
            return p * p, p * a, a * a

        early.extend((size_p, size_a, col_sums(terms)))

    v1 = b["v0"]
    apply(0, b["v0"], w1, v1, build_rest, build_top, build_last)
    for swap in swaps:
        swap.wait_send()

    @pl.when(has_after)
    def _():
        basis_after.wait_send()

    @pl.when(has_before)
    def _():
        basis_before.wait_send()

    apply(1, v1, w2, None, unorder, early_sums, lambda: None)

    size_p, size_a, sums = early
    size_b = col_max(w2)
    inv_p, inv_a, inv_b = 1.0 / size_p, 1.0 / size_a, 1.0 / size_b

    def late_terms(rows):
        value = w2[rows, :] * inv_b
        return p_slot[rows, :] * inv_p * value, w1[rows, :] * inv_a * value, value * value

    sums = sums + col_sums(late_terms)
    sizes = [size_p, size_a, size_b]
    part, box = b["part"], b["box"]
    pairs = ((0, 0), (0, 1), (1, 1), (0, 2), (1, 2), (2, 2))
    coords = (core, x, y, z)
    axes = ("core", "x", "y", "z")

    def sum_copy(stage, k):
        i = stage * 4 + k
        here = box.at[stage, coords[stage]]
        return remote(here, here, b["sum_send"].at[i], b["sum_recv"].at[i], along(axes[stage], k))

    for stage in range(4):
        count = 2 if stage == 0 else 4
        for i in range(6):
            part[i : i + 1, :] = sums[i]
        for i in range(3):
            part[8 + i : 9 + i, :] = sizes[i]
        box[stage, coords[stage]] = part[...]
        for k in range(1, count):
            sum_copy(stage, k).start()
        for k in range(1, count):
            sum_copy(stage, k).wait_recv()
        got = [box[stage, i] for i in range(count)]
        new_sizes = []
        for i in range(3):
            top_size = got[0][8 + i : 9 + i]
            for g in got[1:]:
                top_size = jnp.maximum(top_size, g[8 + i : 9 + i])
            new_sizes.append(top_size)
        factors = [[g[8 + i : 9 + i] / new_sizes[i] for i in range(3)] for g in got]
        sums = []
        for i, (first, second) in enumerate(pairs):
            value = got[0][i : i + 1] * (factors[0][first] * factors[0][second])
            for g, f in zip(got[1:], factors[1:]):
                value = value + g[i : i + 1] * (f[first] * f[second])
            sums.append(value)
        sizes = new_sizes

    along_p, along_a, estimate = project(sums, sizes)
    weights_ref[0:1, :] = along_p
    weights_ref[1:2, :] = along_a
    weights_ref[2:3, :] = estimate
    for stage in range(4):
        for k in range(1, 2 if stage == 0 else 4):
            sum_copy(stage, k).wait_send()


def both_steps(smem_args, vmem_args, hbm_args):
    smem = pl.BlockSpec(memory_space=pltpu.SMEM)
    vmem = pl.BlockSpec(memory_space=pltpu.VMEM)
    anywhere = pl.BlockSpec(memory_space=pl.ANY)
    return pl.pallas_call(
        steps_kernel,
        out_shape=(jax.ShapeDtypeStruct((1024, 256), F32), jax.ShapeDtypeStruct((8, 256), F32)),
        in_specs=[smem] * len(smem_args) + [vmem] * len(vmem_args) + [anywhere] * len(hbm_args),
        out_specs=(vmem, vmem),
        scratch_shapes=list(BUFFERS.values()),
        compiler_params=pltpu.CompilerParams(
            collective_id=1, has_side_effects=True, vmem_limit_bytes=62 * 1024 * 1024
        ),
        name="both_steps",
    )(*smem_args, *vmem_args, *hbm_args)


def result_kernel(weights_ref, pot_ref, image_ref, out_ref, est_ref):
    out_ref[...] = weights_ref[0:1, :] * pot_ref[...] + weights_ref[1:2, :] * image_ref[...]
    est_ref[...] = weights_ref[2, :]


def result(weights, potentials, image):
    return pl.pallas_call(
        result_kernel,
        out_shape=(jax.ShapeDtypeStruct((1024, 256), F32), jax.ShapeDtypeStruct((256,), F32)),
        compiler_params=pltpu.CompilerParams(vmem_limit_bytes=16 * 1024 * 1024),
        name="result",
    )(weights, potentials, image)


def least_squares(beta_norm, first_diag, first_below, second_top, second_diag, second_below):
    first_radius = jnp.sqrt(first_diag * first_diag + first_below * first_below)
    first_cos = first_diag / first_radius
    first_sin = first_below / first_radius
    upper_term = first_cos * second_top + first_sin * second_diag
    lower_term = first_cos * second_diag - first_sin * second_top
    second_radius = jnp.sqrt(lower_term * lower_term + second_below * second_below)
    second_cos = lower_term / second_radius
    second_sin = second_below / second_radius
    weight_two = -first_sin * beta_norm * second_cos / second_radius
    weight_one = (first_cos * beta_norm - upper_term * weight_two) / first_radius
    return (weight_one, weight_two, first_sin * second_sin * beta_norm)


def project(sums, sizes):
    pp, pa, aa, pb, ab, bb = sums
    size_p, size_a, size_b = sizes
    beta = jnp.sqrt(size_p * size_p * pp + EPS)
    scale_p, scale_a, scale_b = size_p / beta, size_a / beta, size_b / beta
    first_first = scale_p * scale_p * pp
    first_image = scale_p * scale_a * pa
    first_diag = first_image
    image_image = scale_a * scale_a * aa
    rest = image_image - first_diag * first_diag * (2.0 - first_first)
    first_below = jnp.sqrt(jnp.maximum(rest, 0.0) + EPS)
    inverse = 1.0 / first_below
    first_second = (first_image - first_diag * first_first) * inverse
    second_second = jnp.maximum(rest, 0.0) * inverse * inverse
    scale_two = scale_b * inverse
    diag_two = first_diag * inverse
    first_b = scale_p * scale_two * pb
    a_b = scale_a * scale_two * ab
    b_b = scale_two * scale_two * bb
    second_top = first_b - diag_two * first_image
    image_image_two = a_b - diag_two * image_image
    second_diag = (image_image_two - first_diag * second_top) * inverse
    square = b_b - 2.0 * diag_two * a_b + diag_two * diag_two * image_image
    rest_two = (
        square
        - second_top * second_top * (2.0 - first_first)
        - second_diag * second_diag * (2.0 - second_second)
        + 2.0 * second_top * second_diag * first_second
    )
    second_below = jnp.sqrt(jnp.maximum(rest_two, 0.0) + EPS)
    weight_one, weight_two, estimate = least_squares(
        beta, first_diag, first_below, second_top, second_diag, second_below
    )
    along_a = weight_two * inverse / beta
    along_p = weight_one / beta - along_a * first_diag
    return along_p, along_a, estimate


def on_device(
    potentials,
    leaf_panels,
    near_blocks,
    near_target,
    near_source,
    near_count,
    leaf_basis,
    far_leaf,
    far_leaf_target,
    far_leaf_source,
    leaf_transfer,
    leaf_parent,
    far_two,
    far_two_target,
    far_two_source,
    two_transfer,
    two_parent,
    far_one,
    far_one_target,
    far_one_source,
):
    c_mat, fl_mat = combine(
        near_target, near_source, near_count, far_leaf_target, far_leaf_source, near_blocks, far_leaf
    )
    own_numbers = (far_two_target, far_two_source, leaf_parent.reshape(1, 8))
    image, weights = both_steps(
        own_numbers + (two_parent, far_one_target, far_one_source),
        own_numbers
        + (
            leaf_panels,
            potentials,
            leaf_basis,
            leaf_transfer,
            far_two,
            jnp.transpose(two_transfer, (1, 2, 0)),
            far_one,
        ),
        (c_mat, fl_mat),
    )
    return result(weights, potentials, image)


def solution(mesh):
    both = P(("grp", "leaf"))
    in_specs = (both,) * 15 + (P(),) * 5
    return jax.shard_map(
        on_device, mesh=mesh, in_specs=in_specs, out_specs=(both, P()), check_vma=False
    )
```

```python
import jax
import jax.numpy as jnp
from jax import lax
from jax.experimental import pallas as pl
from jax.experimental.pallas import tpu as pltpu
from jax.sharding import PartitionSpec as P

P_SIZE = 128
K = 64
HALF = 128
EPS = 1e-06
BF = jnp.bfloat16
F32 = jnp.float32
MESH = pl.DeviceIdType.MESH
VMEM = pltpu.VMEM
DMA = pltpu.SemaphoreType.DMA
NEAR_STEPS = 8


def dot(a, b):
    return jnp.dot(a, b, preferred_element_type=F32)


def combine_kernel(
    near_target,
    near_source,
    near_count,
    far_target,
    far_source,
    near_hbm,
    far_hbm,
    c_hbm,
    fl_hbm,
    blocks,
    far_blocks,
    acc,
    stage,
    far_sum,
    far_stage,
    load_sems,
    sems,
):
    window = 24
    per_step = blocks.shape[0] // NEAR_STEPS
    far_load = pltpu.make_async_copy(far_hbm, far_blocks, load_sems.at[NEAR_STEPS])
    far_load.start()

    def load(step):
        part = pl.ds(step * per_step, per_step)
        return pltpu.make_async_copy(near_hbm.at[part], blocks.at[part], load_sems.at[step])

    for step in range(NEAR_STEPS):
        load(step).start()

    def zero(i, carry):
        acc[i] = jnp.zeros((P_SIZE, P_SIZE), F32)
        return carry

    lax.fori_loop(0, acc.shape[0], zero, 0, unroll=8)
    live = near_count[0]

    def add(j, carry):
        key = near_target[0, j] * window + near_source[0, j]
        acc[key] = acc[key] + blocks[j].astype(F32)
        return carry

    keys = far_target[...] * window + far_source[...]
    row = lax.broadcasted_iota(jnp.int32, (96, keys.shape[1]), 0)
    wanted = (row % 8) * window + 2 * (row // 8)
    even = jnp.where(keys == wanted, 1.0, 0.0).astype(BF)
    odd = jnp.where(keys == wanted + 1, 1.0, 0.0).astype(BF)
    turned = (((1,), (1,)), ((), ()))
    per_far = K // NEAR_STEPS
    far_load.wait()

    def take(step, carry):
        for i in range(per_far):
            a = step * per_far + i
            block = far_blocks[a]
            both = jnp.concatenate(
                [
                    lax.dot_general(even, block, turned, preferred_element_type=F32),
                    lax.dot_general(odd, block, turned, preferred_element_type=F32),
                ],
                axis=1,
            )
            for s in range(window // 2):
                far_sum[pl.ds(s * 512 + a, 8, stride=K), :] = both[8 * s : 8 * s + 8]
        load(step).wait()
        first = step * per_step
        lax.fori_loop(first, jnp.clip(live, first, first + per_step), add, 0)
        return carry

    lax.fori_loop(0, NEAR_STEPS, take, 0)

    def write_far(i, carry):
        rows = pl.ds(pl.multiple_of(i * 16, 16), 16)
        for s in range(12):
            part = far_sum[pl.ds(pl.multiple_of(s * 512 + i * 16, 16), 16), :]
            far_stage[rows, pl.ds(s * P_SIZE, P_SIZE)] = part.astype(BF)
        return carry

    lax.fori_loop(0, 32, write_far, 0, unroll=2)
    copies = [pltpu.make_async_copy(far_stage, fl_hbm, sems.at[8])]
    copies[0].start()
    for t in range(8):
        rows = pl.ds(t * P_SIZE, P_SIZE)

        def write(s, carry, t=t, rows=rows):
            lanes = pl.ds(pl.multiple_of(s * P_SIZE, P_SIZE), P_SIZE)
            stage[rows, lanes] = acc[t * window + s].astype(BF)
            return carry

        lax.fori_loop(0, window, write, 0, unroll=8)
        copies.append(pltpu.make_async_copy(stage.at[rows], c_hbm.at[rows], sems.at[t]))
        copies[-1].start()
    for copy in copies:
        copy.wait()


def combine(near_target, near_source, near_count, far_target, far_source, near_blocks, far_leaf):
    smem = pl.BlockSpec(memory_space=pltpu.SMEM)
    vmem = pl.BlockSpec(memory_space=pltpu.VMEM)
    anywhere = pl.BlockSpec(memory_space=pl.ANY)
    far_turned = jnp.transpose(far_leaf, (1, 2, 0))
    return pl.pallas_call(
        combine_kernel,
        out_shape=(jax.ShapeDtypeStruct((1024, 3072), BF), jax.ShapeDtypeStruct((512, 1536), BF)),
        in_specs=[smem] * 3 + [vmem] * 2 + [anywhere] * 2,
        out_specs=(anywhere, anywhere),
        scratch_shapes=[
            VMEM(near_blocks.shape, BF),
            VMEM(far_turned.shape, BF),
            VMEM((192, P_SIZE, P_SIZE), F32),
            VMEM((1024, 3072), BF),
            VMEM((6144, P_SIZE), F32),
            VMEM((512, 1536), BF),
            DMA((NEAR_STEPS + 1,)),
            DMA((9,)),
        ],
        compiler_params=pltpu.CompilerParams(vmem_limit_bytes=60 * 1024 * 1024),
        cost_estimate=pl.CostEstimate(flops=10**7, bytes_accessed=20 * 10**6, transcendentals=0),
        name="combine",
    )(near_target, near_source, near_count, far_target, far_source, near_blocks, far_turned)


def remote(src, dst, send, recv, device):
    return pltpu.make_async_remote_copy(
        src_ref=src, dst_ref=dst, send_sem=send, recv_sem=recv, device_id=device, device_id_type=MESH
    )


def place():
    x = lax.axis_index("grp")
    leaf = lax.axis_index("leaf")
    core = lax.rem(leaf, 2)
    chip = lax.div(leaf, 2)
    return x, lax.div(chip, 4), lax.rem(chip, 4), core


def leaf_of(z, y, core):
    return (z * 4 + y) * 2 + core


def loop(start, stop, body, unroll=1):
    def step(i, carry):
        body(i)
        return carry

    lax.fori_loop(start, stop, step, 0, unroll=unroll)


def rows_at(i, size):
    return pl.ds(pl.multiple_of(i * size, size), size)


BUFFERS = dict(
    c_mat=VMEM((1024, 3072), BF),
    fl_mat=VMEM((512, 1536), BF),
    tv_mat=VMEM((16, 128, 1024), BF),
    s_mat=VMEM((16, 128, 2048), BF),
    down_mat=VMEM((1024, 2048), BF),
    top_mat=VMEM((128, 2048), BF),
    turned=VMEM((4096, 128), F32),
    two=VMEM((128, K, K), BF),
    top_sums=VMEM((16, 128, K), BF),
    top_all=VMEM((128, 8192), BF),
    up=VMEM((K, 1024), BF),
    far_flat=VMEM((K, 2048), BF),
    transfer=VMEM((16, K, K), BF),
    far_all=VMEM((32, K, K), BF),
    basis=VMEM((24, K, P_SIZE), BF),
    other_target=VMEM((1, 16), jnp.int32),
    other_source=VMEM((1, 16), jnp.int32),
    other_parent=VMEM((1, 8), jnp.int32),
    target_o=pltpu.SMEM((1, 16), jnp.int32),
    source_o=pltpu.SMEM((1, 16), jnp.int32),
    parent_o=pltpu.SMEM((1, 8), jnp.int32),
    v0=VMEM((1024, 256), BF),
    p_slot=VMEM((1024, 256), F32),
    w1=VMEM((1024, 256), F32),
    w2=VMEM((1024, 256), F32),
    high=VMEM((1024, 512), BF),
    part=VMEM((16, 256), F32),
    box=VMEM((4, 4, 16, 256), F32),
    win=VMEM((2, 3072, 256), BF),
    cw=VMEM((1536, 256), BF),
    chalf=VMEM((2, 512, HALF), BF),
    c2=VMEM((2, 1024, HALF), BF),
    local_half=VMEM((2, 512, HALF), F32),
    rs_out=VMEM((16, 128, HALF), BF),
    rs_in=VMEM((2, 16, 128, HALF), BF),
    ag0=VMEM((2, 64, 48, HALF), BF),
    ag1=VMEM((2, 64, 48, HALF), BF),
    ag2=VMEM((2, 64, 32, HALF), BF),
    q_two=VMEM((128, K, HALF), BF),
    gathered=VMEM((2048, HALF), BF),
    far_out=VMEM((16, 128, HALF), BF),
    far_in=VMEM((2, 16, 128, HALF), BF),
    l2=VMEM((2, 2048, HALF), BF),
    sib_out=VMEM((512, HALF), BF),
    sib_in=VMEM((2, 512, HALF), BF),
    merged=VMEM((2, 512, HALF), BF),
    load_sem=DMA((5,)),
    ex_send=DMA((7,)),
    ex_recv=DMA((7,)),
    win_send=DMA((2, 4)),
    win_recv=DMA((2, 4)),
    sib_send=DMA((2, 2)),
    sib_recv=DMA((2, 2)),
    rs_send=DMA((2, 32)),
    rs_recv=DMA((2, 32)),
    ag_send=DMA((2, 27)),
    ag_recv=DMA((2, 27)),
    far_send=DMA((2, 32)),
    far_recv=DMA((2, 32)),
    l2_send=DMA((2, 32)),
    l2_recv=DMA((2, 32)),
    sum_send=DMA((16,)),
    sum_recv=DMA((16,)),
)
NAMES = tuple(BUFFERS)


def steps_kernel(
    target_s,
    source_s,
    parent_s,
    two_parent_s,
    one_target_s,
    one_source_s,
    target_ref,
    source_ref,
    parent_ref,
    panels_row,
    pot_ref,
    basis_ref,
    transfer_ref,
    far_ref,
    two_ref,
    one_ref,
    c_hbm,
    fl_hbm,
    w1_panel,
    weights_ref,
    *scratch,
):
    b = dict(zip(NAMES, scratch))
    basis, transfer, far_all = b["basis"], b["transfer"], b["far_all"]
    up, far_flat = b["up"], b["far_flat"]
    tv_mat, s_mat, down_mat, top_mat = b["tv_mat"], b["s_mat"], b["down_mat"], b["top_mat"]
    x, z, y, core = place()
    chip = z * 4 + y
    me = x * 32 + chip * 2 + core

    loads = [
        pltpu.make_async_copy(c_hbm, b["c_mat"], b["load_sem"].at[0]),
        pltpu.make_async_copy(fl_hbm, b["fl_mat"], b["load_sem"].at[1]),
    ]
    for load in loads:
        load.start()

    sibling = (x, chip * 2 + 1 - core)
    before = (lax.rem(lax.div(me + 127, 32), 4), lax.rem(me + 31, 32))
    after = (lax.rem(lax.div(me + 1, 32), 4), lax.rem(me + 1, 32))
    has_before = me > 0
    has_after = me < 127

    def plane(k):
        k = lax.rem(5 * k, 16)
        tz = lax.rem(z + lax.div(k, 4), 4)
        ty = lax.rem(y + lax.rem(k, 4), 4)
        return tz * 4 + ty, (x, leaf_of(tz, ty, core))

    def along(axis, k):
        if axis == "x":
            return (lax.rem(x + k, 4), leaf_of(z, y, core))
        if axis == "y":
            return (x, leaf_of(z, lax.rem(y + k, 4), core))
        if axis == "z":
            return (x, leaf_of(lax.rem(z + k, 4), y, core))
        return sibling

    barrier = pltpu.get_barrier_semaphore()

    def greet(k):
        pl.semaphore_signal(barrier, inc=1, device_id=plane(k)[1], device_id_type=MESH)

    loop(1, 16, greet)
    for k in range(1, 4):
        pl.semaphore_signal(barrier, inc=1, device_id=along("x", k), device_id_type=MESH)
    pl.semaphore_signal(barrier, inc=1, device_id=sibling, device_id_type=MESH)

    @pl.when(has_before)
    def _():
        pl.semaphore_signal(barrier, inc=1, device_id=before, device_id_type=MESH)

    @pl.when(has_after)
    def _():
        pl.semaphore_signal(barrier, inc=1, device_id=after, device_id_type=MESH)

    high = b["high"]

    def split(i):
        rows = rows_at(i, 128)
        value = pot_ref[rows, :]
        top = value.astype(BF)
        high[rows, pl.ds(0, 256)] = top
        high[rows, pl.ds(256, 256)] = (value - top.astype(F32)).astype(BF)

    loop(0, 8, split)

    def order(i):
        rows = rows_at(i, 128)
        wanted = lax.broadcasted_iota(jnp.int32, (128, 128), 1).astype(F32)
        column = jnp.broadcast_to(panels_row[:, rows].astype(F32), (128, 128)).T
        hot = [jnp.where(column == wanted + 128.0 * q, 1.0, 0.0).astype(BF) for q in range(8)]
        hot = jnp.concatenate(hot, axis=1)
        value = dot(hot, high[...])
        b["v0"][rows, :] = value[:, :256].astype(BF)
        b["p_slot"][rows, :] = value[:, :256] + value[:, 256:]

    loop(0, 8, order)
    basis[pl.ds(8, 8)] = basis_ref[...]
    transfer[pl.ds(0, 8)] = transfer_ref[...]
    far_all[pl.ds(0, 16)] = far_ref[...]

    for it in range(2):

        @pl.when(jnp.logical_not(has_before))
        def _():
            b["win"][it, pl.ds(0, 1024), :] = jnp.zeros((1024, 256), BF)

        @pl.when(jnp.logical_not(has_after))
        def _():
            b["win"][it, pl.ds(2048, 1024), :] = jnp.zeros((1024, 256), BF)

    @pl.when(jnp.logical_not(has_before))
    def _():
        basis[pl.ds(0, 8)] = jnp.zeros((8, K, P_SIZE), BF)

    @pl.when(jnp.logical_not(has_after))
    def _():
        basis[pl.ds(16, 8)] = jnp.zeros((8, K, P_SIZE), BF)

    pl.semaphore_wait(barrier, 19 + has_before.astype(jnp.int32) + has_after.astype(jnp.int32))

    ex_send, ex_recv = b["ex_send"], b["ex_recv"]
    swaps = [
        remote(target_ref, b["other_target"], ex_send.at[0], ex_recv.at[0], sibling),
        remote(source_ref, b["other_source"], ex_send.at[5], ex_recv.at[5], sibling),
        remote(parent_ref, b["other_parent"], ex_send.at[6], ex_recv.at[6], sibling),
        remote(transfer_ref, transfer.at[pl.ds(8, 8)], ex_send.at[1], ex_recv.at[1], sibling),
        remote(far_ref, far_all.at[pl.ds(16, 16)], ex_send.at[2], ex_recv.at[2], sibling),
    ]
    for swap in swaps:
        swap.start()
    basis_after = remote(basis_ref, basis.at[pl.ds(0, 8)], ex_send.at[3], ex_recv.at[3], after)
    basis_before = remote(basis_ref, basis.at[pl.ds(16, 8)], ex_send.at[4], ex_recv.at[4], before)

    @pl.when(has_after)
    def _():
        basis_after.start()

    @pl.when(has_before)
    def _():
        basis_before.start()

    numbers = (
        (target_s, b["target_o"]),
        (source_s, b["source_o"]),
        (parent_s, b["parent_o"]),
    )

    def number(row, i, count):
        own, other = numbers[row]
        return own[0, i] if i < count else other[0, i - count]

    def spread(values, lanes):
        index = lax.broadcasted_iota(jnp.int32, (1, lanes), 1) // K
        found = jnp.zeros((1, lanes), jnp.int32)
        for i, value in enumerate(values):
            found = jnp.where(index == i, value, found)
        return found

    def chosen(found, value):
        return jnp.where(found == value, 1.0, 0.0).astype(BF)

    def build_up():
        for swap in swaps[:4]:
            swap.wait_recv()
        fetches = [
            pltpu.make_async_copy(b["other_" + name], b[name + "_o"], b["load_sem"].at[2 + i])
            for i, name in enumerate(("target", "source", "parent"))
        ]
        for fetch in fetches:
            fetch.start()
        for fetch in fetches:
            fetch.wait()
        parents = [number(2, l, 8) for l in range(16)]
        for i in range(8):
            lanes = pl.ds(i * 128, 128)
            pair = transfer[pl.ds(2 * i, 2)].reshape(128, K)
            up[:, lanes] = pair.astype(F32).T.astype(BF)
        parent_lanes = spread(parents, 1024)

        def build(c):
            tv_mat[c // 2, rows_at(c % 2, K), :] = up[...] * chosen(parent_lanes, c)

        loop(0, 32, build)

    def build_rest():
        swaps[4].wait_recv()
        targets = [number(0, j, 16) for j in range(32)]
        for i in range(16):
            far_flat[:, pl.ds(i * 128, 128)] = jnp.concatenate([far_all[2 * i], far_all[2 * i + 1]], axis=1)
        target_lanes = spread(targets, 2048)

        def build_far(c):
            s_mat[c // 2, rows_at(c % 2, K), :] = far_flat[...] * chosen(target_lanes, c)

        loop(0, 32, build_far)

        turned, two = b["turned"], b["two"]

        def turn(a):
            block = two_ref[a].astype(F32).T
            turned[pl.ds(a, K, stride=K), :] = jnp.concatenate([block[:K], block[K:]], axis=1)

        loop(0, K, turn, 4)

        def shorten(c):
            block = turned[rows_at(c, K), :].astype(BF)
            two[c] = block[:, :K]
            two[K + c] = block[:, K:]

        loop(0, K, shorten, 4)

    def build_top():
        one_lanes = spread([one_target_s[j] for j in range(32)], 2048)
        for i in range(16):
            far_flat[:, pl.ds(i * 128, 128)] = jnp.concatenate([one_ref[2 * i], one_ref[2 * i + 1]], axis=1)
        for h in range(2):
            wanted = two_parent_s[x * 32 + chip * 2 + h]
            top_mat[pl.ds(h * K, K), :] = far_flat[...] * chosen(one_lanes, wanted)

        turned, two, sums, top_all = (b[n] for n in ("turned", "two", "top_sums", "top_all"))

        for h in range(2):
            value = dot(two[x * 32 + chip * 2 + h], top_mat[pl.ds(h * K, K), :])
            for i in range(16):
                turned[pl.ds(i * 128 + h * K, K), :] = value[:, i * 128 : (i + 1) * 128]
        source_lanes = spread([one_source_s[j] for j in range(32)], 2048)

        def pick_sources(u):
            found = jnp.where(source_lanes == u, 1.0, 0.0)
            value = turned[pl.ds(0, 128), :] * found[:, 0:128]
            for i in range(1, 16):
                value = value + turned[pl.ds(i * 128, 128), :] * found[:, i * 128 : (i + 1) * 128]
            sums[u] = (value[:, :K] + value[:, K:]).astype(BF)

        loop(0, 16, pick_sources)

        def whole(i):
            pair = [
                lax.dot_general(
                    sums[two_parent_s[2 * i + h]], two[2 * i + h], (((1,), (1,)), ((), ())), preferred_element_type=F32
                )
                for h in range(2)
            ]
            top_all[:, rows_at(i, 128)] = jnp.concatenate(pair, axis=1).astype(BF)

        loop(0, 64, whole, 4)

    def build_last():
        for l in range(16):
            pair = jnp.concatenate([transfer[l], transfer[l]], axis=1)
            half = lax.broadcasted_iota(jnp.int32, (1, 128), 1) // K
            parent = number(2, l, 8)

            def build_down(i, l=l, pair=pair, half=half, parent=parent):
                down_mat[pl.ds(l * K, K), rows_at(i, 128)] = pair * chosen(half + 2 * i, parent)

            loop(0, 16, build_down, 4)

    def apply(it, v, w, wb, beside_rs, beside_ag, beside_l2):
        win, chalf, c2 = b["win"].at[it], b["chalf"], b["c2"].at[it]
        local_half, cw = b["local_half"], b["cw"]
        rs_out, rs_in = b["rs_out"], b["rs_in"].at[it]
        ag = [b["ag0"].at[it], b["ag1"].at[it], b["ag2"].at[it]]
        q_two, gathered = b["q_two"], b["gathered"]
        far_out, far_in, l2 = b["far_out"], b["far_in"].at[it], b["l2"].at[it]
        sib_out, sib_in, merged = b["sib_out"], b["sib_in"].at[it], b["merged"]

        def window_copy(side, half):
            first, device = (0, after) if side == 0 else (2048, before)
            i = side * 2 + half
            return remote(
                v.at[pl.ds(half * 512, 512)],
                win.at[pl.ds(first + half * 512, 512)],
                b["win_send"].at[it, i],
                b["win_recv"].at[it, i],
                device,
            )

        def window_start(half):
            @pl.when(has_after)
            def _():
                window_copy(0, half).start()

            @pl.when(has_before)
            def _():
                window_copy(1, half).start()

        def window_land(half):
            @pl.when(has_before)
            def _():
                window_copy(0, half).wait_recv()

            @pl.when(has_after)
            def _():
                window_copy(1, half).wait_recv()


        def own_coeffs(i):
            part = dot(basis[8 + i], v[rows_at(i, P_SIZE), :]).astype(BF)
            chalf[0, rows_at(i, K), :] = part[:, :HALF]
            chalf[1, rows_at(i, K), :] = part[:, HALF:]

        loop(0, 8, own_coeffs, 8)
        coeff_swap = remote(
            chalf.at[1 - core], c2.at[pl.ds(512, 512)], b["sib_send"].at[it, 0], b["sib_recv"].at[it, 0], sibling
        )
        coeff_swap.start()

        window_start(0)
        if it == 0:
            window_start(1)
        c2[pl.ds(0, 512), :] = chalf[core]
        win[pl.ds(1024, 1024), :] = v[...]
        if it == 0:
            build_up()
        coeff_swap.wait_recv()

        rs_rows = (pl.ds(0, 96), pl.ds(96, 32))

        def rs_copy(h, k):
            there, device = plane(k)
            rows, i = rs_rows[h], h * 16 + k
            return remote(
                rs_out.at[there, rows], rs_in.at[k, rows], b["rs_send"].at[it, i], b["rs_recv"].at[it, i], device
            )

        for h in range(2):

            def rs_step(k, h=h):
                there, _ = plane(k)
                rs_out[there, rs_rows[h]] = dot(tv_mat[there, rs_rows[h]], c2[...]).astype(BF)
                rs_copy(h, k).start()

            loop(1, 16, rs_step)
        rs_in[0] = dot(tv_mat[chip], c2[...]).astype(BF)
        beside_rs()

        def rs_total(h):
            def rs_sum(k, total):
                rs_copy(h, k).wait_recv()
                return total + rs_in[k, rs_rows[h]].astype(F32)

            return lax.fori_loop(1, 16, rs_sum, rs_in[0, rs_rows[h]].astype(F32)).astype(BF)

        homes = ((z * 4 + y) * 4 + x, (x * 4 + z) * 4 + y, (y * 4 + x) * 4 + z)
        orders = (("x", "y", "z"), ("y", "z", "x"), ("z", "x", "y"))
        lasts = (z, x, y)

        def ag_copy(stream, stage, k):
            if stage == 0:
                first, count = homes[stream], 1
            elif stage == 1:
                first, count = lax.div(homes[stream], 4) * 4, 4
            else:
                first, count = lasts[stream] * 16, 16
            part = ag[stream].at[pl.ds(first, count)]
            i = (stream * 3 + stage) * 3 + k - 1
            return remote(
                part, part, b["ag_send"].at[it, i], b["ag_recv"].at[it, i], along(orders[stream][stage], k)
            )

        def ag_start(stream, stage):
            for k in range(1, 4):
                ag_copy(stream, stage, k).start()

        def ag_land(stream, stage):
            for k in range(1, 4):
                ag_copy(stream, stage, k).wait_recv()

        total = rs_total(0)
        ag[0][homes[0]] = total[0:48]
        ag[1][homes[1]] = total[48:96]
        ag_start(0, 0)
        ag_start(1, 0)
        total = rs_total(1)
        ag[2][homes[2]] = total
        ag_start(2, 0)
        for stream in range(3):
            ag_land(stream, 0)
            ag_start(stream, 1)
        for stream in range(3):
            ag_land(stream, 1)
            ag_start(stream, 2)

        beside_ag()

        window_land(0)
        if it == 0:
            for load in loads:
                load.wait()

            @pl.when(has_before)
            def _():
                basis_after.wait_recv()

            @pl.when(has_after)
            def _():
                basis_before.wait_recv()

        def window_coeffs(i):
            cw[rows_at(i, K), :] = dot(basis[i], win[rows_at(i, P_SIZE), :]).astype(BF)

        loop(0, 4, window_coeffs, 4)
        loop(8, 20, window_coeffs, 4)

        def near_dot(i, first, size):
            return dot(b["c_mat"][rows_at(i, 128), pl.ds(first, size)], win[pl.ds(first, size), :])

        def near_most(i):
            w[rows_at(i, 128), :] = near_dot(i, 0, 512) + near_dot(i, 1024, 1536)

        loop(0, 8, near_most)
        for stream in range(3):
            ag_land(stream, 2)

        if it == 1:
            window_start(1)

        def join(i):
            ip, g = i // 4, i % 4
            iz, iy = ip // 4, ip % 4
            first, second, third = ag[0][i], ag[1][(g * 4 + iz) * 4 + iy], ag[2][(iy * 4 + g) * 4 + iz]
            q_two[g * 32 + 2 * ip] = jnp.concatenate([first, second[0:16]], axis=0)
            q_two[g * 32 + 2 * ip + 1] = jnp.concatenate([second[16:48], third], axis=0)

        loop(0, 64, join, 4)

        for j in range(32):
            gathered[pl.ds(j * K, K), :] = q_two[number(1, j, 16)]

        def far_copy(h, k):
            there, device = plane(k)
            rows, i = pl.ds(h * K, K), h * 16 + k
            return remote(
                far_out.at[there, rows],
                far_in.at[k, rows],
                b["far_send"].at[it, i],
                b["far_recv"].at[it, i],
                device,
            )

        for h in range(2):

            def far_step(k, h=h):
                there, _ = plane(k)
                far_out[there, pl.ds(h * K, K)] = dot(s_mat[there, pl.ds(h * K, K)], gathered[...]).astype(BF)
                far_copy(h, k).start()

            loop(1, 16, far_step)
        own = dot(s_mat[chip], gathered[...])

        def fall(i, total):
            part = q_two[pl.ds(i * 16, 16)].reshape(1024, HALF)
            return total + dot(b["top_all"][:, rows_at(i, 1024)], part)

        own = lax.fori_loop(0, 8, fall, own)

        def l2_copy(h, k):
            part = l2.at[rows_at(chip * 2 + h, K)]
            i = h * 16 + k
            return remote(part, part, b["l2_send"].at[it, i], b["l2_recv"].at[it, i], plane(k)[1])

        for h in range(2):

            def far_sum(k, total, h=h):
                far_copy(h, k).wait_recv()
                return total + far_in[k, pl.ds(h * K, K)].astype(F32)

            half_sum = lax.fori_loop(1, 16, far_sum, own[h * K : (h + 1) * K])
            l2[rows_at(chip * 2 + h, K), :] = half_sum.astype(BF)

            def l2_start(k, h=h):
                l2_copy(h, k).start()

            loop(1, 16, l2_start)

        def drain(k):
            for h in range(2):
                rs_copy(h, k).wait_send()
                far_copy(h, k).wait_send()

        loop(1, 16, drain)
        coeff_swap.wait_send()
        for stream in range(3):
            for stage in range(3):
                for k in range(1, 4):
                    ag_copy(stream, stage, k).wait_send()

        for half in range(2):

            @pl.when(has_after)
            def _(half=half):
                window_copy(0, half).wait_send()

            @pl.when(has_before)
            def _(half=half):
                window_copy(1, half).wait_send()

        beside_l2()

        window_land(1)
        loop(4, 8, window_coeffs, 4)
        loop(20, 24, window_coeffs, 4)

        def leaf_far(i):
            part = dot(b["fl_mat"][rows_at(i, 128), :], cw[...])
            local_half[0, rows_at(i, 128), :] = part[:, :HALF]
            local_half[1, rows_at(i, 128), :] = part[:, HALF:]

        loop(0, 4, leaf_far)

        def near_rest(i):
            w[rows_at(i, 128), :] = w[rows_at(i, 128), :] + near_dot(i, 512, 512) + near_dot(i, 2560, 512)

        loop(0, 8, near_rest)

        def l2_land(k):
            for h in range(2):
                l2_copy(h, k).wait_recv()

        loop(1, 16, l2_land)

        def down_sibling(i):
            sib_out[rows_at(i, 128), :] = dot(down_mat[rows_at(i + 4, 128), :], l2[...]).astype(BF)

        loop(0, 4, down_sibling)
        leaf_swap = remote(sib_out, sib_in, b["sib_send"].at[it, 1], b["sib_recv"].at[it, 1], sibling)
        leaf_swap.start()

        def down_own(i):
            rows = rows_at(i, 128)
            merged[core, rows, :] = (local_half[core, rows, :] + dot(down_mat[rows, :], l2[...])).astype(BF)

        loop(0, 4, down_own)
        leaf_swap.wait_recv()
        merged[1 - core] = (local_half[1 - core] + sib_in[...].astype(F32)).astype(BF)

        def finish(i):
            rows = rows_at(i, P_SIZE)
            for h in range(2):
                lanes = pl.ds(h * HALF, HALF)
                value = w[rows, lanes] + lax.dot_general(
                    basis[8 + i],
                    merged[h, rows_at(i, K), :],
                    (((0,), (0,)), ((), ())),
                    preferred_element_type=F32,
                )
                w[rows, lanes] = value
                if wb is not None:
                    wb[rows, lanes] = value.astype(BF)

        loop(0, 8, finish, 2)
        leaf_swap.wait_send()

        def l2_sent(k):
            for h in range(2):
                l2_copy(h, k).wait_send()

        loop(1, 16, l2_sent)

    p_slot, w1, w2 = b["p_slot"], b["w1"], b["w2"]

    def unorder():
        def split_image(i):
            rows = rows_at(i, 128)
            value = w1[rows, :]
            top = value.astype(BF)
            high[rows, pl.ds(0, 256)] = top
            high[rows, pl.ds(256, 256)] = (value - top.astype(F32)).astype(BF)

        loop(0, 8, split_image)

        def reorder(i):
            wanted = lax.broadcasted_iota(jnp.int32, (128, 1024), 0) + i * 128
            hot = jnp.where(panels_row[...] == wanted, 1.0, 0.0).astype(BF)
            value = dot(hot, high[...])
            w1_panel[rows_at(i, 128), :] = value[:, :256] + value[:, 256:]

        loop(0, 8, reorder)

    def col_max(ref):
        return jnp.maximum(jnp.max(jnp.abs(ref[...]), axis=0, keepdims=True), 1e-30)

    def col_sums(terms):
        def add(i, carry):
            return tuple(
                c + jnp.sum(t.reshape(4, 8, 256), axis=0) for c, t in zip(carry, terms(rows_at(i, 32)))
            )

        sums = lax.fori_loop(0, 32, add, tuple(jnp.zeros((8, 256), F32) for _ in range(3)), unroll=2)
        return [jnp.sum(s, axis=0, keepdims=True) for s in sums]

    early = []

    def early_sums():
        size_p, size_a = col_max(p_slot), col_max(w1)
        inv_p, inv_a = 1.0 / size_p, 1.0 / size_a

        def terms(rows):
            p, a = p_slot[rows, :] * inv_p, w1[rows, :] * inv_a
            return p * p, p * a, a * a

        early.extend((size_p, size_a, col_sums(terms)))

    v1 = b["v0"]
    apply(0, b["v0"], w1, v1, build_rest, build_top, build_last)
    for swap in swaps:
        swap.wait_send()

    @pl.when(has_after)
    def _():
        basis_after.wait_send()

    @pl.when(has_before)
    def _():
        basis_before.wait_send()

    apply(1, v1, w2, None, unorder, early_sums, lambda: None)

    size_p, size_a, sums = early
    size_b = col_max(w2)
    inv_p, inv_a, inv_b = 1.0 / size_p, 1.0 / size_a, 1.0 / size_b

    def late_terms(rows):
        value = w2[rows, :] * inv_b
        return p_slot[rows, :] * inv_p * value, w1[rows, :] * inv_a * value, value * value

    sums = sums + col_sums(late_terms)
    sizes = [size_p, size_a, size_b]
    part, box = b["part"], b["box"]
    pairs = ((0, 0), (0, 1), (1, 1), (0, 2), (1, 2), (2, 2))
    coords = (core, x, y, z)
    axes = ("core", "x", "y", "z")

    def sum_copy(stage, k):
        i = stage * 4 + k
        here = box.at[stage, coords[stage]]
        return remote(here, here, b["sum_send"].at[i], b["sum_recv"].at[i], along(axes[stage], k))

    for stage in range(4):
        count = 2 if stage == 0 else 4
        for i in range(6):
            part[i : i + 1, :] = sums[i]
        for i in range(3):
            part[8 + i : 9 + i, :] = sizes[i]
        box[stage, coords[stage]] = part[...]
        for k in range(1, count):
            sum_copy(stage, k).start()
        for k in range(1, count):
            sum_copy(stage, k).wait_recv()
        got = [box[stage, i] for i in range(count)]
        new_sizes = []
        for i in range(3):
            top_size = got[0][8 + i : 9 + i]
            for g in got[1:]:
                top_size = jnp.maximum(top_size, g[8 + i : 9 + i])
            new_sizes.append(top_size)
        factors = [[g[8 + i : 9 + i] / new_sizes[i] for i in range(3)] for g in got]
        sums = []
        for i, (first, second) in enumerate(pairs):
            value = got[0][i : i + 1] * (factors[0][first] * factors[0][second])
            for g, f in zip(got[1:], factors[1:]):
                value = value + g[i : i + 1] * (f[first] * f[second])
            sums.append(value)
        sizes = new_sizes

    along_p, along_a, estimate = project(sums, sizes)
    weights_ref[0:1, :] = along_p
    weights_ref[1:2, :] = along_a
    weights_ref[2:3, :] = estimate
    for stage in range(4):
        for k in range(1, 2 if stage == 0 else 4):
            sum_copy(stage, k).wait_send()


def both_steps(smem_args, vmem_args, hbm_args):
    smem = pl.BlockSpec(memory_space=pltpu.SMEM)
    vmem = pl.BlockSpec(memory_space=pltpu.VMEM)
    anywhere = pl.BlockSpec(memory_space=pl.ANY)
    return pl.pallas_call(
        steps_kernel,
        out_shape=(jax.ShapeDtypeStruct((1024, 256), F32), jax.ShapeDtypeStruct((8, 256), F32)),
        in_specs=[smem] * len(smem_args) + [vmem] * len(vmem_args) + [anywhere] * len(hbm_args),
        out_specs=(vmem, vmem),
        scratch_shapes=list(BUFFERS.values()),
        compiler_params=pltpu.CompilerParams(
            collective_id=1, has_side_effects=True, vmem_limit_bytes=62 * 1024 * 1024
        ),
        name="both_steps",
    )(*smem_args, *vmem_args, *hbm_args)


def result_kernel(weights_ref, pot_ref, image_ref, out_ref, est_ref):
    out_ref[...] = weights_ref[0:1, :] * pot_ref[...] + weights_ref[1:2, :] * image_ref[...]
    est_ref[...] = weights_ref[2, :]


def result(weights, potentials, image):
    return pl.pallas_call(
        result_kernel,
        out_shape=(jax.ShapeDtypeStruct((1024, 256), F32), jax.ShapeDtypeStruct((256,), F32)),
        compiler_params=pltpu.CompilerParams(vmem_limit_bytes=60 * 1024 * 1024),
        name="result",
    )(weights, potentials, image)


def least_squares(beta_norm, first_diag, first_below, second_top, second_diag, second_below):
    first_radius = jnp.sqrt(first_diag * first_diag + first_below * first_below)
    first_cos = first_diag / first_radius
    first_sin = first_below / first_radius
    upper_term = first_cos * second_top + first_sin * second_diag
    lower_term = first_cos * second_diag - first_sin * second_top
    second_radius = jnp.sqrt(lower_term * lower_term + second_below * second_below)
    second_cos = lower_term / second_radius
    second_sin = second_below / second_radius
    weight_two = -first_sin * beta_norm * second_cos / second_radius
    weight_one = (first_cos * beta_norm - upper_term * weight_two) / first_radius
    return (weight_one, weight_two, first_sin * second_sin * beta_norm)


def project(sums, sizes):
    pp, pa, aa, pb, ab, bb = sums
    size_p, size_a, size_b = sizes
    beta = jnp.sqrt(size_p * size_p * pp + EPS)
    scale_p, scale_a, scale_b = size_p / beta, size_a / beta, size_b / beta
    first_first = scale_p * scale_p * pp
    first_image = scale_p * scale_a * pa
    first_diag = first_image
    image_image = scale_a * scale_a * aa
    rest = image_image - first_diag * first_diag * (2.0 - first_first)
    first_below = jnp.sqrt(jnp.maximum(rest, 0.0) + EPS)
    inverse = 1.0 / first_below
    first_second = (first_image - first_diag * first_first) * inverse
    second_second = jnp.maximum(rest, 0.0) * inverse * inverse
    scale_two = scale_b * inverse
    diag_two = first_diag * inverse
    first_b = scale_p * scale_two * pb
    a_b = scale_a * scale_two * ab
    b_b = scale_two * scale_two * bb
    second_top = first_b - diag_two * first_image
    image_image_two = a_b - diag_two * image_image
    second_diag = (image_image_two - first_diag * second_top) * inverse
    square = b_b - 2.0 * diag_two * a_b + diag_two * diag_two * image_image
    rest_two = (
        square
        - second_top * second_top * (2.0 - first_first)
        - second_diag * second_diag * (2.0 - second_second)
        + 2.0 * second_top * second_diag * first_second
    )
    second_below = jnp.sqrt(jnp.maximum(rest_two, 0.0) + EPS)
    weight_one, weight_two, estimate = least_squares(
        beta, first_diag, first_below, second_top, second_diag, second_below
    )
    along_a = weight_two * inverse / beta
    along_p = weight_one / beta - along_a * first_diag
    return along_p, along_a, estimate


def on_device(
    potentials,
    leaf_panels,
    near_blocks,
    near_target,
    near_source,
    near_count,
    leaf_basis,
    far_leaf,
    far_leaf_target,
    far_leaf_source,
    leaf_transfer,
    leaf_parent,
    far_two,
    far_two_target,
    far_two_source,
    two_transfer,
    two_parent,
    far_one,
    far_one_target,
    far_one_source,
):
    c_mat, fl_mat = combine(
        near_target, near_source, near_count, far_leaf_target, far_leaf_source, near_blocks, far_leaf
    )
    own_numbers = (far_two_target, far_two_source, leaf_parent.reshape(1, 8))
    image, weights = both_steps(
        own_numbers + (two_parent, far_one_target, far_one_source),
        own_numbers
        + (
            leaf_panels,
            potentials,
            leaf_basis,
            leaf_transfer,
            far_two,
            jnp.transpose(two_transfer, (1, 2, 0)),
            far_one,
        ),
        (c_mat, fl_mat),
    )
    return result(weights, potentials, image)


def solution(mesh):
    both = P(("grp", "leaf"))
    in_specs = (both,) * 15 + (P(),) * 5
    return jax.shard_map(
        on_device, mesh=mesh, in_specs=in_specs, out_specs=(both, P()), check_vma=False
    )
```

```python
import jax
import jax.numpy as jnp
from jax import lax
from jax.experimental import pallas as pl
from jax.experimental.pallas import tpu as pltpu
from jax.sharding import PartitionSpec as P

P_SIZE = 128
K = 64
HALF = 128
EPS = 1e-06
BF = jnp.bfloat16
F32 = jnp.float32
MESH = pl.DeviceIdType.MESH
VMEM = pltpu.VMEM
DMA = pltpu.SemaphoreType.DMA
NEAR_STEPS = 8


def dot(a, b):
    return jnp.dot(a, b, preferred_element_type=F32)


def combine_kernel(near_target, near_source, near_count, near_hbm, c_hbm, blocks, acc, stage, load_sems, sems):
    window = 24
    per_step = blocks.shape[0] // NEAR_STEPS
    loads = []
    for step in range(NEAR_STEPS):
        part = pl.ds(step * per_step, per_step)
        loads.append(pltpu.make_async_copy(near_hbm.at[part], blocks.at[part], load_sems.at[step]))
        loads[-1].start()

    def zero(i, carry):
        acc[i] = jnp.zeros((P_SIZE, P_SIZE), F32)
        return carry

    lax.fori_loop(0, acc.shape[0], zero, 0, unroll=8)
    live = near_count[0]

    def add(j, carry):
        key = near_target[0, j] * window + near_source[0, j]
        acc[key] = acc[key] + blocks[j].astype(F32)
        return carry

    for step in range(NEAR_STEPS):
        loads[step].wait()
        first = step * per_step
        lax.fori_loop(first, jnp.clip(live, first, first + per_step), add, 0)
    copies = []
    for t in range(8):
        rows = pl.ds(t * P_SIZE, P_SIZE)

        def write(s, carry, t=t, rows=rows):
            lanes = pl.ds(pl.multiple_of(s * P_SIZE, P_SIZE), P_SIZE)
            stage[rows, lanes] = acc[t * window + s].astype(BF)
            return carry

        lax.fori_loop(0, window, write, 0, unroll=8)
        copies.append(pltpu.make_async_copy(stage.at[rows], c_hbm.at[rows], sems.at[t]))
        copies[-1].start()
    for copy in copies:
        copy.wait()


def combine(near_target, near_source, near_count, near_blocks):
    smem = pl.BlockSpec(memory_space=pltpu.SMEM)
    anywhere = pl.BlockSpec(memory_space=pl.ANY)
    return pl.pallas_call(
        combine_kernel,
        out_shape=jax.ShapeDtypeStruct((1024, 3072), BF),
        in_specs=[smem] * 3 + [anywhere],
        out_specs=anywhere,
        scratch_shapes=[
            VMEM(near_blocks.shape, BF),
            VMEM((192, P_SIZE, P_SIZE), F32),
            VMEM((1024, 3072), BF),
            DMA((NEAR_STEPS,)),
            DMA((8,)),
        ],
        compiler_params=pltpu.CompilerParams(vmem_limit_bytes=56 * 1024 * 1024),
        cost_estimate=pl.CostEstimate(flops=10**7, bytes_accessed=20 * 10**6, transcendentals=0),
        name="combine",
    )(near_target, near_source, near_count, near_blocks)


def remote(src, dst, send, recv, device):
    return pltpu.make_async_remote_copy(
        src_ref=src, dst_ref=dst, send_sem=send, recv_sem=recv, device_id=device, device_id_type=MESH
    )


def place():
    x = lax.axis_index("grp")
    leaf = lax.axis_index("leaf")
    core = lax.rem(leaf, 2)
    chip = lax.div(leaf, 2)
    return x, lax.div(chip, 4), lax.rem(chip, 4), core


def leaf_of(z, y, core):
    return (z * 4 + y) * 2 + core


def loop(start, stop, body, unroll=1):
    def step(i, carry):
        body(i)
        return carry

    lax.fori_loop(start, stop, step, 0, unroll=unroll)


def rows_at(i, size):
    return pl.ds(pl.multiple_of(i * size, size), size)


BUFFERS = dict(
    c_mat=VMEM((1024, 3072), BF),
    fl_mat=VMEM((512, 1536), BF),
    tv_mat=VMEM((16, 128, 1024), BF),
    s_mat=VMEM((16, 128, 2048), BF),
    down_mat=VMEM((1024, 2048), BF),
    top_mat=VMEM((128, 2048), BF),
    turned=VMEM((6144, 128), F32),
    two=VMEM((128, K, K), BF),
    top_sums=VMEM((16, 128, K), BF),
    far_chunk=VMEM((2, 16, K, 192), BF),
    chunk_sem=DMA((2,)),
    top_all=VMEM((128, 8192), BF),
    up=VMEM((K, 1024), BF),
    far_flat=VMEM((K, 2048), BF),
    transfer=VMEM((16, K, K), BF),
    far_all=VMEM((32, K, K), BF),
    basis=VMEM((24, K, P_SIZE), BF),
    other_target=VMEM((1, 16), jnp.int32),
    other_source=VMEM((1, 16), jnp.int32),
    other_parent=VMEM((1, 8), jnp.int32),
    target_o=pltpu.SMEM((1, 16), jnp.int32),
    source_o=pltpu.SMEM((1, 16), jnp.int32),
    parent_o=pltpu.SMEM((1, 8), jnp.int32),
    v0=VMEM((1024, 256), BF),
    p_slot=VMEM((1024, 256), F32),
    w1=VMEM((1024, 256), F32),
    w2=VMEM((1024, 256), F32),
    high=VMEM((1024, 512), BF),
    part=VMEM((16, 256), F32),
    box=VMEM((4, 4, 16, 256), F32),
    win=VMEM((2, 3072, 256), BF),
    cw=VMEM((1536, 256), BF),
    chalf=VMEM((2, 512, HALF), BF),
    c2=VMEM((2, 1024, HALF), BF),
    local_half=VMEM((2, 512, HALF), F32),
    rs_out=VMEM((16, 128, HALF), BF),
    rs_in=VMEM((2, 16, 128, HALF), BF),
    ag0=VMEM((2, 64, 48, HALF), BF),
    ag1=VMEM((2, 64, 48, HALF), BF),
    ag2=VMEM((2, 64, 32, HALF), BF),
    q_two=VMEM((128, K, HALF), BF),
    gathered=VMEM((2048, HALF), BF),
    far_out=VMEM((16, 128, HALF), BF),
    far_in=VMEM((2, 16, 128, HALF), BF),
    l2=VMEM((2, 2048, HALF), BF),
    sib_out=VMEM((512, HALF), BF),
    sib_in=VMEM((2, 512, HALF), BF),
    merged=VMEM((2, 512, HALF), BF),
    load_sem=DMA((5,)),
    ex_send=DMA((7,)),
    ex_recv=DMA((7,)),
    win_send=DMA((2, 4)),
    win_recv=DMA((2, 4)),
    sib_send=DMA((2, 2)),
    sib_recv=DMA((2, 2)),
    rs_send=DMA((2, 32)),
    rs_recv=DMA((2, 32)),
    ag_send=DMA((2, 27)),
    ag_recv=DMA((2, 27)),
    far_send=DMA((2, 32)),
    far_recv=DMA((2, 32)),
    l2_send=DMA((2, 32)),
    l2_recv=DMA((2, 32)),
    sum_send=DMA((16,)),
    sum_recv=DMA((16,)),
)
NAMES = tuple(BUFFERS)


def steps_kernel(
    target_s,
    source_s,
    parent_s,
    two_parent_s,
    one_target_s,
    one_source_s,
    target_ref,
    source_ref,
    parent_ref,
    panels_row,
    pot_ref,
    basis_ref,
    transfer_ref,
    far_ref,
    two_ref,
    one_ref,
    far_target_ref,
    far_source_ref,
    c_hbm,
    far_leaf_hbm,
    w1_panel,
    weights_ref,
    *scratch,
):
    b = dict(zip(NAMES, scratch))
    basis, transfer, far_all = b["basis"], b["transfer"], b["far_all"]
    up, far_flat = b["up"], b["far_flat"]
    tv_mat, s_mat, down_mat, top_mat = b["tv_mat"], b["s_mat"], b["down_mat"], b["top_mat"]
    x, z, y, core = place()
    chip = z * 4 + y
    me = x * 32 + chip * 2 + core

    loads = [
        pltpu.make_async_copy(c_hbm, b["c_mat"], b["load_sem"].at[0]),
    ]
    for load in loads:
        load.start()

    def far_fetch(q):
        return pltpu.make_async_copy(
            far_leaf_hbm.at[pl.ds(q * 16, 16)], b["far_chunk"].at[q % 2], b["chunk_sem"].at[q % 2]
        )

    for q in range(2):
        far_fetch(q).start()

    sibling = (x, chip * 2 + 1 - core)
    before = (lax.rem(lax.div(me + 127, 32), 4), lax.rem(me + 31, 32))
    after = (lax.rem(lax.div(me + 1, 32), 4), lax.rem(me + 1, 32))
    has_before = me > 0
    has_after = me < 127

    def plane(k):
        k = lax.rem(5 * k, 16)
        tz = lax.rem(z + lax.div(k, 4), 4)
        ty = lax.rem(y + lax.rem(k, 4), 4)
        return tz * 4 + ty, (x, leaf_of(tz, ty, core))

    def along(axis, k):
        if axis == "x":
            return (lax.rem(x + k, 4), leaf_of(z, y, core))
        if axis == "y":
            return (x, leaf_of(z, lax.rem(y + k, 4), core))
        if axis == "z":
            return (x, leaf_of(lax.rem(z + k, 4), y, core))
        return sibling

    barrier = pltpu.get_barrier_semaphore()

    def greet(k):
        pl.semaphore_signal(barrier, inc=1, device_id=plane(k)[1], device_id_type=MESH)

    loop(1, 16, greet)
    for k in range(1, 4):
        pl.semaphore_signal(barrier, inc=1, device_id=along("x", k), device_id_type=MESH)
    pl.semaphore_signal(barrier, inc=1, device_id=sibling, device_id_type=MESH)

    @pl.when(has_before)
    def _():
        pl.semaphore_signal(barrier, inc=1, device_id=before, device_id_type=MESH)

    @pl.when(has_after)
    def _():
        pl.semaphore_signal(barrier, inc=1, device_id=after, device_id_type=MESH)

    high = b["high"]

    def split(i):
        rows = rows_at(i, 128)
        value = pot_ref[rows, :]
        top = value.astype(BF)
        high[rows, pl.ds(0, 256)] = top
        high[rows, pl.ds(256, 256)] = (value - top.astype(F32)).astype(BF)

    loop(0, 8, split)

    def order(i):
        rows = rows_at(i, 128)
        wanted = lax.broadcasted_iota(jnp.int32, (128, 128), 1).astype(F32)
        column = jnp.broadcast_to(panels_row[:, rows].astype(F32), (128, 128)).T
        hot = [jnp.where(column == wanted + 128.0 * q, 1.0, 0.0).astype(BF) for q in range(8)]
        hot = jnp.concatenate(hot, axis=1)
        value = dot(hot, high[...])
        b["v0"][rows, :] = value[:, :256].astype(BF)
        b["p_slot"][rows, :] = value[:, :256] + value[:, 256:]

    loop(0, 8, order)
    basis[pl.ds(8, 8)] = basis_ref[...]
    transfer[pl.ds(0, 8)] = transfer_ref[...]
    far_all[pl.ds(0, 16)] = far_ref[...]

    for it in range(2):

        @pl.when(jnp.logical_not(has_before))
        def _():
            b["win"][it, pl.ds(0, 1024), :] = jnp.zeros((1024, 256), BF)

        @pl.when(jnp.logical_not(has_after))
        def _():
            b["win"][it, pl.ds(2048, 1024), :] = jnp.zeros((1024, 256), BF)

    @pl.when(jnp.logical_not(has_before))
    def _():
        basis[pl.ds(0, 8)] = jnp.zeros((8, K, P_SIZE), BF)

    @pl.when(jnp.logical_not(has_after))
    def _():
        basis[pl.ds(16, 8)] = jnp.zeros((8, K, P_SIZE), BF)

    pl.semaphore_wait(barrier, 19 + has_before.astype(jnp.int32) + has_after.astype(jnp.int32))

    ex_send, ex_recv = b["ex_send"], b["ex_recv"]
    swaps = [
        remote(target_ref, b["other_target"], ex_send.at[0], ex_recv.at[0], sibling),
        remote(source_ref, b["other_source"], ex_send.at[5], ex_recv.at[5], sibling),
        remote(parent_ref, b["other_parent"], ex_send.at[6], ex_recv.at[6], sibling),
        remote(transfer_ref, transfer.at[pl.ds(8, 8)], ex_send.at[1], ex_recv.at[1], sibling),
        remote(far_ref, far_all.at[pl.ds(16, 16)], ex_send.at[2], ex_recv.at[2], sibling),
    ]
    for swap in swaps:
        swap.start()
    basis_after = remote(basis_ref, basis.at[pl.ds(0, 8)], ex_send.at[3], ex_recv.at[3], after)
    basis_before = remote(basis_ref, basis.at[pl.ds(16, 8)], ex_send.at[4], ex_recv.at[4], before)

    @pl.when(has_after)
    def _():
        basis_after.start()

    @pl.when(has_before)
    def _():
        basis_before.start()

    numbers = (
        (target_s, b["target_o"]),
        (source_s, b["source_o"]),
        (parent_s, b["parent_o"]),
    )

    def number(row, i, count):
        own, other = numbers[row]
        return own[0, i] if i < count else other[0, i - count]

    def spread(values, lanes):
        index = lax.broadcasted_iota(jnp.int32, (1, lanes), 1) // K
        found = jnp.zeros((1, lanes), jnp.int32)
        for i, value in enumerate(values):
            found = jnp.where(index == i, value, found)
        return found

    def chosen(found, value):
        return jnp.where(found == value, 1.0, 0.0).astype(BF)

    def build_up():
        for swap in swaps[:4]:
            swap.wait_recv()
        fetches = [
            pltpu.make_async_copy(b["other_" + name], b[name + "_o"], b["load_sem"].at[2 + i])
            for i, name in enumerate(("target", "source", "parent"))
        ]
        for fetch in fetches:
            fetch.start()
        for fetch in fetches:
            fetch.wait()
        parents = [number(2, l, 8) for l in range(16)]
        for i in range(8):
            lanes = pl.ds(i * 128, 128)
            pair = transfer[pl.ds(2 * i, 2)].reshape(128, K)
            up[:, lanes] = pair.astype(F32).T.astype(BF)
        parent_lanes = spread(parents, 1024)

        def build(c):
            tv_mat[c // 2, rows_at(c % 2, K), :] = up[...] * chosen(parent_lanes, c)

        loop(0, 32, build)

    def build_rest():
        swaps[4].wait_recv()
        targets = [number(0, j, 16) for j in range(32)]
        for i in range(16):
            far_flat[:, pl.ds(i * 128, 128)] = jnp.concatenate([far_all[2 * i], far_all[2 * i + 1]], axis=1)
        target_lanes = spread(targets, 2048)

        def build_far(c):
            s_mat[c // 2, rows_at(c % 2, K), :] = far_flat[...] * chosen(target_lanes, c)

        loop(0, 32, build_far)

        turned, two = b["turned"], b["two"]

        def turn(a):
            block = two_ref[a].astype(F32).T
            turned[pl.ds(a, K, stride=K), :] = jnp.concatenate([block[:K], block[K:]], axis=1)

        loop(0, K, turn, 4)

        def shorten(c):
            block = turned[rows_at(c, K), :].astype(BF)
            two[c] = block[:, :K]
            two[K + c] = block[:, K:]

        loop(0, K, shorten, 4)

    def build_top():
        one_lanes = spread([one_target_s[j] for j in range(32)], 2048)
        for i in range(16):
            far_flat[:, pl.ds(i * 128, 128)] = jnp.concatenate([one_ref[2 * i], one_ref[2 * i + 1]], axis=1)
        for h in range(2):
            wanted = two_parent_s[x * 32 + chip * 2 + h]
            top_mat[pl.ds(h * K, K), :] = far_flat[...] * chosen(one_lanes, wanted)

        turned, two, sums, top_all = (b[n] for n in ("turned", "two", "top_sums", "top_all"))

        for h in range(2):
            value = dot(two[x * 32 + chip * 2 + h], top_mat[pl.ds(h * K, K), :])
            for i in range(16):
                turned[pl.ds(i * 128 + h * K, K), :] = value[:, i * 128 : (i + 1) * 128]
        source_lanes = spread([one_source_s[j] for j in range(32)], 2048)

        def pick_sources(u):
            found = jnp.where(source_lanes == u, 1.0, 0.0)
            value = turned[pl.ds(0, 128), :] * found[:, 0:128]
            for i in range(1, 16):
                value = value + turned[pl.ds(i * 128, 128), :] * found[:, i * 128 : (i + 1) * 128]
            sums[u] = (value[:, :K] + value[:, K:]).astype(BF)

        loop(0, 16, pick_sources)

        def whole(i):
            pair = [
                lax.dot_general(
                    sums[two_parent_s[2 * i + h]], two[2 * i + h], (((1,), (1,)), ((), ())), preferred_element_type=F32
                )
                for h in range(2)
            ]
            top_all[:, rows_at(i, 128)] = jnp.concatenate(pair, axis=1).astype(BF)

        loop(0, 64, whole, 4)

    def add_far(quarters):
        keys = far_target_ref[...] * 24 + far_source_ref[...]
        row = lax.broadcasted_iota(jnp.int32, (96, 192), 0)
        wanted = lax.rem(row, 8) * 24 + 2 * lax.div(row, 8)
        even = jnp.where(keys == wanted, 1.0, 0.0).astype(BF)
        odd = jnp.where(keys == wanted + 1, 1.0, 0.0).astype(BF)
        for q in quarters:
            far_fetch(q).wait()

            def add(step, q=q):
                for i in range(8):
                    block = b["far_chunk"][q % 2, step * 8 + i]
                    both = [
                        lax.dot_general(part, block, (((1,), (1,)), ((), ())), preferred_element_type=F32)
                        for part in (even, odd)
                    ]
                    both = jnp.concatenate(both, axis=1)
                    a = q * 16 + step * 8 + i
                    for s in range(12):
                        b["turned"][pl.ds(s * 512 + a, 8, stride=K), :] = both[8 * s : 8 * s + 8]

            loop(0, 2, add)
            if q < 2:
                far_fetch(q + 2).start()

    def build_last():
        for l in range(16):
            pair = jnp.concatenate([transfer[l], transfer[l]], axis=1)
            half = lax.broadcasted_iota(jnp.int32, (1, 128), 1) // K
            parent = number(2, l, 8)

            def build_down(i, l=l, pair=pair, half=half, parent=parent):
                down_mat[pl.ds(l * K, K), rows_at(i, 128)] = pair * chosen(half + 2 * i, parent)

            loop(0, 16, build_down, 4)

        add_far((2, 3))

        def write_far(i):
            for s in range(12):
                part = b["turned"][rows_at(s * 32 + i, 16), :]
                b["fl_mat"][rows_at(i, 16), pl.ds(s * P_SIZE, P_SIZE)] = part.astype(BF)

        loop(0, 32, write_far, 2)

    def apply(it, v, w, wb, beside_rs, beside_ag, beside_far, beside_l2):
        win, chalf, c2 = b["win"].at[it], b["chalf"], b["c2"].at[it]
        local_half, cw = b["local_half"], b["cw"]
        rs_out, rs_in = b["rs_out"], b["rs_in"].at[it]
        ag = [b["ag0"].at[it], b["ag1"].at[it], b["ag2"].at[it]]
        q_two, gathered = b["q_two"], b["gathered"]
        far_out, far_in, l2 = b["far_out"], b["far_in"].at[it], b["l2"].at[it]
        sib_out, sib_in, merged = b["sib_out"], b["sib_in"].at[it], b["merged"]

        def window_copy(side, half):
            first, device = (0, after) if side == 0 else (2048, before)
            i = side * 2 + half
            return remote(
                v.at[pl.ds(half * 512, 512)],
                win.at[pl.ds(first + half * 512, 512)],
                b["win_send"].at[it, i],
                b["win_recv"].at[it, i],
                device,
            )

        def window_start(half):
            @pl.when(has_after)
            def _():
                window_copy(0, half).start()

            @pl.when(has_before)
            def _():
                window_copy(1, half).start()

        def window_land(half):
            @pl.when(has_before)
            def _():
                window_copy(0, half).wait_recv()

            @pl.when(has_after)
            def _():
                window_copy(1, half).wait_recv()


        def own_coeffs(i):
            part = dot(basis[8 + i], v[rows_at(i, P_SIZE), :]).astype(BF)
            chalf[0, rows_at(i, K), :] = part[:, :HALF]
            chalf[1, rows_at(i, K), :] = part[:, HALF:]

        loop(0, 8, own_coeffs, 8)
        coeff_swap = remote(
            chalf.at[1 - core], c2.at[pl.ds(512, 512)], b["sib_send"].at[it, 0], b["sib_recv"].at[it, 0], sibling
        )
        coeff_swap.start()

        window_start(0)
        if it == 0:
            window_start(1)
        c2[pl.ds(0, 512), :] = chalf[core]
        win[pl.ds(1024, 1024), :] = v[...]
        if it == 0:
            build_up()
        coeff_swap.wait_recv()

        rs_rows = (pl.ds(0, 96), pl.ds(96, 32))

        def rs_copy(h, k):
            there, device = plane(k)
            rows, i = rs_rows[h], h * 16 + k
            return remote(
                rs_out.at[there, rows], rs_in.at[k, rows], b["rs_send"].at[it, i], b["rs_recv"].at[it, i], device
            )

        for h in range(2):

            def rs_step(k, h=h):
                there, _ = plane(k)
                rs_out[there, rs_rows[h]] = dot(tv_mat[there, rs_rows[h]], c2[...]).astype(BF)
                rs_copy(h, k).start()

            loop(1, 16, rs_step)
        rs_in[0] = dot(tv_mat[chip], c2[...]).astype(BF)
        beside_rs()

        def rs_total(h):
            def rs_sum(k, total):
                rs_copy(h, k).wait_recv()
                return total + rs_in[k, rs_rows[h]].astype(F32)

            return lax.fori_loop(1, 16, rs_sum, rs_in[0, rs_rows[h]].astype(F32)).astype(BF)

        homes = ((z * 4 + y) * 4 + x, (x * 4 + z) * 4 + y, (y * 4 + x) * 4 + z)
        orders = (("x", "y", "z"), ("y", "z", "x"), ("z", "x", "y"))
        lasts = (z, x, y)

        def ag_copy(stream, stage, k):
            if stage == 0:
                first, count = homes[stream], 1
            elif stage == 1:
                first, count = lax.div(homes[stream], 4) * 4, 4
            else:
                first, count = lasts[stream] * 16, 16
            part = ag[stream].at[pl.ds(first, count)]
            i = (stream * 3 + stage) * 3 + k - 1
            return remote(
                part, part, b["ag_send"].at[it, i], b["ag_recv"].at[it, i], along(orders[stream][stage], k)
            )

        def ag_start(stream, stage):
            for k in range(1, 4):
                ag_copy(stream, stage, k).start()

        def ag_land(stream, stage):
            for k in range(1, 4):
                ag_copy(stream, stage, k).wait_recv()

        total = rs_total(0)
        ag[0][homes[0]] = total[0:48]
        ag[1][homes[1]] = total[48:96]
        ag_start(0, 0)
        ag_start(1, 0)
        total = rs_total(1)
        ag[2][homes[2]] = total
        ag_start(2, 0)
        for stream in range(3):
            ag_land(stream, 0)
            ag_start(stream, 1)
        for stream in range(3):
            ag_land(stream, 1)
            ag_start(stream, 2)

        beside_ag()

        window_land(0)
        if it == 0:
            for load in loads:
                load.wait()

            @pl.when(has_before)
            def _():
                basis_after.wait_recv()

            @pl.when(has_after)
            def _():
                basis_before.wait_recv()

        def window_coeffs(i):
            cw[rows_at(i, K), :] = dot(basis[i], win[rows_at(i, P_SIZE), :]).astype(BF)

        loop(0, 4, window_coeffs, 4)
        loop(8, 20, window_coeffs, 4)

        def near_dot(i, first, size):
            return dot(b["c_mat"][rows_at(i, 128), pl.ds(first, size)], win[pl.ds(first, size), :])

        def near_most(i):
            w[rows_at(i, 128), :] = near_dot(i, 0, 512) + near_dot(i, 1024, 1536)

        loop(0, 8, near_most)
        for stream in range(3):
            ag_land(stream, 2)

        if it == 1:
            window_start(1)

        def join(i):
            ip, g = i // 4, i % 4
            iz, iy = ip // 4, ip % 4
            first, second, third = ag[0][i], ag[1][(g * 4 + iz) * 4 + iy], ag[2][(iy * 4 + g) * 4 + iz]
            q_two[g * 32 + 2 * ip] = jnp.concatenate([first, second[0:16]], axis=0)
            q_two[g * 32 + 2 * ip + 1] = jnp.concatenate([second[16:48], third], axis=0)

        loop(0, 64, join, 4)

        for j in range(32):
            gathered[pl.ds(j * K, K), :] = q_two[number(1, j, 16)]

        def far_copy(h, k):
            there, device = plane(k)
            rows, i = pl.ds(h * K, K), h * 16 + k
            return remote(
                far_out.at[there, rows],
                far_in.at[k, rows],
                b["far_send"].at[it, i],
                b["far_recv"].at[it, i],
                device,
            )

        for h in range(2):

            def far_step(k, h=h):
                there, _ = plane(k)
                far_out[there, pl.ds(h * K, K)] = dot(s_mat[there, pl.ds(h * K, K)], gathered[...]).astype(BF)
                far_copy(h, k).start()

            loop(1, 16, far_step)
        own = dot(s_mat[chip], gathered[...])

        def fall(i, total):
            part = q_two[pl.ds(i * 16, 16)].reshape(1024, HALF)
            return total + dot(b["top_all"][:, rows_at(i, 1024)], part)

        own = lax.fori_loop(0, 8, fall, own)
        beside_far()

        def l2_copy(h, k):
            part = l2.at[rows_at(chip * 2 + h, K)]
            i = h * 16 + k
            return remote(part, part, b["l2_send"].at[it, i], b["l2_recv"].at[it, i], plane(k)[1])

        for h in range(2):

            def far_sum(k, total, h=h):
                far_copy(h, k).wait_recv()
                return total + far_in[k, pl.ds(h * K, K)].astype(F32)

            half_sum = lax.fori_loop(1, 16, far_sum, own[h * K : (h + 1) * K])
            l2[rows_at(chip * 2 + h, K), :] = half_sum.astype(BF)

            def l2_start(k, h=h):
                l2_copy(h, k).start()

            loop(1, 16, l2_start)

        def drain(k):
            for h in range(2):
                rs_copy(h, k).wait_send()
                far_copy(h, k).wait_send()

        loop(1, 16, drain)
        coeff_swap.wait_send()
        for stream in range(3):
            for stage in range(3):
                for k in range(1, 4):
                    ag_copy(stream, stage, k).wait_send()

        for half in range(2):

            @pl.when(has_after)
            def _(half=half):
                window_copy(0, half).wait_send()

            @pl.when(has_before)
            def _(half=half):
                window_copy(1, half).wait_send()

        beside_l2()

        window_land(1)
        loop(4, 8, window_coeffs, 4)
        loop(20, 24, window_coeffs, 4)

        def leaf_far(i):
            part = dot(b["fl_mat"][rows_at(i, 128), :], cw[...])
            local_half[0, rows_at(i, 128), :] = part[:, :HALF]
            local_half[1, rows_at(i, 128), :] = part[:, HALF:]

        loop(0, 4, leaf_far)

        def near_rest(i):
            w[rows_at(i, 128), :] = w[rows_at(i, 128), :] + near_dot(i, 512, 512) + near_dot(i, 2560, 512)

        loop(0, 8, near_rest)

        def l2_land(k):
            for h in range(2):
                l2_copy(h, k).wait_recv()

        loop(1, 16, l2_land)

        def down_sibling(i):
            sib_out[rows_at(i, 128), :] = dot(down_mat[rows_at(i + 4, 128), :], l2[...]).astype(BF)

        loop(0, 4, down_sibling)
        leaf_swap = remote(sib_out, sib_in, b["sib_send"].at[it, 1], b["sib_recv"].at[it, 1], sibling)
        leaf_swap.start()

        def down_own(i):
            rows = rows_at(i, 128)
            merged[core, rows, :] = (local_half[core, rows, :] + dot(down_mat[rows, :], l2[...])).astype(BF)

        loop(0, 4, down_own)
        leaf_swap.wait_recv()
        merged[1 - core] = (local_half[1 - core] + sib_in[...].astype(F32)).astype(BF)

        def finish(i):
            rows = rows_at(i, P_SIZE)
            for h in range(2):
                lanes = pl.ds(h * HALF, HALF)
                value = w[rows, lanes] + lax.dot_general(
                    basis[8 + i],
                    merged[h, rows_at(i, K), :],
                    (((0,), (0,)), ((), ())),
                    preferred_element_type=F32,
                )
                w[rows, lanes] = value
                if wb is not None:
                    wb[rows, lanes] = value.astype(BF)

        loop(0, 8, finish, 2)
        leaf_swap.wait_send()

        def l2_sent(k):
            for h in range(2):
                l2_copy(h, k).wait_send()

        loop(1, 16, l2_sent)

    p_slot, w1, w2 = b["p_slot"], b["w1"], b["w2"]

    def unorder():
        def split_image(i):
            rows = rows_at(i, 128)
            value = w1[rows, :]
            top = value.astype(BF)
            high[rows, pl.ds(0, 256)] = top
            high[rows, pl.ds(256, 256)] = (value - top.astype(F32)).astype(BF)

        loop(0, 8, split_image)

        def reorder(i):
            wanted = lax.broadcasted_iota(jnp.int32, (128, 1024), 0) + i * 128
            hot = jnp.where(panels_row[...] == wanted, 1.0, 0.0).astype(BF)
            value = dot(hot, high[...])
            w1_panel[rows_at(i, 128), :] = value[:, :256] + value[:, 256:]

        loop(0, 8, reorder)

    def col_max(ref):
        return jnp.maximum(jnp.max(jnp.abs(ref[...]), axis=0, keepdims=True), 1e-30)

    def col_sums(terms):
        def add(i, carry):
            return tuple(
                c + jnp.sum(t.reshape(4, 8, 256), axis=0) for c, t in zip(carry, terms(rows_at(i, 32)))
            )

        sums = lax.fori_loop(0, 32, add, tuple(jnp.zeros((8, 256), F32) for _ in range(3)), unroll=2)
        return [jnp.sum(s, axis=0, keepdims=True) for s in sums]

    early = []

    def early_sums():
        size_p, size_a = col_max(p_slot), col_max(w1)
        inv_p, inv_a = 1.0 / size_p, 1.0 / size_a

        def terms(rows):
            p, a = p_slot[rows, :] * inv_p, w1[rows, :] * inv_a
            return p * p, p * a, a * a

        early.extend((size_p, size_a, col_sums(terms)))

    v1 = b["v0"]
    apply(0, b["v0"], w1, v1, build_rest, build_top, lambda: add_far((0, 1)), build_last)
    for swap in swaps:
        swap.wait_send()

    @pl.when(has_after)
    def _():
        basis_after.wait_send()

    @pl.when(has_before)
    def _():
        basis_before.wait_send()

    apply(1, v1, w2, None, unorder, early_sums, lambda: None, lambda: None)

    size_p, size_a, sums = early
    size_b = col_max(w2)
    inv_p, inv_a, inv_b = 1.0 / size_p, 1.0 / size_a, 1.0 / size_b

    def late_terms(rows):
        value = w2[rows, :] * inv_b
        return p_slot[rows, :] * inv_p * value, w1[rows, :] * inv_a * value, value * value

    sums = sums + col_sums(late_terms)
    sizes = [size_p, size_a, size_b]
    part, box = b["part"], b["box"]
    pairs = ((0, 0), (0, 1), (1, 1), (0, 2), (1, 2), (2, 2))
    coords = (core, x, y, z)
    axes = ("core", "x", "y", "z")

    def sum_copy(stage, k):
        i = stage * 4 + k
        here = box.at[stage, coords[stage]]
        return remote(here, here, b["sum_send"].at[i], b["sum_recv"].at[i], along(axes[stage], k))

    for stage in range(4):
        count = 2 if stage == 0 else 4
        for i in range(6):
            part[i : i + 1, :] = sums[i]
        for i in range(3):
            part[8 + i : 9 + i, :] = sizes[i]
        box[stage, coords[stage]] = part[...]
        for k in range(1, count):
            sum_copy(stage, k).start()
        for k in range(1, count):
            sum_copy(stage, k).wait_recv()
        got = [box[stage, i] for i in range(count)]
        new_sizes = []
        for i in range(3):
            top_size = got[0][8 + i : 9 + i]
            for g in got[1:]:
                top_size = jnp.maximum(top_size, g[8 + i : 9 + i])
            new_sizes.append(top_size)
        factors = [[g[8 + i : 9 + i] / new_sizes[i] for i in range(3)] for g in got]
        sums = []
        for i, (first, second) in enumerate(pairs):
            value = got[0][i : i + 1] * (factors[0][first] * factors[0][second])
            for g, f in zip(got[1:], factors[1:]):
                value = value + g[i : i + 1] * (f[first] * f[second])
            sums.append(value)
        sizes = new_sizes

    along_p, along_a, estimate = project(sums, sizes)
    weights_ref[0:1, :] = along_p
    weights_ref[1:2, :] = along_a
    weights_ref[2:3, :] = estimate
    for stage in range(4):
        for k in range(1, 2 if stage == 0 else 4):
            sum_copy(stage, k).wait_send()


def both_steps(smem_args, vmem_args, hbm_args):
    smem = pl.BlockSpec(memory_space=pltpu.SMEM)
    vmem = pl.BlockSpec(memory_space=pltpu.VMEM)
    anywhere = pl.BlockSpec(memory_space=pl.ANY)
    return pl.pallas_call(
        steps_kernel,
        out_shape=(jax.ShapeDtypeStruct((1024, 256), F32), jax.ShapeDtypeStruct((8, 256), F32)),
        in_specs=[smem] * len(smem_args) + [vmem] * len(vmem_args) + [anywhere] * len(hbm_args),
        out_specs=(vmem, vmem),
        scratch_shapes=list(BUFFERS.values()),
        compiler_params=pltpu.CompilerParams(
            collective_id=1, has_side_effects=True, vmem_limit_bytes=62 * 1024 * 1024
        ),
        name="both_steps",
    )(*smem_args, *vmem_args, *hbm_args)


def result_kernel(weights_ref, pot_ref, image_ref, out_ref, est_ref):
    out_ref[...] = weights_ref[0:1, :] * pot_ref[...] + weights_ref[1:2, :] * image_ref[...]
    est_ref[...] = weights_ref[2, :]


def result(weights, potentials, image):
    return pl.pallas_call(
        result_kernel,
        out_shape=(jax.ShapeDtypeStruct((1024, 256), F32), jax.ShapeDtypeStruct((256,), F32)),
        compiler_params=pltpu.CompilerParams(vmem_limit_bytes=60 * 1024 * 1024),
        name="result",
    )(weights, potentials, image)


def least_squares(beta_norm, first_diag, first_below, second_top, second_diag, second_below):
    first_radius = jnp.sqrt(first_diag * first_diag + first_below * first_below)
    first_cos = first_diag / first_radius
    first_sin = first_below / first_radius
    upper_term = first_cos * second_top + first_sin * second_diag
    lower_term = first_cos * second_diag - first_sin * second_top
    second_radius = jnp.sqrt(lower_term * lower_term + second_below * second_below)
    second_cos = lower_term / second_radius
    second_sin = second_below / second_radius
    weight_two = -first_sin * beta_norm * second_cos / second_radius
    weight_one = (first_cos * beta_norm - upper_term * weight_two) / first_radius
    return (weight_one, weight_two, first_sin * second_sin * beta_norm)


def project(sums, sizes):
    pp, pa, aa, pb, ab, bb = sums
    size_p, size_a, size_b = sizes
    beta = jnp.sqrt(size_p * size_p * pp + EPS)
    scale_p, scale_a, scale_b = size_p / beta, size_a / beta, size_b / beta
    first_first = scale_p * scale_p * pp
    first_image = scale_p * scale_a * pa
    first_diag = first_image
    image_image = scale_a * scale_a * aa
    rest = image_image - first_diag * first_diag * (2.0 - first_first)
    first_below = jnp.sqrt(jnp.maximum(rest, 0.0) + EPS)
    inverse = 1.0 / first_below
    first_second = (first_image - first_diag * first_first) * inverse
    second_second = jnp.maximum(rest, 0.0) * inverse * inverse
    scale_two = scale_b * inverse
    diag_two = first_diag * inverse
    first_b = scale_p * scale_two * pb
    a_b = scale_a * scale_two * ab
    b_b = scale_two * scale_two * bb
    second_top = first_b - diag_two * first_image
    image_image_two = a_b - diag_two * image_image
    second_diag = (image_image_two - first_diag * second_top) * inverse
    square = b_b - 2.0 * diag_two * a_b + diag_two * diag_two * image_image
    rest_two = (
        square
        - second_top * second_top * (2.0 - first_first)
        - second_diag * second_diag * (2.0 - second_second)
        + 2.0 * second_top * second_diag * first_second
    )
    second_below = jnp.sqrt(jnp.maximum(rest_two, 0.0) + EPS)
    weight_one, weight_two, estimate = least_squares(
        beta, first_diag, first_below, second_top, second_diag, second_below
    )
    along_a = weight_two * inverse / beta
    along_p = weight_one / beta - along_a * first_diag
    return along_p, along_a, estimate


def on_device(
    potentials,
    leaf_panels,
    near_blocks,
    near_target,
    near_source,
    near_count,
    leaf_basis,
    far_leaf,
    far_leaf_target,
    far_leaf_source,
    leaf_transfer,
    leaf_parent,
    far_two,
    far_two_target,
    far_two_source,
    two_transfer,
    two_parent,
    far_one,
    far_one_target,
    far_one_source,
):
    c_mat = combine(near_target, near_source, near_count, near_blocks)
    own_numbers = (far_two_target, far_two_source, leaf_parent.reshape(1, 8))
    image, weights = both_steps(
        own_numbers + (two_parent, far_one_target, far_one_source),
        own_numbers
        + (
            leaf_panels,
            potentials,
            leaf_basis,
            leaf_transfer,
            far_two,
            jnp.transpose(two_transfer, (1, 2, 0)),
            far_one,
            far_leaf_target,
            far_leaf_source,
        ),
        (c_mat, jnp.transpose(far_leaf, (1, 2, 0))),
    )
    return result(weights, potentials, image)


def solution(mesh):
    both = P(("grp", "leaf"))
    in_specs = (both,) * 15 + (P(),) * 5
    return jax.shard_map(
        on_device, mesh=mesh, in_specs=in_specs, out_specs=(both, P()), check_vma=False
    )
```

```python
import jax
import jax.numpy as jnp
from jax import lax
from jax.experimental import pallas as pl
from jax.experimental.pallas import tpu as pltpu
from jax.sharding import PartitionSpec as P

P_SIZE = 128
K = 64
HALF = 128
EPS = 1e-06
BF = jnp.bfloat16
F32 = jnp.float32
MESH = pl.DeviceIdType.MESH
VMEM = pltpu.VMEM
DMA = pltpu.SemaphoreType.DMA
NEAR_STEPS = 8


def dot(a, b):
    return jnp.dot(a, b, preferred_element_type=F32)


def combine_kernel(near_target, near_source, near_count, near_hbm, c_hbm, blocks, acc, stage, load_sems, sems):
    window = 24
    per_step = blocks.shape[0] // NEAR_STEPS
    loads = []
    for step in range(NEAR_STEPS):
        part = pl.ds(step * per_step, per_step)
        loads.append(pltpu.make_async_copy(near_hbm.at[part], blocks.at[part], load_sems.at[step]))
        loads[-1].start()

    def zero(i, carry):
        acc[i] = jnp.zeros((P_SIZE, P_SIZE), F32)
        return carry

    lax.fori_loop(0, acc.shape[0], zero, 0, unroll=8)
    live = near_count[0]

    def add(j, carry):
        key = near_target[0, j] * window + near_source[0, j]
        acc[key] = acc[key] + blocks[j].astype(F32)
        return carry

    for step in range(NEAR_STEPS):
        loads[step].wait()
        first = step * per_step
        lax.fori_loop(first, jnp.clip(live, first, first + per_step), add, 0)
    copies = []
    for t in range(8):
        rows = pl.ds(t * P_SIZE, P_SIZE)

        def write(s, carry, t=t, rows=rows):
            lanes = pl.ds(pl.multiple_of(s * P_SIZE, P_SIZE), P_SIZE)
            stage[rows, lanes] = acc[t * window + s].astype(BF)
            return carry

        lax.fori_loop(0, window, write, 0, unroll=8)
        copies.append(pltpu.make_async_copy(stage.at[rows], c_hbm.at[rows], sems.at[t]))
        copies[-1].start()
    for copy in copies:
        copy.wait()


def combine(near_target, near_source, near_count, near_blocks):
    smem = pl.BlockSpec(memory_space=pltpu.SMEM)
    anywhere = pl.BlockSpec(memory_space=pl.ANY)
    return pl.pallas_call(
        combine_kernel,
        out_shape=jax.ShapeDtypeStruct((1024, 3072), BF),
        in_specs=[smem] * 3 + [anywhere],
        out_specs=anywhere,
        scratch_shapes=[
            VMEM(near_blocks.shape, BF),
            VMEM((192, P_SIZE, P_SIZE), F32),
            VMEM((1024, 3072), BF),
            DMA((NEAR_STEPS,)),
            DMA((8,)),
        ],
        compiler_params=pltpu.CompilerParams(vmem_limit_bytes=56 * 1024 * 1024),
        cost_estimate=pl.CostEstimate(flops=10**7, bytes_accessed=20 * 10**6, transcendentals=0),
        name="combine",
    )(near_target, near_source, near_count, near_blocks)


def remote(src, dst, send, recv, device):
    return pltpu.make_async_remote_copy(
        src_ref=src, dst_ref=dst, send_sem=send, recv_sem=recv, device_id=device, device_id_type=MESH
    )


def place():
    x = lax.axis_index("grp")
    leaf = lax.axis_index("leaf")
    core = lax.rem(leaf, 2)
    chip = lax.div(leaf, 2)
    return x, lax.div(chip, 4), lax.rem(chip, 4), core


def leaf_of(z, y, core):
    return (z * 4 + y) * 2 + core


def loop(start, stop, body, unroll=1):
    def step(i, carry):
        body(i)
        return carry

    lax.fori_loop(start, stop, step, 0, unroll=unroll)


def rows_at(i, size):
    return pl.ds(pl.multiple_of(i * size, size), size)


BUFFERS = dict(
    c_mat=VMEM((1024, 3072), BF),
    fl_mat=VMEM((512, 1536), BF),
    tv_mat=VMEM((16, 128, 1024), BF),
    s_mat=VMEM((16, 128, 2048), BF),
    down_mat=VMEM((1024, 2048), BF),
    top_mat=VMEM((128, 2048), BF),
    turned=VMEM((6144, 128), F32),
    two=VMEM((128, K, K), BF),
    top_sums=VMEM((16, 128, K), BF),
    far_chunk=VMEM((2, 16, K, 192), BF),
    chunk_sem=DMA((2,)),
    top_all=VMEM((128, 8192), BF),
    up=VMEM((K, 1024), BF),
    far_flat=VMEM((K, 2048), BF),
    transfer=VMEM((16, K, K), BF),
    far_all=VMEM((32, K, K), BF),
    basis=VMEM((24, K, P_SIZE), BF),
    other_target=VMEM((1, 16), jnp.int32),
    other_source=VMEM((1, 16), jnp.int32),
    other_parent=VMEM((1, 8), jnp.int32),
    target_o=pltpu.SMEM((1, 16), jnp.int32),
    source_o=pltpu.SMEM((1, 16), jnp.int32),
    parent_o=pltpu.SMEM((1, 8), jnp.int32),
    v0=VMEM((1024, 256), BF),
    p_slot=VMEM((1024, 256), F32),
    w1=VMEM((1024, 256), F32),
    w2=VMEM((1024, 256), F32),
    high=VMEM((1024, 512), BF),
    part=VMEM((16, 256), F32),
    box=VMEM((4, 4, 16, 256), F32),
    win=VMEM((2, 3072, 256), BF),
    cw=VMEM((1536, 256), BF),
    chalf=VMEM((2, 512, HALF), BF),
    c2=VMEM((2, 1024, HALF), BF),
    local_half=VMEM((2, 512, HALF), F32),
    rs_out=VMEM((16, 128, HALF), BF),
    rs_in=VMEM((2, 16, 128, HALF), BF),
    ag0=VMEM((2, 64, 48, HALF), BF),
    ag1=VMEM((2, 64, 48, HALF), BF),
    ag2=VMEM((2, 64, 32, HALF), BF),
    q_two=VMEM((128, K, HALF), BF),
    gathered=VMEM((2048, HALF), BF),
    far_out=VMEM((16, 128, HALF), BF),
    far_in=VMEM((2, 16, 128, HALF), BF),
    l2=VMEM((2, 2048, HALF), BF),
    sib_out=VMEM((512, HALF), BF),
    sib_in=VMEM((2, 512, HALF), BF),
    merged=VMEM((2, 512, HALF), BF),
    load_sem=DMA((5,)),
    ex_send=DMA((7,)),
    ex_recv=DMA((7,)),
    win_send=DMA((2, 4)),
    win_recv=DMA((2, 4)),
    sib_send=DMA((2, 2)),
    sib_recv=DMA((2, 2)),
    rs_send=DMA((2, 32)),
    rs_recv=DMA((2, 32)),
    ag_send=DMA((2, 27)),
    ag_recv=DMA((2, 27)),
    far_send=DMA((2, 32)),
    far_recv=DMA((2, 32)),
    l2_send=DMA((2, 32)),
    l2_recv=DMA((2, 32)),
    sum_send=DMA((16,)),
    sum_recv=DMA((16,)),
)
NAMES = tuple(BUFFERS)


def steps_kernel(
    target_s,
    source_s,
    parent_s,
    two_parent_s,
    one_target_s,
    one_source_s,
    target_ref,
    source_ref,
    parent_ref,
    panels_row,
    pot_ref,
    basis_ref,
    transfer_ref,
    far_ref,
    two_ref,
    one_ref,
    far_target_ref,
    far_source_ref,
    c_hbm,
    far_leaf_hbm,
    w1_panel,
    weights_ref,
    *scratch,
):
    b = dict(zip(NAMES, scratch))
    basis, transfer, far_all = b["basis"], b["transfer"], b["far_all"]
    up, far_flat = b["up"], b["far_flat"]
    tv_mat, s_mat, down_mat, top_mat = b["tv_mat"], b["s_mat"], b["down_mat"], b["top_mat"]
    x, z, y, core = place()
    chip = z * 4 + y
    me = x * 32 + chip * 2 + core

    loads = [
        pltpu.make_async_copy(c_hbm, b["c_mat"], b["load_sem"].at[0]),
    ]
    for load in loads:
        load.start()

    def far_fetch(q):
        return pltpu.make_async_copy(
            far_leaf_hbm.at[pl.ds(q * 16, 16)], b["far_chunk"].at[q % 2], b["chunk_sem"].at[q % 2]
        )

    for q in range(2):
        far_fetch(q).start()

    sibling = (x, chip * 2 + 1 - core)
    before = (lax.rem(lax.div(me + 127, 32), 4), lax.rem(me + 31, 32))
    after = (lax.rem(lax.div(me + 1, 32), 4), lax.rem(me + 1, 32))
    has_before = me > 0
    has_after = me < 127

    def plane(k):
        k = lax.rem(5 * k, 16)
        tz = lax.rem(z + lax.div(k, 4), 4)
        ty = lax.rem(y + lax.rem(k, 4), 4)
        return tz * 4 + ty, (x, leaf_of(tz, ty, core))

    def along(axis, k):
        if axis == "x":
            return (lax.rem(x + k, 4), leaf_of(z, y, core))
        if axis == "y":
            return (x, leaf_of(z, lax.rem(y + k, 4), core))
        if axis == "z":
            return (x, leaf_of(lax.rem(z + k, 4), y, core))
        return sibling

    barrier = pltpu.get_barrier_semaphore()

    def greet(k):
        pl.semaphore_signal(barrier, inc=1, device_id=plane(k)[1], device_id_type=MESH)

    loop(1, 16, greet)
    for k in range(1, 4):
        pl.semaphore_signal(barrier, inc=1, device_id=along("x", k), device_id_type=MESH)
    pl.semaphore_signal(barrier, inc=1, device_id=sibling, device_id_type=MESH)

    @pl.when(has_before)
    def _():
        pl.semaphore_signal(barrier, inc=1, device_id=before, device_id_type=MESH)

    @pl.when(has_after)
    def _():
        pl.semaphore_signal(barrier, inc=1, device_id=after, device_id_type=MESH)

    high = b["high"]

    def split(i):
        rows = rows_at(i, 128)
        value = pot_ref[rows, :]
        top = value.astype(BF)
        high[rows, pl.ds(0, 256)] = top
        high[rows, pl.ds(256, 256)] = (value - top.astype(F32)).astype(BF)

    loop(0, 8, split)

    def order(i):
        rows = rows_at(i, 128)
        wanted = lax.broadcasted_iota(jnp.int32, (128, 128), 1).astype(F32)
        column = jnp.broadcast_to(panels_row[:, rows].astype(F32), (128, 128)).T
        hot = [jnp.where(column == wanted + 128.0 * q, 1.0, 0.0).astype(BF) for q in range(8)]
        hot = jnp.concatenate(hot, axis=1)
        value = dot(hot, high[...])
        b["v0"][rows, :] = value[:, :256].astype(BF)
        b["p_slot"][rows, :] = value[:, :256] + value[:, 256:]

    loop(0, 8, order)
    basis[pl.ds(8, 8)] = basis_ref[...]
    transfer[pl.ds(0, 8)] = transfer_ref[...]
    far_all[pl.ds(0, 16)] = far_ref[...]

    for it in range(2):

        @pl.when(jnp.logical_not(has_before))
        def _():
            b["win"][it, pl.ds(0, 1024), :] = jnp.zeros((1024, 256), BF)

        @pl.when(jnp.logical_not(has_after))
        def _():
            b["win"][it, pl.ds(2048, 1024), :] = jnp.zeros((1024, 256), BF)

    @pl.when(jnp.logical_not(has_before))
    def _():
        basis[pl.ds(0, 8)] = jnp.zeros((8, K, P_SIZE), BF)

    @pl.when(jnp.logical_not(has_after))
    def _():
        basis[pl.ds(16, 8)] = jnp.zeros((8, K, P_SIZE), BF)

    def first_coeffs(i):
        part = dot(basis_ref[i], b["v0"][rows_at(i, P_SIZE), :]).astype(BF)
        b["chalf"][0, rows_at(i, K), :] = part[:, :HALF]
        b["chalf"][1, rows_at(i, K), :] = part[:, HALF:]

    loop(0, 8, first_coeffs, 8)
    pl.semaphore_wait(barrier, 19 + has_before.astype(jnp.int32) + has_after.astype(jnp.int32))

    ex_send, ex_recv = b["ex_send"], b["ex_recv"]
    swaps = [
        remote(target_ref, b["other_target"], ex_send.at[0], ex_recv.at[0], sibling),
        remote(source_ref, b["other_source"], ex_send.at[5], ex_recv.at[5], sibling),
        remote(parent_ref, b["other_parent"], ex_send.at[6], ex_recv.at[6], sibling),
        remote(transfer_ref, transfer.at[pl.ds(8, 8)], ex_send.at[1], ex_recv.at[1], sibling),
        remote(far_ref, far_all.at[pl.ds(16, 16)], ex_send.at[2], ex_recv.at[2], sibling),
    ]
    for swap in swaps:
        swap.start()
    basis_after = remote(basis_ref, basis.at[pl.ds(0, 8)], ex_send.at[3], ex_recv.at[3], after)
    basis_before = remote(basis_ref, basis.at[pl.ds(16, 8)], ex_send.at[4], ex_recv.at[4], before)

    @pl.when(has_after)
    def _():
        basis_after.start()

    @pl.when(has_before)
    def _():
        basis_before.start()

    numbers = (
        (target_s, b["target_o"]),
        (source_s, b["source_o"]),
        (parent_s, b["parent_o"]),
    )

    def number(row, i, count):
        own, other = numbers[row]
        return own[0, i] if i < count else other[0, i - count]

    def spread(values, lanes):
        index = lax.broadcasted_iota(jnp.int32, (1, lanes), 1) // K
        found = jnp.zeros((1, lanes), jnp.int32)
        for i, value in enumerate(values):
            found = jnp.where(index == i, value, found)
        return found

    def chosen(found, value):
        return jnp.where(found == value, 1.0, 0.0).astype(BF)

    def build_up():
        for swap in swaps[:4]:
            swap.wait_recv()
        fetches = [
            pltpu.make_async_copy(b["other_" + name], b[name + "_o"], b["load_sem"].at[2 + i])
            for i, name in enumerate(("target", "source", "parent"))
        ]
        for fetch in fetches:
            fetch.start()
        for fetch in fetches:
            fetch.wait()
        parents = [number(2, l, 8) for l in range(16)]
        for i in range(8):
            lanes = pl.ds(i * 128, 128)
            pair = transfer[pl.ds(2 * i, 2)].reshape(128, K)
            up[:, lanes] = pair.astype(F32).T.astype(BF)
        parent_lanes = spread(parents, 1024)

        def build(c):
            tv_mat[c // 2, rows_at(c % 2, K), :] = up[...] * chosen(parent_lanes, c)

        loop(0, 32, build)

    def build_rest():
        swaps[4].wait_recv()
        targets = [number(0, j, 16) for j in range(32)]
        for i in range(16):
            far_flat[:, pl.ds(i * 128, 128)] = jnp.concatenate([far_all[2 * i], far_all[2 * i + 1]], axis=1)
        target_lanes = spread(targets, 2048)

        def build_far(c):
            s_mat[c // 2, rows_at(c % 2, K), :] = far_flat[...] * chosen(target_lanes, c)

        loop(0, 32, build_far)

        turned, two = b["turned"], b["two"]

        def turn(a):
            block = two_ref[a].astype(F32).T
            turned[pl.ds(a, K, stride=K), :] = jnp.concatenate([block[:K], block[K:]], axis=1)

        loop(0, K, turn, 4)

        def shorten(c):
            block = turned[rows_at(c, K), :].astype(BF)
            two[c] = block[:, :K]
            two[K + c] = block[:, K:]

        loop(0, K, shorten, 4)

    def build_top():
        one_lanes = spread([one_target_s[j] for j in range(32)], 2048)
        for i in range(16):
            far_flat[:, pl.ds(i * 128, 128)] = jnp.concatenate([one_ref[2 * i], one_ref[2 * i + 1]], axis=1)
        for h in range(2):
            wanted = two_parent_s[x * 32 + chip * 2 + h]
            top_mat[pl.ds(h * K, K), :] = far_flat[...] * chosen(one_lanes, wanted)

        turned, two, sums, top_all = (b[n] for n in ("turned", "two", "top_sums", "top_all"))

        for h in range(2):
            value = dot(two[x * 32 + chip * 2 + h], top_mat[pl.ds(h * K, K), :])
            for i in range(16):
                turned[pl.ds(i * 128 + h * K, K), :] = value[:, i * 128 : (i + 1) * 128]
        source_lanes = spread([one_source_s[j] for j in range(32)], 2048)

        def pick_sources(u):
            found = jnp.where(source_lanes == u, 1.0, 0.0)
            value = turned[pl.ds(0, 128), :] * found[:, 0:128]
            for i in range(1, 16):
                value = value + turned[pl.ds(i * 128, 128), :] * found[:, i * 128 : (i + 1) * 128]
            sums[u] = (value[:, :K] + value[:, K:]).astype(BF)

        loop(0, 16, pick_sources)

        def whole(i):
            pair = [
                lax.dot_general(
                    sums[two_parent_s[2 * i + h]], two[2 * i + h], (((1,), (1,)), ((), ())), preferred_element_type=F32
                )
                for h in range(2)
            ]
            top_all[:, rows_at(i, 128)] = jnp.concatenate(pair, axis=1).astype(BF)

        loop(0, 64, whole, 4)

    def add_far(quarters):
        keys = far_target_ref[...] * 24 + far_source_ref[...]
        row = lax.broadcasted_iota(jnp.int32, (96, 192), 0)
        wanted = lax.rem(row, 8) * 24 + 2 * lax.div(row, 8)
        even = jnp.where(keys == wanted, 1.0, 0.0).astype(BF)
        odd = jnp.where(keys == wanted + 1, 1.0, 0.0).astype(BF)
        for q in quarters:
            far_fetch(q).wait()

            def add(step, q=q):
                for i in range(8):
                    block = b["far_chunk"][q % 2, step * 8 + i]
                    both = [
                        lax.dot_general(part, block, (((1,), (1,)), ((), ())), preferred_element_type=F32)
                        for part in (even, odd)
                    ]
                    both = jnp.concatenate(both, axis=1)
                    a = q * 16 + step * 8 + i
                    for s in range(12):
                        b["turned"][pl.ds(s * 512 + a, 8, stride=K), :] = both[8 * s : 8 * s + 8]

            loop(0, 2, add)
            if q < 2:
                far_fetch(q + 2).start()

    def build_last():
        for l in range(16):
            pair = jnp.concatenate([transfer[l], transfer[l]], axis=1)
            half = lax.broadcasted_iota(jnp.int32, (1, 128), 1) // K
            parent = number(2, l, 8)

            def build_down(i, l=l, pair=pair, half=half, parent=parent):
                down_mat[pl.ds(l * K, K), rows_at(i, 128)] = pair * chosen(half + 2 * i, parent)

            loop(0, 16, build_down, 4)

        add_far((2, 3))

        def write_far(i):
            for s in range(12):
                part = b["turned"][rows_at(s * 32 + i, 16), :]
                b["fl_mat"][rows_at(i, 16), pl.ds(s * P_SIZE, P_SIZE)] = part.astype(BF)

        loop(0, 32, write_far, 2)

    def apply(it, v, w, wb, beside_rs, beside_ag, beside_far, beside_l2):
        win, chalf, c2 = b["win"].at[it], b["chalf"], b["c2"].at[it]
        local_half, cw = b["local_half"], b["cw"]
        rs_out, rs_in = b["rs_out"], b["rs_in"].at[it]
        ag = [b["ag0"].at[it], b["ag1"].at[it], b["ag2"].at[it]]
        q_two, gathered = b["q_two"], b["gathered"]
        far_out, far_in, l2 = b["far_out"], b["far_in"].at[it], b["l2"].at[it]
        sib_out, sib_in, merged = b["sib_out"], b["sib_in"].at[it], b["merged"]

        def window_copy(side, half):
            first, device = (0, after) if side == 0 else (2048, before)
            i = side * 2 + half
            return remote(
                v.at[pl.ds(half * 512, 512)],
                win.at[pl.ds(first + half * 512, 512)],
                b["win_send"].at[it, i],
                b["win_recv"].at[it, i],
                device,
            )

        def window_start(half):
            @pl.when(has_after)
            def _():
                window_copy(0, half).start()

            @pl.when(has_before)
            def _():
                window_copy(1, half).start()

        def window_land(half):
            @pl.when(has_before)
            def _():
                window_copy(0, half).wait_recv()

            @pl.when(has_after)
            def _():
                window_copy(1, half).wait_recv()


        def own_coeffs(i):
            part = dot(basis[8 + i], v[rows_at(i, P_SIZE), :]).astype(BF)
            chalf[0, rows_at(i, K), :] = part[:, :HALF]
            chalf[1, rows_at(i, K), :] = part[:, HALF:]

        if it == 1:
            loop(0, 8, own_coeffs, 8)
        coeff_swap = remote(
            chalf.at[1 - core], c2.at[pl.ds(512, 512)], b["sib_send"].at[it, 0], b["sib_recv"].at[it, 0], sibling
        )
        coeff_swap.start()

        window_start(0)
        if it == 0:
            window_start(1)
        c2[pl.ds(0, 512), :] = chalf[core]
        win[pl.ds(1024, 1024), :] = v[...]
        if it == 0:
            build_up()
        coeff_swap.wait_recv()

        rs_rows = (pl.ds(0, 96), pl.ds(96, 32))

        def rs_copy(h, k):
            there, device = plane(k)
            rows, i = rs_rows[h], h * 16 + k
            return remote(
                rs_out.at[there, rows], rs_in.at[k, rows], b["rs_send"].at[it, i], b["rs_recv"].at[it, i], device
            )

        for h in range(2):

            def rs_step(k, h=h):
                there, _ = plane(k)
                rs_out[there, rs_rows[h]] = dot(tv_mat[there, rs_rows[h]], c2[...]).astype(BF)
                rs_copy(h, k).start()

            loop(1, 16, rs_step)
        rs_in[0] = dot(tv_mat[chip], c2[...]).astype(BF)
        beside_rs()

        def rs_total(h):
            def rs_sum(k, total):
                rs_copy(h, k).wait_recv()
                return total + rs_in[k, rs_rows[h]].astype(F32)

            return lax.fori_loop(1, 16, rs_sum, rs_in[0, rs_rows[h]].astype(F32)).astype(BF)

        homes = ((z * 4 + y) * 4 + x, (x * 4 + z) * 4 + y, (y * 4 + x) * 4 + z)
        orders = (("x", "y", "z"), ("y", "z", "x"), ("z", "x", "y"))
        lasts = (z, x, y)

        def ag_copy(stream, stage, k):
            if stage == 0:
                first, count = homes[stream], 1
            elif stage == 1:
                first, count = lax.div(homes[stream], 4) * 4, 4
            else:
                first, count = lasts[stream] * 16, 16
            part = ag[stream].at[pl.ds(first, count)]
            i = (stream * 3 + stage) * 3 + k - 1
            return remote(
                part, part, b["ag_send"].at[it, i], b["ag_recv"].at[it, i], along(orders[stream][stage], k)
            )

        def ag_start(stream, stage):
            for k in range(1, 4):
                ag_copy(stream, stage, k).start()

        def ag_land(stream, stage):
            for k in range(1, 4):
                ag_copy(stream, stage, k).wait_recv()

        total = rs_total(0)
        ag[0][homes[0]] = total[0:48]
        ag[1][homes[1]] = total[48:96]
        ag_start(0, 0)
        ag_start(1, 0)
        total = rs_total(1)
        ag[2][homes[2]] = total
        ag_start(2, 0)
        for stream in range(3):
            ag_land(stream, 0)
            ag_start(stream, 1)
        for stream in range(3):
            ag_land(stream, 1)
            ag_start(stream, 2)

        beside_ag()

        window_land(0)
        if it == 0:
            for load in loads:
                load.wait()

            @pl.when(has_before)
            def _():
                basis_after.wait_recv()

            @pl.when(has_after)
            def _():
                basis_before.wait_recv()

        def window_coeffs(i):
            cw[rows_at(i, K), :] = dot(basis[i], win[rows_at(i, P_SIZE), :]).astype(BF)

        loop(0, 4, window_coeffs, 4)
        loop(8, 20, window_coeffs, 4)

        def near_dot(i, first, size):
            return dot(b["c_mat"][rows_at(i, 128), pl.ds(first, size)], win[pl.ds(first, size), :])

        def near_most(i):
            w[rows_at(i, 128), :] = near_dot(i, 0, 512) + near_dot(i, 1024, 1536)

        loop(0, 8, near_most)
        for stream in range(3):
            ag_land(stream, 2)

        if it == 1:
            window_start(1)

        def join(i):
            ip, g = i // 4, i % 4
            iz, iy = ip // 4, ip % 4
            first, second, third = ag[0][i], ag[1][(g * 4 + iz) * 4 + iy], ag[2][(iy * 4 + g) * 4 + iz]
            q_two[g * 32 + 2 * ip] = jnp.concatenate([first, second[0:16]], axis=0)
            q_two[g * 32 + 2 * ip + 1] = jnp.concatenate([second[16:48], third], axis=0)

        loop(0, 64, join, 8)

        for j in range(32):
            gathered[pl.ds(j * K, K), :] = q_two[number(1, j, 16)]

        def far_copy(h, k):
            there, device = plane(k)
            rows, i = pl.ds(h * K, K), h * 16 + k
            return remote(
                far_out.at[there, rows],
                far_in.at[k, rows],
                b["far_send"].at[it, i],
                b["far_recv"].at[it, i],
                device,
            )

        for h in range(2):

            def far_step(k, h=h):
                there, _ = plane(k)
                far_out[there, pl.ds(h * K, K)] = dot(s_mat[there, pl.ds(h * K, K)], gathered[...]).astype(BF)
                far_copy(h, k).start()

            loop(1, 16, far_step)
        own = dot(s_mat[chip], gathered[...])

        def fall(i, total):
            part = q_two[pl.ds(i * 16, 16)].reshape(1024, HALF)
            return total + dot(b["top_all"][:, rows_at(i, 1024)], part)

        own = lax.fori_loop(0, 8, fall, own)
        beside_far()

        def l2_copy(h, k):
            part = l2.at[rows_at(chip * 2 + h, K)]
            i = h * 16 + k
            return remote(part, part, b["l2_send"].at[it, i], b["l2_recv"].at[it, i], plane(k)[1])

        for h in range(2):

            def far_sum(k, total, h=h):
                far_copy(h, k).wait_recv()
                return total + far_in[k, pl.ds(h * K, K)].astype(F32)

            half_sum = lax.fori_loop(1, 16, far_sum, own[h * K : (h + 1) * K])
            l2[rows_at(chip * 2 + h, K), :] = half_sum.astype(BF)

            def l2_start(k, h=h):
                l2_copy(h, k).start()

            loop(1, 16, l2_start)

        def drain(k):
            for h in range(2):
                rs_copy(h, k).wait_send()
                far_copy(h, k).wait_send()

        loop(1, 16, drain)
        coeff_swap.wait_send()
        for stream in range(3):
            for stage in range(3):
                for k in range(1, 4):
                    ag_copy(stream, stage, k).wait_send()

        for half in range(2):

            @pl.when(has_after)
            def _(half=half):
                window_copy(0, half).wait_send()

            @pl.when(has_before)
            def _(half=half):
                window_copy(1, half).wait_send()

        beside_l2()

        window_land(1)
        loop(4, 8, window_coeffs, 4)
        loop(20, 24, window_coeffs, 4)

        def leaf_far(i):
            part = dot(b["fl_mat"][rows_at(i, 128), :], cw[...])
            local_half[0, rows_at(i, 128), :] = part[:, :HALF]
            local_half[1, rows_at(i, 128), :] = part[:, HALF:]

        loop(0, 4, leaf_far)

        def near_rest(i):
            w[rows_at(i, 128), :] = w[rows_at(i, 128), :] + near_dot(i, 512, 512) + near_dot(i, 2560, 512)

        loop(0, 8, near_rest)

        def l2_land(k):
            for h in range(2):
                l2_copy(h, k).wait_recv()

        loop(1, 16, l2_land)

        def down_sibling(i):
            sib_out[rows_at(i, 128), :] = dot(down_mat[rows_at(i + 4, 128), :], l2[...]).astype(BF)

        loop(0, 4, down_sibling, 2)
        leaf_swap = remote(sib_out, sib_in, b["sib_send"].at[it, 1], b["sib_recv"].at[it, 1], sibling)
        leaf_swap.start()

        def down_own(i):
            rows = rows_at(i, 128)
            merged[core, rows, :] = (local_half[core, rows, :] + dot(down_mat[rows, :], l2[...])).astype(BF)

        loop(0, 4, down_own, 2)
        leaf_swap.wait_recv()
        merged[1 - core] = (local_half[1 - core] + sib_in[...].astype(F32)).astype(BF)

        def finish(i):
            rows = rows_at(i, P_SIZE)
            for h in range(2):
                lanes = pl.ds(h * HALF, HALF)
                value = w[rows, lanes] + lax.dot_general(
                    basis[8 + i],
                    merged[h, rows_at(i, K), :],
                    (((0,), (0,)), ((), ())),
                    preferred_element_type=F32,
                )
                w[rows, lanes] = value
                if wb is not None:
                    wb[rows, lanes] = value.astype(BF)

        loop(0, 8, finish, 4)
        leaf_swap.wait_send()

        def l2_sent(k):
            for h in range(2):
                l2_copy(h, k).wait_send()

        loop(1, 16, l2_sent)

    p_slot, w1, w2 = b["p_slot"], b["w1"], b["w2"]

    def unorder():
        def split_image(i):
            rows = rows_at(i, 128)
            value = w1[rows, :]
            top = value.astype(BF)
            high[rows, pl.ds(0, 256)] = top
            high[rows, pl.ds(256, 256)] = (value - top.astype(F32)).astype(BF)

        loop(0, 8, split_image)

        def reorder(i):
            wanted = lax.broadcasted_iota(jnp.int32, (128, 1024), 0) + i * 128
            hot = jnp.where(panels_row[...] == wanted, 1.0, 0.0).astype(BF)
            value = dot(hot, high[...])
            w1_panel[rows_at(i, 128), :] = value[:, :256] + value[:, 256:]

        loop(0, 8, reorder)

    def col_max(ref):
        return jnp.maximum(jnp.max(jnp.abs(ref[...]), axis=0, keepdims=True), 1e-30)

    def col_sums(terms):
        def add(i, carry):
            return tuple(
                c + jnp.sum(t.reshape(4, 8, 256), axis=0) for c, t in zip(carry, terms(rows_at(i, 32)))
            )

        sums = lax.fori_loop(0, 32, add, tuple(jnp.zeros((8, 256), F32) for _ in range(3)), unroll=2)
        return [jnp.sum(s, axis=0, keepdims=True) for s in sums]

    early = []

    def early_sums():
        size_p, size_a = col_max(p_slot), col_max(w1)
        inv_p, inv_a = 1.0 / size_p, 1.0 / size_a

        def terms(rows):
            p, a = p_slot[rows, :] * inv_p, w1[rows, :] * inv_a
            return p * p, p * a, a * a

        early.extend((size_p, size_a, col_sums(terms)))

    v1 = b["v0"]
    apply(0, b["v0"], w1, v1, build_rest, build_top, lambda: add_far((0, 1)), build_last)
    for swap in swaps:
        swap.wait_send()

    @pl.when(has_after)
    def _():
        basis_after.wait_send()

    @pl.when(has_before)
    def _():
        basis_before.wait_send()

    apply(1, v1, w2, None, unorder, early_sums, lambda: None, lambda: None)

    size_p, size_a, sums = early
    size_b = col_max(w2)
    inv_p, inv_a, inv_b = 1.0 / size_p, 1.0 / size_a, 1.0 / size_b

    def late_terms(rows):
        value = w2[rows, :] * inv_b
        return p_slot[rows, :] * inv_p * value, w1[rows, :] * inv_a * value, value * value

    sums = sums + col_sums(late_terms)
    sizes = [size_p, size_a, size_b]
    part, box = b["part"], b["box"]
    pairs = ((0, 0), (0, 1), (1, 1), (0, 2), (1, 2), (2, 2))
    coords = (core, x, y, z)
    axes = ("core", "x", "y", "z")

    def sum_copy(stage, k):
        i = stage * 4 + k
        here = box.at[stage, coords[stage]]
        return remote(here, here, b["sum_send"].at[i], b["sum_recv"].at[i], along(axes[stage], k))

    for stage in range(4):
        count = 2 if stage == 0 else 4
        for i in range(6):
            part[i : i + 1, :] = sums[i]
        for i in range(3):
            part[8 + i : 9 + i, :] = sizes[i]
        box[stage, coords[stage]] = part[...]
        for k in range(1, count):
            sum_copy(stage, k).start()
        for k in range(1, count):
            sum_copy(stage, k).wait_recv()
        got = [box[stage, i] for i in range(count)]
        new_sizes = []
        for i in range(3):
            top_size = got[0][8 + i : 9 + i]
            for g in got[1:]:
                top_size = jnp.maximum(top_size, g[8 + i : 9 + i])
            new_sizes.append(top_size)
        factors = [[g[8 + i : 9 + i] / new_sizes[i] for i in range(3)] for g in got]
        sums = []
        for i, (first, second) in enumerate(pairs):
            value = got[0][i : i + 1] * (factors[0][first] * factors[0][second])
            for g, f in zip(got[1:], factors[1:]):
                value = value + g[i : i + 1] * (f[first] * f[second])
            sums.append(value)
        sizes = new_sizes

    along_p, along_a, estimate = project(sums, sizes)
    weights_ref[0:1, :] = along_p
    weights_ref[1:2, :] = along_a
    weights_ref[2:3, :] = estimate
    for stage in range(4):
        for k in range(1, 2 if stage == 0 else 4):
            sum_copy(stage, k).wait_send()


def both_steps(smem_args, vmem_args, hbm_args):
    smem = pl.BlockSpec(memory_space=pltpu.SMEM)
    vmem = pl.BlockSpec(memory_space=pltpu.VMEM)
    anywhere = pl.BlockSpec(memory_space=pl.ANY)
    return pl.pallas_call(
        steps_kernel,
        out_shape=(jax.ShapeDtypeStruct((1024, 256), F32), jax.ShapeDtypeStruct((8, 256), F32)),
        in_specs=[smem] * len(smem_args) + [vmem] * len(vmem_args) + [anywhere] * len(hbm_args),
        out_specs=(vmem, vmem),
        scratch_shapes=list(BUFFERS.values()),
        compiler_params=pltpu.CompilerParams(
            collective_id=1, has_side_effects=True, vmem_limit_bytes=62 * 1024 * 1024
        ),
        name="both_steps",
    )(*smem_args, *vmem_args, *hbm_args)


def result_kernel(weights_ref, pot_ref, image_ref, out_ref, est_ref):
    out_ref[...] = weights_ref[0:1, :] * pot_ref[...] + weights_ref[1:2, :] * image_ref[...]
    est_ref[...] = weights_ref[2, :]


def result(weights, potentials, image):
    return pl.pallas_call(
        result_kernel,
        out_shape=(jax.ShapeDtypeStruct((1024, 256), F32), jax.ShapeDtypeStruct((256,), F32)),
        compiler_params=pltpu.CompilerParams(vmem_limit_bytes=60 * 1024 * 1024),
        name="result",
    )(weights, potentials, image)


def least_squares(beta_norm, first_diag, first_below, second_top, second_diag, second_below):
    first_radius = jnp.sqrt(first_diag * first_diag + first_below * first_below)
    first_cos = first_diag / first_radius
    first_sin = first_below / first_radius
    upper_term = first_cos * second_top + first_sin * second_diag
    lower_term = first_cos * second_diag - first_sin * second_top
    second_radius = jnp.sqrt(lower_term * lower_term + second_below * second_below)
    second_cos = lower_term / second_radius
    second_sin = second_below / second_radius
    weight_two = -first_sin * beta_norm * second_cos / second_radius
    weight_one = (first_cos * beta_norm - upper_term * weight_two) / first_radius
    return (weight_one, weight_two, first_sin * second_sin * beta_norm)


def project(sums, sizes):
    pp, pa, aa, pb, ab, bb = sums
    size_p, size_a, size_b = sizes
    beta = jnp.sqrt(size_p * size_p * pp + EPS)
    scale_p, scale_a, scale_b = size_p / beta, size_a / beta, size_b / beta
    first_first = scale_p * scale_p * pp
    first_image = scale_p * scale_a * pa
    first_diag = first_image
    image_image = scale_a * scale_a * aa
    rest = image_image - first_diag * first_diag * (2.0 - first_first)
    first_below = jnp.sqrt(jnp.maximum(rest, 0.0) + EPS)
    inverse = 1.0 / first_below
    first_second = (first_image - first_diag * first_first) * inverse
    second_second = jnp.maximum(rest, 0.0) * inverse * inverse
    scale_two = scale_b * inverse
    diag_two = first_diag * inverse
    first_b = scale_p * scale_two * pb
    a_b = scale_a * scale_two * ab
    b_b = scale_two * scale_two * bb
    second_top = first_b - diag_two * first_image
    image_image_two = a_b - diag_two * image_image
    second_diag = (image_image_two - first_diag * second_top) * inverse
    square = b_b - 2.0 * diag_two * a_b + diag_two * diag_two * image_image
    rest_two = (
        square
        - second_top * second_top * (2.0 - first_first)
        - second_diag * second_diag * (2.0 - second_second)
        + 2.0 * second_top * second_diag * first_second
    )
    second_below = jnp.sqrt(jnp.maximum(rest_two, 0.0) + EPS)
    weight_one, weight_two, estimate = least_squares(
        beta, first_diag, first_below, second_top, second_diag, second_below
    )
    along_a = weight_two * inverse / beta
    along_p = weight_one / beta - along_a * first_diag
    return along_p, along_a, estimate


def on_device(
    potentials,
    leaf_panels,
    near_blocks,
    near_target,
    near_source,
    near_count,
    leaf_basis,
    far_leaf,
    far_leaf_target,
    far_leaf_source,
    leaf_transfer,
    leaf_parent,
    far_two,
    far_two_target,
    far_two_source,
    two_transfer,
    two_parent,
    far_one,
    far_one_target,
    far_one_source,
):
    c_mat = combine(near_target, near_source, near_count, near_blocks)
    own_numbers = (far_two_target, far_two_source, leaf_parent.reshape(1, 8))
    image, weights = both_steps(
        own_numbers + (two_parent, far_one_target, far_one_source),
        own_numbers
        + (
            leaf_panels,
            potentials,
            leaf_basis,
            leaf_transfer,
            far_two,
            jnp.transpose(two_transfer, (1, 2, 0)),
            far_one,
            far_leaf_target,
            far_leaf_source,
        ),
        (c_mat, jnp.transpose(far_leaf, (1, 2, 0))),
    )
    return result(weights, potentials, image)


def solution(mesh):
    both = P(("grp", "leaf"))
    in_specs = (both,) * 15 + (P(),) * 5
    return jax.shard_map(
        on_device, mesh=mesh, in_specs=in_specs, out_specs=(both, P()), check_vma=False
    )
```
